32 devices in a mesh: blk: 16 (over z, y, core), fsdp: 2 (over x).
Axes of the slice: x: 2, y: 2, z: 4, core: 2. Of those that a mesh axis runs over, the one named last changes fastest.
Arguments:
- latents: bfloat16 [3, 16, 512, 1024], P(None, 'blk', 'fsdp'), may hold values from -6 to 6
- pixels: bfloat16 [3, 32768, 261], P(None, 'blk'), may hold values from -6 to 6
- segment_ids: int32 [3, 32768], P(None, 'blk'), may hold values from 0 to 16, as said below
- pad_ids: int32 [3], replicated, may hold values from 0 to 16
- block_map: int32 [3, 17], replicated, may hold values from 0 to 15, as said below
- norm_gains: bfloat16 [4, 1024], P(None, 'fsdp'), may hold values from 0.099609375 to 1.8984375
- norm_biases: bfloat16 [4, 1024], P(None, 'fsdp'), may hold values from -2 to 2
- pixel_gain: bfloat16 [261], replicated, may hold values from 0.099609375 to 1.8984375
- pixel_bias: bfloat16 [261], replicated, may hold values from -2 to 2
- cross_query: bfloat16 [1024, 1024], P('fsdp'), may hold values from -0.1875 to 0.1875
- cross_kv: bfloat16 [261, 2048], P(None, 'fsdp'), may hold values from -0.375 to 0.375
- cross_out: bfloat16 [1024, 1024], P('fsdp'), may hold values from -4 to 4
- cross_up: bfloat16 [1024, 1024], P('fsdp'), may hold values from -0.1875 to 0.1875
- cross_down: bfloat16 [1024, 1024], P('fsdp'), may hold values from -0.1875 to 0.1875
- self_qkv: bfloat16 [1024, 3072], P('fsdp'), may hold values from -0.1875 to 0.1875
- self_out: bfloat16 [1024, 1024], P('fsdp'), may hold values from -2 to 2
- self_up: bfloat16 [1024, 1024], P('fsdp'), may hold values from -0.1875 to 0.1875
- self_down: bfloat16 [1024, 1024], P('fsdp'), may hold values from -0.1875 to 0.1875
- cotangent: bfloat16 [3, 16, 512, 1024], P(None, 'blk', 'fsdp'), may hold values from -6 to 6
Outputs:
- mixed: bfloat16 [3, 16, 512, 1024], P(None, 'blk', 'fsdp')
- latents_grad: float32 [3, 16, 512, 1024], P(None, 'blk', 'fsdp')
- norm_gains_grad: float32 [4, 1024], P(None, 'fsdp')
- norm_biases_grad: float32 [4, 1024], P(None, 'fsdp')
- pixel_gain_grad: float32 [261], replicated
- pixel_bias_grad: float32 [261], replicated
- cross_query_grad: float32 [1024, 1024], P('fsdp')
- cross_kv_grad: float32 [261, 2048], P(None, 'fsdp')
- cross_out_grad: float32 [1024, 1024], P('fsdp')
- cross_up_grad: float32 [1024, 1024], P('fsdp')
- cross_down_grad: float32 [1024, 1024], P('fsdp')
- self_qkv_grad: float32 [1024, 3072], P('fsdp')
- self_out_grad: float32 [1024, 1024], P('fsdp')
- self_up_grad: float32 [1024, 1024], P('fsdp')
- self_down_grad: float32 [1024, 1024], P('fsdp')
The draws below stay inside these ranges and needn't reach their ends.
Inputs may be any that keep to these rules, and one draw needn't show every extreme that they name: `segment_ids`: each value of 0 to 16 other than the micro-batch's pad id names one image. Images are packed one after another in increasing order of their values, each in consecutive slots, and the pad id fills the slots after the last image. An image has 1024 to 1792 slots, except one image of each micro-batch that has exactly 3072. `block_map`: over the values other than the micro-batch's pad id it is a permutation of the 16 latent blocks; at the pad id it holds some block.
All inputs are finite; a program needn't handle non-finite values.
Results may differ from the reference program's by a relative error of at most 0.02.
Values may be sent and summed in bfloat16 or wider, within the bound.
No kernel may reach another device: no remote copies, remote signals or barrier semaphores. Data moves between devices by JAX's collectives and lax.ppermute only.
A program may use at most 320 MiB of HBM per device.

```python
import jax
import jax.numpy as jnp
from jax import lax

D = 1024
L = 512
C = 261
F = 1024
HEADS = 8
PIX_DEV = 2048
MB = 3
IMAGES = 16
SLOTS = 32768
IMG_MOST = 3072


def micro_layout(key, padding):
    streams = jax.random.split(key, 6)
    biggest = jax.random.randint(streams[1], (), 0, IMAGES)
    drawn_sizes = jax.random.randint(streams[2], (IMAGES,), PIX_DEV // 2, 7 * PIX_DEV // 8 + 1)
    ranking = jnp.arange(IMAGES)
    lengths = jnp.where(ranking == biggest, IMG_MOST, drawn_sizes)
    finish = jnp.cumsum(lengths)
    position = jnp.arange(SLOTS)
    member = jnp.sum((position[:, None] >= finish[None, :]).astype(jnp.int32), axis=1)
    labels = jnp.where(member == IMAGES, padding, member + (member >= padding).astype(jnp.int32))
    owners = jax.random.permutation(streams[4], IMAGES)
    leftover = jax.random.randint(streams[5], (), 0, IMAGES)
    every_label = jnp.arange(IMAGES + 1)
    shifted = jnp.clip(every_label - (every_label > padding).astype(jnp.int32), 0, IMAGES - 1)
    block_table = jnp.where(every_label == padding, leftover, owners[shifted])
    return (labels.astype(jnp.int32), padding.astype(jnp.int32), block_table.astype(jnp.int32))


def all_layouts(key):
    outer = jax.random.split(key, 3)
    micro_keys = jax.random.split(outer[0], MB)
    ordering = jax.random.permutation(outer[1], MB)
    free_pads = jax.random.randint(outer[2], (MB,), 0, IMAGES + 1)
    paddings = jnp.where(ordering == 0, 0, jnp.where(ordering == 1, IMAGES, free_pads))
    return jax.vmap(micro_layout)(micro_keys, paddings)


def draw_segment_ids(key, part):
    segments, padding, block_table = all_layouts(key)
    return segments


def draw_pad_ids(key, part):
    segments, padding, block_table = all_layouts(key)
    return padding


def draw_block_map(key, part):
    segments, padding, block_table = all_layouts(key)
    return block_table


def level_of(rng, dims, cuts, low, largest):
    level, own = 1.0, jax.random.fold_in(rng, 6)
    for dim, blocks in cuts:
        steps = jnp.exp(jax.random.uniform(jax.random.fold_in(own, dim), (blocks,), jnp.float32, low / len(cuts), largest / len(cuts)))
        level = level * jnp.repeat(steps, dims[dim] // blocks).reshape([-1 if axis == dim else 1 for axis in range(len(dims))])
    return level


def noise(own_key, extent, scale, reach, cuts=(), held_as=jnp.bfloat16):
    level = level_of(own_key, extent, cuts, -0.22, 0.18) if cuts else 1.0
    values = jax.random.normal(own_key, extent, jnp.float32) * scale * level
    return jnp.minimum(jnp.maximum(values, -reach), reach).astype(held_as)


def setup_inputs(seed: int = 0) -> dict:
    streams_of = jax.random.split(jax.random.key(seed), 20)
    return {
        "latents": noise(streams_of[0], (MB, IMAGES, L, D), 1.0, 6.0, ((1, 16), (2, 2))),
        "pixels": noise(streams_of[1], (MB, SLOTS, C), 1.0, 6.0, ((1, 16),)),
        "segment_ids": draw_segment_ids(jax.random.fold_in(streams_of[19], 71), 0),
        "pad_ids": draw_pad_ids(jax.random.fold_in(streams_of[19], 71), 0),
        "block_map": draw_block_map(jax.random.fold_in(streams_of[19], 71), 0),
        "norm_gains": jnp.clip(1.0 + 0.18 * jax.random.normal(streams_of[5], (4, D), jnp.float32), 0.099609375, 1.8984375).astype(jnp.bfloat16),
        "norm_biases": noise(streams_of[6], (4, D), 0.3, 2.0, ((1, 2),)),
        "pixel_gain": jnp.clip(1.0 + 0.18 * jax.random.normal(streams_of[7], (C,), jnp.float32), 0.099609375, 1.8984375).astype(jnp.bfloat16),
        "pixel_bias": noise(streams_of[8], (C,), 0.3, 2.0),
        "cross_query": noise(streams_of[9], (D, D), D ** -0.5, 0.1875, ((0, 2),)),
        "cross_kv": noise(streams_of[10], (C, 2 * D), C ** -0.5, 0.375, ((1, 2),)),
        "cross_out": noise(streams_of[11], (D, D), (max(D // 512, 1)) ** -0.5, 4.0, ((0, 2),)),
        "cross_up": noise(streams_of[12], (D, F), D ** -0.5, 0.1875, ((0, 2),)),
        "cross_down": noise(streams_of[13], (F, D), F ** -0.5, 0.1875, ((0, 2),)),
        "self_qkv": noise(streams_of[14], (D, 3 * D), D ** -0.5, 0.1875, ((0, 2),)),
        "self_out": noise(streams_of[15], (D, D), (max(D // 128, 1)) ** -0.5, 2.0, ((0, 2),)),
        "self_up": noise(streams_of[16], (D, F), D ** -0.5, 0.1875, ((0, 2),)),
        "self_down": noise(streams_of[17], (F, D), F ** -0.5, 0.1875, ((0, 2),)),
        "cotangent": noise(streams_of[18], (MB, IMAGES, L, D), 1.0, 6.0, ((1, 16), (2, 2))),
    }


@jax.custom_vjp
def low(v):
    return lax.optimization_barrier(v.astype(jnp.bfloat16)).astype(jnp.float32)

@jax.custom_vjp
def low_back(v):
    return v

def low_keep(v):
    return (low(v), None)

def low_pass(kept, grad):
    return (grad,)

def back_keep(v):
    return (v, None)

def back_low(kept, grad):
    return (low(grad),)
low.defvjp(low_keep, low_pass)
low_back.defvjp(back_keep, back_low)
epsilon = 1e-05
masked_score = -1e+30

def layer_norm(inputs, scaler, offset):
    centre = inputs - lax.optimization_barrier(jnp.mean(inputs, axis=-1, keepdims=True))
    spread = lax.optimization_barrier(jnp.mean(centre * centre, axis=-1, keepdims=True))
    return centre * lax.rsqrt(spread + epsilon) * scaler + offset

def product(matrix_a, matrix_b):
    return jnp.dot(matrix_a, matrix_b, preferred_element_type=jnp.float32, precision=lax.Precision.HIGHEST)

def feed_forward(inputs, scaler, offset, w_up, w_down):
    hidden = low(layer_norm(inputs, scaler, offset))
    upward = low_back(product(hidden, w_up))
    active = low(jax.nn.gelu(upward, approximate=False))
    return low_back(product(active, w_down))

def latent_block(params, latent, pixel_rows, validity):
    gain_rows = params[0]
    bias_rows = params[1]
    pixel_scaler = params[2]
    pixel_offset = params[3]
    w_query = params[4]
    w_pair = params[5]
    w_out = params[6]
    w_up = params[7]
    w_down = params[8]
    w_triple = params[9]
    w_self_out = params[10]
    w_self_up = params[11]
    w_self_down = params[12]
    row_count = latent.shape[0]
    model_width = latent.shape[1]
    head_size = model_width // HEADS
    hidden = low(layer_norm(latent, gain_rows[0], bias_rows[0]))
    queries = low_back(low(product(hidden, w_query)))
    pixel_hidden = low(layer_norm(pixel_rows, pixel_scaler, pixel_offset))
    pair_rows = product(pixel_hidden, w_pair)
    key_rows = low_back(low(pair_rows[:, :model_width]))
    value_rows = low_back(low(pair_rows[:, model_width:]))
    scores = low_back(product(queries, key_rows.T) * model_width ** (-0.5))
    scores = jnp.where(validity[None, :], scores, masked_score)
    shares = jax.nn.softmax(scores, axis=-1)
    attended = low_back(low(product(low(shares), value_rows)))
    first_sum = latent + low_back(product(attended, w_out))
    second_sum = first_sum + feed_forward(first_sum, gain_rows[1], bias_rows[1], w_up, w_down)
    hidden = low(layer_norm(second_sum, gain_rows[2], bias_rows[2]))
    triple = low_back(low(product(hidden, w_triple)))
    q_heads = triple[:, :model_width].reshape(row_count, HEADS, head_size)
    k_heads = triple[:, model_width:2 * model_width].reshape(row_count, HEADS, head_size)
    v_heads = triple[:, 2 * model_width:].reshape(row_count, HEADS, head_size)
    scores = jnp.einsum('qhd,khd->hqk', q_heads, k_heads, precision=lax.Precision.HIGHEST)
    scores = low_back(scores * head_size ** (-0.5))
    shares = jax.nn.softmax(scores, axis=-1)
    blended = jnp.einsum('hqk,khd->qhd', low(shares), v_heads, precision=lax.Precision.HIGHEST)
    blended = low_back(low(blended.reshape(row_count, model_width)))
    third_sum = second_sum + low_back(product(blended, w_self_out))
    return third_sum + feed_forward(third_sum, gain_rows[3], bias_rows[3], w_self_up, w_self_down)

def reference(latents, pixels, segment_ids, pad_ids, block_map, norm_gains, norm_biases, pixel_gain, pixel_bias, cross_query, cross_kv, cross_out, cross_up, cross_down, self_qkv, self_out, self_up, self_down, cotangent):
    params = (norm_gains.astype(jnp.float32), norm_biases.astype(jnp.float32), pixel_gain.astype(jnp.float32), pixel_bias.astype(jnp.float32), cross_query.astype(jnp.float32), cross_kv.astype(jnp.float32), cross_out.astype(jnp.float32), cross_up.astype(jnp.float32), cross_down.astype(jnp.float32), self_qkv.astype(jnp.float32), self_out.astype(jnp.float32), self_up.astype(jnp.float32), self_down.astype(jnp.float32))
    images = latents.shape[1]
    slot_count = pixels.shape[1]
    labels = jnp.arange(images + 1, dtype=jnp.int32)
    blocks = jnp.arange(images, dtype=jnp.int32)
    places = jnp.arange(IMG_MOST, dtype=jnp.int32)
    gradients = tuple((jnp.zeros(weight.shape, jnp.float32) for weight in params))
    outputs = []
    input_grads = []
    for microbatch in range(MB):
        segments = segment_ids[microbatch].astype(jnp.int32)
        owners = jnp.where(labels == pad_ids[microbatch], images, block_map[microbatch]).astype(jnp.int32)
        counts = lax.optimization_barrier(jnp.sum((segments[None, :] == labels[:, None]).astype(jnp.int32), axis=1)).astype(jnp.int32)
        starts = (jnp.cumsum(counts) - counts).astype(jnp.int32)
        ordering = jnp.argsort(segments, stable=True).astype(jnp.int32)
        matching = (owners[None, :] == blocks[:, None]).astype(jnp.int32)
        first_slot = lax.optimization_barrier(jnp.sum(matching * starts[None, :], axis=1)).astype(jnp.int32)
        lengths = lax.optimization_barrier(jnp.sum(matching * counts[None, :], axis=1)).astype(jnp.int32)
        gather_at = ordering[jnp.clip(first_slot[:, None] + places[None, :], 0, slot_count - 1)]
        validity = places[None, :] < lengths[:, None]
        pixel_groups = pixels[microbatch][gather_at].astype(jnp.float32)

        def forward(weights, latent_in):

            def one_block(block_items):
                return latent_block(weights, block_items[0], block_items[1], block_items[2])
            return lax.map(jax.checkpoint(one_block), (latent_in, pixel_groups, validity))
        result, pullback = jax.vjp(forward, params, latents[microbatch].astype(jnp.float32))
        weight_grads, latent_grads = pullback(cotangent[microbatch].astype(jnp.float32))
        gradients = tuple((running + arriving for running, arriving in zip(gradients, weight_grads)))
        outputs.append(result.astype(jnp.bfloat16))
        input_grads.append(latent_grads)
    return (jnp.stack(outputs), jnp.stack(input_grads), gradients[0], gradients[1], gradients[2], gradients[3], gradients[4], gradients[5], gradients[6], gradients[7], gradients[8], gradients[9], gradients[10], gradients[11], gradients[12])
```

```python
import functools

import jax
import jax.numpy as jnp
from jax import lax
from jax.experimental import pallas as pl
from jax.experimental.pallas import tpu as pltpu
from jax.sharding import PartitionSpec as P

HEADS = 8
FEATURE_ROWS = 272
VMEM_LIMIT = 56 * 1024 * 1024

epsilon = 1e-05
masked_score = -1e30
low_type = jnp.bfloat16


def product(a, b):
    return jnp.dot(a, b, preferred_element_type=jnp.float32)


def product_tn(a, b):
    return lax.dot_general(a, b, (((0,), (0,)), ((), ())), preferred_element_type=jnp.float32)


def product_nt(a, b):
    return lax.dot_general(a, b, (((1,), (1,)), ((), ())), preferred_element_type=jnp.float32)


def normalise(rows):
    centre = rows - jnp.mean(rows, axis=-1, keepdims=True)
    scale = lax.rsqrt(jnp.mean(centre * centre, axis=-1, keepdims=True) + epsilon)
    return centre * scale, scale


def norm_backward(upstream, normed, scale, gain):
    gain_term = jnp.sum(upstream * normed, axis=0)
    bias_term = jnp.sum(upstream, axis=0)
    inner = upstream * gain
    down = scale * (
        inner
        - jnp.mean(inner, axis=-1, keepdims=True)
        - normed * jnp.mean(inner * normed, axis=-1, keepdims=True)
    )
    return down, gain_term, bias_term


def feed_forward(rows, gain, bias, w_up, w_down):
    normed, scale = normalise(rows)
    hidden = (normed * gain + bias).astype(low_type)
    upward = product(hidden, w_up)
    share = 0.5 * (1.0 + lax.erf(upward * (0.5**0.5)))
    slope = share + upward * jnp.exp(-0.5 * upward * upward) * 0.3989422804014327
    active = (upward * share).astype(low_type)
    return rows + product(active, w_down), (hidden, slope, active)


def feed_backward(upstream, low, rows, stored, gain, w_up, w_down):
    hidden, slope, active = stored
    grad_down = product_tn(active, low)
    grad_upward = (product_nt(low, w_down) * slope).astype(low_type)
    grad_up = product_tn(hidden, grad_upward)
    normed, scale = normalise(rows)
    down, gain_term, bias_term = norm_backward(product_nt(grad_upward, w_up), normed, scale, gain)
    return upstream + down, grad_up, grad_down, gain_term, bias_term


def nt(a, b):
    return lax.dot_general(a, b, (((1,), (1,)), ((), ())), preferred_element_type=jnp.float32)


def tn(a, b):
    return lax.dot_general(a, b, (((0,), (0,)), ((), ())), preferred_element_type=jnp.float32)


def params(*semantics):
    return pltpu.CompilerParams(dimension_semantics=semantics, vmem_limit_bytes=VMEM_LIMIT)


def pixel_kernel(micro_ref, pixel_ref, count_ref, out_ref):
    features = pixel_ref.shape[1]
    width = out_ref.shape[3]
    pixels = pixel_ref[0].astype(jnp.float32)
    centre = pixels - jnp.mean(pixels, axis=0, keepdims=True)
    spread = jnp.mean(centre * centre, axis=0, keepdims=True)
    normed = centre * lax.rsqrt(spread + epsilon)
    pad = jnp.zeros((FEATURE_ROWS - features, normed.shape[1]), jnp.float32)
    tall = jnp.concatenate([normed, pad], axis=0)
    row = lax.broadcasted_iota(jnp.int32, (FEATURE_ROWS, width), 0)
    high, rest = count_ref[0][:1, :width], count_ref[0][1:2, :width]
    for part in range(out_ref.shape[0]):
        piece = tall[:, part * width : (part + 1) * width]
        piece = jnp.where(row == features, 1.0, piece)
        piece = jnp.where(row == features + 1, high, jnp.where(row == features + 2, rest, piece))
        out_ref[part, 0] = piece.astype(low_type)


def prepare_pixels(pixels, micro, counts, width):
    routed = micro.shape[0]
    features, slots = pixels.shape[1:]
    step = min(slots, 1024)
    return pl.pallas_call(
        pixel_kernel,
        out_shape=jax.ShapeDtypeStruct((slots // width, routed, FEATURE_ROWS, width), low_type),
        grid_spec=pltpu.PrefetchScalarGridSpec(
            num_scalar_prefetch=1,
            grid=(routed, slots // step),
            in_specs=[
                pl.BlockSpec((1, features, step), lambda i, s, m: (m[i], 0, s)),
                pl.BlockSpec((1, 8, 128), lambda i, s, m: (i, 0, 0)),
            ],
            out_specs=pl.BlockSpec((step // width, 1, FEATURE_ROWS, width), lambda i, s, m: (s, i, 0, 0)),
        ),
        compiler_params=params("arbitrary", "arbitrary"),
        name="prepare_pixels",
    )(micro, pixels, counts)


def side_by_side(ref):
    return jnp.concatenate([ref[tile, 0] for tile in range(ref.shape[0])], axis=1)


def cross_forward_kernel(items, big_ref, query_ref, first_ref, second_ref, mask_ref, out_ref):
    item = pl.program_id(0) // items
    lanes = mask_ref.shape[2] // 2

    def attend(features, mask):
        scores = product(query_ref[...], features) + mask
        top = jnp.max(scores, axis=-1, keepdims=True)
        weights = jnp.exp(scores - top)
        total = jnp.sum(weights, axis=-1, keepdims=True)
        out_ref[...] = nt(weights.astype(low_type), features) / total

    @pl.when(big_ref[item] == 0)
    def small():
        attend(side_by_side(first_ref), mask_ref[0][:1, :lanes])

    @pl.when(big_ref[item] != 0)
    def large():
        both = jnp.concatenate([side_by_side(first_ref), side_by_side(second_ref)], axis=1)
        attend(both, mask_ref[0][:1])


def cross_backward_kernel(items, big_ref, query_ref, grad_ref, first_ref, second_ref, mask_ref, out_ref):
    item = pl.program_id(0) // items
    lanes = mask_ref.shape[2] // 2

    def attend(features, mask):
        scores = product(query_ref[...], features) + mask
        top = jnp.max(scores, axis=-1, keepdims=True)
        weights = jnp.exp(scores - top)
        shares = weights / jnp.sum(weights, axis=-1, keepdims=True)
        grad_shares = product(grad_ref[...], features)
        inner = jnp.sum(shares * grad_shares, axis=-1, keepdims=True)
        grad_scores = (shares * (grad_shares - inner)).astype(low_type)
        out_ref[...] = nt(grad_scores, features)

    @pl.when(big_ref[item] == 0)
    def small():
        attend(side_by_side(first_ref), mask_ref[0][:1, :lanes])

    @pl.when(big_ref[item] != 0)
    def large():
        both = jnp.concatenate([side_by_side(first_ref), side_by_side(second_ref)], axis=1)
        attend(both, mask_ref[0][:1])


def cross_call(kernel, big, rows, first, second, mask, block, per_item):
    count = rows[0].shape[0]
    tiles, width = first.shape[0], first.shape[3]
    row_spec = pl.BlockSpec((block, FEATURE_ROWS), lambda i, big: (i, 0))
    tile_spec = pl.BlockSpec((tiles, 1, FEATURE_ROWS, width), lambda i, big: (0, i // per_item, 0, 0))
    return pl.pallas_call(
        functools.partial(kernel, per_item),
        out_shape=jax.ShapeDtypeStruct((count, FEATURE_ROWS), jnp.float32),
        grid_spec=pltpu.PrefetchScalarGridSpec(
            num_scalar_prefetch=1,
            grid=(count // block,),
            in_specs=[row_spec] * len(rows)
            + [tile_spec, tile_spec]
            + [pl.BlockSpec((1, 8, mask.shape[2]), lambda i, big: (i // per_item, 0, 0))],
            out_specs=row_spec,
        ),
        compiler_params=params("arbitrary"),
        name="cross_attention",
    )(big, *rows, first, second, mask)


def self_forward_kernel(groups, scaling, q_ref, k_ref, v_ref, more_k_ref, more_v_ref, out_ref):
    for q_rows, own, more in groups:
        keys, values = keys_of(own, more, k_ref, v_ref, more_k_ref, more_v_ref)
        scores = nt(q_ref[q_rows], keys) * scaling
        weights = jnp.exp(scores - jnp.max(scores, axis=-1, keepdims=True))
        total = jnp.sum(weights, axis=-1, keepdims=True)
        out_ref[q_rows, :] = (product(weights.astype(low_type), values) / total).astype(low_type)


def keys_of(own, more, k_ref, v_ref, more_k_ref, more_v_ref):
    keys, values = [], []
    if own is not None:
        keys.append(k_ref[own])
        values.append(v_ref[own])
    if more is not None:
        keys.append(more_k_ref[more])
        values.append(more_v_ref[more])
    if len(keys) == 1:
        return keys[0], values[0]
    return jnp.concatenate(keys, axis=0), jnp.concatenate(values, axis=0)


def self_backward_kernel(
    groups,
    scaling,
    q_ref,
    k_ref,
    v_ref,
    more_k_ref,
    more_v_ref,
    grad_ref,
    dq_ref,
    dk_ref,
    dv_ref,
    more_dk_ref,
    more_dv_ref,
):
    for q_rows, own, more in groups:
        keys, values = keys_of(own, more, k_ref, v_ref, more_k_ref, more_v_ref)
        queries = q_ref[q_rows]
        grads = grad_ref[q_rows]
        scores = nt(keys, queries) * scaling
        weights = jnp.exp(scores - jnp.max(scores, axis=0, keepdims=True))
        shares = weights / jnp.sum(weights, axis=0, keepdims=True)
        grad_shares = nt(values, grads)
        inner = jnp.sum(shares * grad_shares, axis=0, keepdims=True)
        grad_scores = (shares * (grad_shares - inner)).astype(low_type)
        dq_ref[q_rows, :] = (tn(grad_scores, keys) * scaling).astype(low_type)
        dk = (product(grad_scores, queries) * scaling).astype(low_type)
        dv = product(shares.astype(low_type), grads).astype(low_type)
        split = 0
        if own is not None:
            split = own.stop - own.start
            dk_ref[own, :] = dk[:split]
            dv_ref[own, :] = dv[:split]
        if more is not None:
            more_dk_ref[more, :] = dk[split:]
            more_dv_ref[more, :] = dv[split:]


def self_specs(triple, more, heads):
    rows, width = triple.shape[0], triple.shape[1] // 3 // heads
    extra = more.shape[0]
    return [
        pl.BlockSpec((rows, width), lambda h: (0, h)),
        pl.BlockSpec((rows, width), lambda h: (0, heads + h)),
        pl.BlockSpec((rows, width), lambda h: (0, 2 * heads + h)),
        pl.BlockSpec((extra, width), lambda h: (0, h)),
        pl.BlockSpec((extra, width), lambda h: (0, heads + h)),
    ]


def self_forward(triple, more, groups):
    rows, model = triple.shape[0], triple.shape[1] // 3
    head = model // HEADS
    return pl.pallas_call(
        functools.partial(self_forward_kernel, groups, head**-0.5),
        out_shape=jax.ShapeDtypeStruct((rows, model), low_type),
        grid=(HEADS,),
        in_specs=self_specs(triple, more, HEADS),
        out_specs=pl.BlockSpec((rows, head), lambda h: (0, h)),
        compiler_params=params("arbitrary"),
        name="self_forward",
    )(triple, triple, triple, more, more)


def self_backward(triple, more, grads, groups):
    rows, model = triple.shape[0], triple.shape[1] // 3
    head = model // HEADS
    extra = more.shape[0]
    row_spec = pl.BlockSpec((rows, head), lambda h: (0, h))
    extra_spec = pl.BlockSpec((extra, head), lambda h: (0, h))
    return pl.pallas_call(
        functools.partial(self_backward_kernel, groups, head**-0.5),
        out_shape=[jax.ShapeDtypeStruct((rows, model), low_type)] * 3
        + [jax.ShapeDtypeStruct((extra, model), low_type)] * 2,
        grid=(HEADS,),
        in_specs=self_specs(triple, more, HEADS) + [row_spec],
        out_specs=[row_spec] * 3 + [extra_spec] * 2,
        compiler_params=params("arbitrary"),
        name="self_backward",
    )(triple, triple, triple, more, more, grads)


def ordered(bit, own, other, axis=0):
    first = jnp.where(bit == 0, own, other)
    last = jnp.where(bit == 0, other, own)
    return jnp.concatenate([first, last], axis=axis)


def half_of(array, bit, axis):
    size = array.shape[axis] // 2
    return lax.dynamic_slice_in_dim(array, bit * size, size, axis)


def swap(array, axis_name, mask):
    size = lax.axis_size(axis_name)
    return lax.ppermute(array, axis_name, [(i, i ^ mask) for i in range(size)])


class Plan:
    def __init__(self, micro_count, rows):
        self.blocks = lax.axis_size("blk")
        self.shards = lax.axis_size("fsdp")
        self.b = lax.axis_index("blk")
        self.x = lax.axis_index("fsdp")
        self.core = self.b & 1
        self.rows = rows
        self.micro_count = micro_count
        self.paired = self.shards == 2 and self.blocks % 2 == 0 and micro_count == 3
        if self.paired:
            self.micro = jnp.stack([self.x, jnp.int32(2)]).astype(jnp.int32)
            self.block_rows = rows
            self.per_item = 2
            self.groups = (
                (slice(0, 2 * rows), slice(0, 2 * rows), None),
                (slice(2 * rows, 3 * rows), slice(2 * rows, 3 * rows), slice(0, rows)),
            )
        else:
            self.micro = jnp.arange(micro_count, dtype=jnp.int32)
            self.block_rows = rows
            self.per_item = 1
            whole = rows * self.shards
            self.groups = tuple(
                (slice(i * rows, (i + 1) * rows), None, slice(i * whole, (i + 1) * whole))
                for i in range(micro_count)
            )

    def block_of(self, item, device):
        if self.paired and item == 1:
            return (device | 1) - 1 + self.x
        return device

    def turn(self, array):
        places = []
        for x in range(2):
            for b in range(self.blocks):
                core = b % 2
                places.append((b * 2 + x, (b - core + x) * 2 + core))
        return lax.ppermute(array, ("blk", "fsdp"), places)

    def spread(self, arrays, gate):
        if not self.paired:
            return [array.reshape(-1, array.shape[-1]) for array in arrays]
        rows = self.rows
        own = [lax.dynamic_index_in_dim(array, self.x, 0, False) for array in arrays]
        away = [lax.dynamic_index_in_dim(array, 1 - self.x, 0, False) for array in arrays]
        away = swap(jnp.concatenate(away, axis=0), "fsdp", 1)
        last = self.turn(jnp.concatenate([array[2] for array in arrays], axis=0))
        away, last = after(away, gate), after(last, gate)
        return [
            jnp.concatenate(
                [own[i], away[i * rows : (i + 1) * rows], last[i * rows : (i + 1) * rows]], axis=0
            )
            for i in range(len(arrays))
        ]

    def send_back(self, array):
        if not self.paired:
            return (array,)
        own, away, shared = (array[i * self.rows : (i + 1) * self.rows] for i in range(3))
        return own, swap(away, "fsdp", 1), self.turn(shared)

    def placed(self, parts):
        if not self.paired:
            return parts[0].reshape(self.micro_count, self.rows, -1)
        own, other, shared = parts
        return jnp.stack([jnp.where(self.x == 0, own, other), jnp.where(self.x == 0, other, own), shared])

    def columns(self, pair, norms, gate):
        if not self.paired:
            return (
                lax.all_gather(pair, "fsdp", axis=1, tiled=True),
                lax.all_gather(norms, "fsdp", axis=1, tiled=True),
            )
        rows, width = pair.shape
        flat = norms.reshape(-1, width)
        other = after(swap(jnp.concatenate([pair, flat], axis=0), "fsdp", 1), gate)
        return (
            ordered(self.x, pair, other[:rows], 1),
            ordered(self.x, norms, other[rows:].reshape(norms.shape), 1),
        )

    def fetch(self, weights):
        if not self.paired:
            return None
        model = weights[0].shape[1] if weights[0].shape[0] * 2 >= weights[0].shape[1] else weights[0].shape[0] * 2
        halves = []
        for weight in weights:
            half = half_of(weight, self.core, 0)
            halves += [half[:, at : at + model] for at in range(0, half.shape[1], model)]
        return swap(jnp.concatenate(halves, axis=0), "fsdp", 1)

    def whole(self, weights, near):
        if not self.paired:
            return [lax.all_gather(weight, "fsdp", axis=0, tiled=True) for weight in weights]
        far = swap(near, "blk", 1)
        model = near.shape[1]
        half = weights[0].shape[0] // 2
        results, at = [], 0
        for weight in weights:
            parts = []
            for column in range(0, weight.shape[1], model):
                away = ordered(self.core, near[at : at + half], far[at : at + half])
                parts.append(ordered(self.x, weight[:, column : column + model], away))
                at += half
            results.append(parts[0] if len(parts) == 1 else jnp.concatenate(parts, axis=1))
        return results

    def partner_rows(self, pairs):
        if self.paired:
            return swap(pairs[2 * self.rows :], "blk", 1)
        wide = pairs.reshape(self.micro_count, self.rows, -1)
        return lax.all_gather(wide, "fsdp", axis=1, tiled=True).reshape(-1, wide.shape[-1])

    def own_pairs(self, own, more):
        if self.paired:
            back = swap(more, "blk", 1).astype(jnp.float32)
            last = own[2 * self.rows :].astype(jnp.float32) + back
            return jnp.concatenate([own[: 2 * self.rows], last.astype(low_type)], axis=0)
        wide = more.reshape(self.micro_count, self.rows * self.shards, -1)
        back = lax.psum_scatter(wide, "fsdp", scatter_dimension=1, tiled=True)
        return back.reshape(-1, back.shape[-1])


def added(kept, received):
    return (kept.astype(jnp.float32) + received.astype(jnp.float32)).astype(low_type)


def after(value, *others):
    return lax.optimization_barrier((value,) + others)[0]


class Group:
    def __init__(self, plan, units, order):
        self.plan = plan
        self.units = units
        self.order = order
        core = plan.core
        self.send = jnp.concatenate([half_of(unit, 1 - core, 1) for unit in units], axis=1)
        self.kept = jnp.concatenate([half_of(unit, core, 1) for unit in units], axis=1)
        self.way = ("blk", 1)

    def halve(self, received, bit, axis, way):
        self.send = added(half_of(self.kept, 1 - bit, axis), half_of(received, 1 - bit, axis))
        self.kept = added(half_of(self.kept, bit, axis), half_of(received, bit, axis))
        self.way = way

    def push(self):
        received = swap(self.send, *self.way)
        step, self.order = self.order[:1], self.order[1:]
        plan = self.plan
        if step == "x":
            mask = plan.shards // 2
            while mask > 1:
                self.halve(received, jnp.where((plan.x & mask) > 0, 1, 0), 0, ("fsdp", mask))
                received = swap(self.send, *self.way)
                mask //= 2
            self.halve(received, plan.x & 1, 0, ("fsdp", 1))
            return self.send
        if step == "y":
            self.halve(received, (plan.b >> 1) & 1, 1, ("blk", 2))
            return self.send
        self.send = added(self.kept, received)[0]
        return self.send

    def chips_sum(self):
        blocks = self.plan.blocks
        groups = [list(range(low, blocks, 4)) for low in range(4)]
        rows, width = self.send.shape
        parts = lax.all_to_all(
            self.send, "blk", split_axis=0, concat_axis=0, axis_index_groups=groups, tiled=True
        )
        parts = parts.reshape(blocks // 4, rows * 4 // blocks, width).astype(jnp.float32)
        self.held = jnp.sum(parts, axis=0).astype(low_type)
        return self.held

    def finish(self):
        other = swap(self.held, "blk", 1)
        results, at = [], 0
        for unit in self.units:
            size = unit.shape[1] // 2
            own_part, other_part = self.held[at : at + size], other[at : at + size]
            results.append(ordered(self.plan.core, own_part, other_part).astype(jnp.float32))
            at += size
        return results


def chips_spread(groups):
    plan = groups[0].plan
    blocks = plan.blocks
    same_core = [
        [z * 4 + y * 2 + core for y in range(2) for z in range(blocks // 4)] for core in range(2)
    ]
    sizes = [group.held.shape[0] for group in groups]
    held = jnp.concatenate([group.held for group in groups], axis=0)
    held = lax.all_gather(held, "blk", axis_index_groups=same_core)
    at = 0
    for group, size in zip(groups, sizes):
        group.held = held[:, at : at + size].reshape(-1, held.shape[2])
        at += size


def route_pixels(plan, pixels, segment_ids, pad_ids, block_map):
    blocks, labels = plan.blocks, block_map.shape[1]
    slots, features = pixels.shape[1:]
    width = slots // blocks
    routed = plan.micro.shape[0]
    label_ids = jnp.arange(labels, dtype=jnp.int32)

    def of_items(array):
        return jnp.stack([lax.dynamic_index_in_dim(array, plan.micro[i], 0, False) for i in range(routed)])

    picked = of_items(segment_ids)
    counts = jnp.sum((picked[:, None, :] == label_ids[None, :, None]).astype(jnp.int32), axis=2)
    counts = jnp.stack([counts >> 4, counts & 15], axis=1).astype(jnp.float32)
    counts = jnp.pad(counts, ((0, 0), (0, 6), (0, 128 - labels)))
    chunks = prepare_pixels(jnp.swapaxes(pixels, 1, 2), plan.micro, counts, width)
    spread = lax.all_to_all(chunks, "blk", split_axis=0, concat_axis=0, tiled=True)
    arrived = spread[:, :, features + 1 : features + 3, :labels].astype(jnp.int32)
    totals = jnp.sum(16 * arrived[:, :, 0] + arrived[:, :, 1], axis=0)
    owners = of_items(block_map)
    images = label_ids[None, :] != of_items(pad_ids)[:, None]
    totals = jnp.where(images, totals, 0)
    earlier = label_ids[None, :] < label_ids[:, None]
    starts = jnp.sum(jnp.where(earlier[None], totals[:, None, :], 0), axis=2)
    devices = jnp.arange(blocks, dtype=jnp.int32)

    def extents(wanted):
        hit = (owners[:, None, :] == wanted[:, :, None]) & images[:, None, :]
        start = jnp.sum(jnp.where(hit, starts[:, None, :], 0), axis=2)
        return start, start + jnp.sum(jnp.where(hit, totals[:, None, :], 0), axis=2)

    def chunk_at(start, place):
        first = start // width
        return first + ((place - first) & (blocks - 1))

    def source_of(chunk):
        return jnp.clip(chunk // blocks, 0, blocks - 1)

    item = jnp.arange(routed, dtype=jnp.int32)
    wanted = jnp.stack([plan.block_of(i, devices) for i in range(routed)])
    start, finish = extents(wanted)
    flat = spread.reshape(blocks * routed, FEATURE_ROWS, width)
    piece_at = source_of(chunk_at(start, plan.b)) * routed + item[:, None]
    pieces = jnp.take(flat, piece_at.T.reshape(-1), axis=0, mode="clip")
    pieces = pieces.reshape(blocks, routed, FEATURE_ROWS, width)
    first = lax.all_to_all(pieces, "blk", split_axis=0, concat_axis=0, tiled=True)
    largest = jnp.argmax(totals, axis=1)
    largest_start = jnp.sum(jnp.where(label_ids[None, :] == largest[:, None], starts, 0), axis=1)
    second_at = source_of(chunk_at(largest_start, plan.b) + blocks) * routed + item
    second = lax.all_gather(jnp.take(flat, second_at, axis=0, mode="clip"), "blk", axis=0, tiled=False)
    mine = jnp.stack([plan.block_of(i, plan.b) for i in range(routed)])[:, None]
    start, finish = extents(mine)
    slot = (width * chunk_at(start, devices[None, :]))[:, :, None] + jnp.arange(width, dtype=jnp.int32)
    slot = slot.reshape(routed, -1)
    slot = jnp.concatenate([slot, slot + width * blocks], axis=1)
    mask = jnp.where((slot >= start) & (slot < finish), 0.0, masked_score)
    mask = jnp.broadcast_to(mask[:, None, :], (routed, 8, mask.shape[1]))
    big = ((finish - 1) // width - start // width >= blocks).astype(jnp.int32)[:, 0]
    if width < 128:
        join = 128 // width

        def merged(array):
            parts = array.reshape(blocks // join, join, routed, FEATURE_ROWS, width)
            return parts.transpose(0, 2, 3, 1, 4).reshape(blocks // join, routed, FEATURE_ROWS, 128)

        first, second = merged(first), merged(second)
    return chunks, pieces, first, second, mask, big


def on_device(
    latents,
    pixels,
    segment_ids,
    pad_ids,
    block_map,
    norm_gains,
    norm_biases,
    pixel_gain,
    pixel_bias,
    cross_query,
    cross_kv,
    cross_out,
    cross_up,
    cross_down,
    self_qkv,
    self_out,
    self_up,
    self_down,
    cotangent,
):
    micro_count, unused, rows, model = latents.shape
    features = pixels.shape[2]
    plan = Plan(micro_count, rows)
    scaling = model**-0.5

    chunks, pieces, first, second, mask, big = route_pixels(plan, pixels, segment_ids, pad_ids, block_map)
    if plan.paired:
        latents, cotangent = after(latents, chunks), after(cotangent, chunks)
        cross_kv, cross_query = after(cross_kv, chunks), after(cross_query, chunks)
    latent, upstream = plan.spread([latents[:, 0], cotangent[:, 0]], pieces)
    latent, upstream = latent.astype(jnp.float32), upstream.astype(jnp.float32)
    w_pair, norms = plan.columns(cross_kv, jnp.concatenate([norm_gains, norm_biases], axis=0), pieces)
    norms = norms.astype(jnp.float32)
    gains, biases = norms[:4], norms[4:]
    w_key, w_value = w_pair[:, :model], w_pair[:, model:]
    early = [cross_query]
    middle = [cross_out, cross_up, cross_down]
    late = [self_qkv, self_out, self_up, self_down]
    near_early, near_middle, near_late = plan.fetch(early), plan.fetch(middle), plan.fetch(late)
    if plan.paired:
        near_early, near_middle = after(near_early, pieces), after(near_middle, pieces)
        near_late = after(near_late, first)
    (w_query,) = plan.whole(early, near_early)
    w_out, w_up, w_down = plan.whole(middle, near_middle)
    w_triple, w_self_out, w_self_up, w_self_down = plan.whole(late, near_late)
    pixel_scaler = pixel_gain.astype(jnp.float32)
    pixel_offset = pixel_bias.astype(jnp.float32)

    def widened(rows_f32, scale):
        against = jnp.sum(rows_f32 * pixel_offset, axis=-1, keepdims=True)
        wide = jnp.concatenate([rows_f32 * pixel_scaler, against], axis=1) * scale
        return jnp.pad(wide, ((0, 0), (0, FEATURE_ROWS - features - 1))).astype(low_type)

    def narrowed(wide):
        return wide[:, :features] * pixel_scaler + wide[:, features : features + 1] * pixel_offset

    normed, scale = normalise(latent)
    hidden = (normed * gains[0] + biases[0]).astype(low_type)
    queries = product(hidden, w_query).astype(low_type)
    query_features = product_nt(queries, w_key)
    wide_queries = widened(query_features, scaling)
    summed = cross_call(
        cross_forward_kernel, big, [wide_queries], first, second, mask, plan.block_rows, plan.per_item
    )
    attended_features = narrowed(summed).astype(low_type)
    attended = product(attended_features, w_value).astype(low_type)
    first_sum = latent + product(attended, w_out)
    second_sum, stored_one = feed_forward(first_sum, gains[1], biases[1], w_up, w_down)
    normed_two, scale_two = normalise(second_sum)
    hidden_two = (normed_two * gains[2] + biases[2]).astype(low_type)
    triple = product(hidden_two, w_triple).astype(low_type)
    more = plan.partner_rows(triple[:, model:])
    blended = self_forward(triple, more, plan.groups)
    third_sum = second_sum + product(blended, w_self_out)
    mixed, stored_three = feed_forward(third_sum, gains[3], biases[3], w_self_up, w_self_down)
    mixed = plan.send_back(mixed.astype(low_type))

    def unit(grad):
        return grad.astype(low_type).reshape(plan.shards, -1, model)

    low = upstream.astype(low_type)
    upstream, grad_self_up, grad_self_down, gain_three, bias_three = feed_backward(
        upstream, low, third_sum, stored_three, gains[3], w_self_up, w_self_down
    )
    low = upstream.astype(low_type)
    grad_self_out = product_tn(blended, low)
    one = Group(plan, [unit(grad_self_up), unit(grad_self_down), unit(grad_self_out)], "xy")
    grad_blended = product_nt(low, w_self_out).astype(low_type)
    grad_blended = after(grad_blended, one.send)
    dq, dk, dv, more_dk, more_dv = self_backward(triple, more, grad_blended, plan.groups)
    pairs = plan.own_pairs(
        jnp.concatenate([dk, dv], axis=1), jnp.concatenate([more_dk, more_dv], axis=1)
    )
    pairs = after(pairs, one.push())
    grad_q = product_tn(hidden_two, dq)
    grad_k = product_tn(hidden_two, pairs[:, :model])
    grad_v = product_tn(hidden_two, pairs[:, model:])
    grad_hidden = product_nt(jnp.concatenate([dq, pairs], axis=1), w_triple)
    down, gain_two, bias_two = norm_backward(grad_hidden, normed_two, scale_two, gains[2])
    upstream = upstream + down
    low = upstream.astype(low_type)
    grad_down = product_tn(stored_one[2], low)
    two = Group(plan, [unit(grad_q), unit(grad_k), unit(grad_v), unit(grad_down)], "xy")
    low = after(low, one.push(), two.send, *mixed[1:2])
    upstream, grad_up, unused, gain_one, bias_one = feed_backward(
        upstream, low, first_sum, stored_one, gains[1], w_up, w_down
    )
    upstream = after(upstream, two.push(), *mixed[2:])
    low = upstream.astype(low_type)
    grad_out = product_tn(attended, low)
    grad_attended = product_nt(low, w_out).astype(low_type)
    grad_value = product_tn(attended_features, grad_attended)
    grad_features = product_nt(grad_attended, w_value)
    three = Group(plan, [unit(grad_up), unit(grad_out)], "yx")
    wide_grads = after(widened(grad_features, 1.0), one.push(), three.send)
    score_sums = cross_call(
        cross_backward_kernel,
        big,
        [wide_queries, wide_grads],
        first,
        second,
        mask,
        plan.block_rows,
        plan.per_item,
    )
    score_sums = after(score_sums, one.chips_sum(), three.push())
    key_sums = (narrowed(score_sums) * scaling).astype(low_type)
    grad_queries = product(key_sums, w_key).astype(low_type)
    grad_key = product_tn(key_sums, queries)
    pixel_gain_term = jnp.sum(
        query_features * score_sums[:, :features] * scaling + grad_features * summed[:, :features], axis=0
    )
    pixel_bias_term = jnp.sum(
        query_features * score_sums[:, features : features + 1] * scaling
        + grad_features * summed[:, features : features + 1],
        axis=0,
    )
    grad_query = product_tn(hidden, grad_queries)
    down, gain_zero, bias_zero = norm_backward(product_nt(grad_queries, w_query), normed, scale, gains[0])
    latents_grad = (upstream + down).astype(low_type)

    shards = plan.shards
    width = 2 * model // shards
    rows_of_pair = jnp.pad(jnp.concatenate([grad_key, grad_value], axis=1), ((0, 264 - features), (0, 0)))
    norm_terms = jnp.stack(
        [gain_zero, gain_one, gain_two, gain_three, bias_zero, bias_one, bias_two, bias_three]
    )
    pixel_terms = jnp.pad(jnp.stack([pixel_gain_term, pixel_bias_term]), ((0, 0), (0, 512 - features)))
    pixel_rows = pixel_terms.reshape(1, -1, width)
    tall = jnp.concatenate(
        [
            rows_of_pair.reshape(264, shards, width).transpose(1, 0, 2),
            norm_terms.reshape(8, shards, model // shards).transpose(1, 0, 2).reshape(shards, 4, width),
            jnp.broadcast_to(pixel_rows, (shards,) + pixel_rows.shape[1:]),
            jnp.zeros((shards, 384 - 268 - pixel_rows.shape[1], width), jnp.float32),
        ],
        axis=1,
    )
    four = Group(plan, [unit(grad_query), tall.astype(low_type).reshape(shards, -1, model)], "yx")
    four.send = after(four.send, two.push())
    chips_spread([one])
    four.send = after(four.push(), three.push())
    two.send = after(two.push(), four.send)
    latents_grad = after(latents_grad, two.send)
    three.send = after(three.push(), two.send)
    two.chips_sum()
    three.send = after(three.send, two.held)
    four.send = after(four.push(), three.send)
    chips_spread([two])
    three.chips_sum()
    four.send = after(four.push(), three.held)
    four.chips_sum()
    chips_spread([three, four])
    latents_grad = plan.placed(plan.send_back(latents_grad)).astype(jnp.float32)
    grad_self_up, grad_self_down, grad_self_out = one.finish()
    grad_q, grad_k, grad_v, grad_down = two.finish()
    grad_up, grad_out = three.finish()
    grad_query, tall = four.finish()
    tall = tall.reshape(384, width)
    norm_part = tall[264:268].reshape(8, model // shards)
    pixel_part = tall[268 : 268 + pixel_rows.shape[1]].reshape(2, 512)
    return (
        plan.placed(mixed)[:, None],
        latents_grad[:, None],
        norm_part[:4],
        norm_part[4:],
        pixel_part[0, :features],
        pixel_part[1, :features],
        grad_query,
        tall[:features],
        grad_out,
        grad_up,
        grad_down,
        jnp.concatenate([grad_q, grad_k, grad_v], axis=1),
        grad_self_out,
        grad_self_up,
        grad_self_down,
    )


def solution(mesh):
    placed = (
        P(None, "blk", "fsdp", None),
        P(None, "blk", None),
        P(None, "blk"),
        P(),
        P(),
        P(None, "fsdp"),
        P(None, "fsdp"),
        P(),
        P(),
        P("fsdp", None),
        P(None, "fsdp"),
        P("fsdp", None),
        P("fsdp", None),
        P("fsdp", None),
        P("fsdp", None),
        P("fsdp", None),
        P("fsdp", None),
        P("fsdp", None),
        P(None, "blk", "fsdp", None),
    )
    return jax.shard_map(
        on_device,
        mesh=mesh,
        in_specs=placed,
        out_specs=(
            P(None, "blk", "fsdp", None),
            P(None, "blk", "fsdp", None),
            P(None, "fsdp"),
            P(None, "fsdp"),
            P(),
            P(),
            P("fsdp", None),
            P(None, "fsdp"),
            P("fsdp", None),
            P("fsdp", None),
            P("fsdp", None),
            P("fsdp", None),
            P("fsdp", None),
            P("fsdp", None),
            P("fsdp", None),
        ),
        check_vma=False,
    )
```

```python
import functools

import jax
import jax.numpy as jnp
from jax import lax
from jax.experimental import pallas as pl
from jax.experimental.pallas import tpu as pltpu
from jax.sharding import PartitionSpec as P

HEADS = 8
FEATURE_ROWS = 272
VMEM_LIMIT = 56 * 1024 * 1024

epsilon = 1e-05
masked_score = -1e30
low_type = jnp.bfloat16


def product(a, b):
    return jnp.dot(a, b, preferred_element_type=jnp.float32)


def product_tn(a, b):
    return lax.dot_general(a, b, (((0,), (0,)), ((), ())), preferred_element_type=jnp.float32)


def product_nt(a, b):
    return lax.dot_general(a, b, (((1,), (1,)), ((), ())), preferred_element_type=jnp.float32)


def normalise(rows):
    centre = rows - jnp.mean(rows, axis=-1, keepdims=True)
    scale = lax.rsqrt(jnp.mean(centre * centre, axis=-1, keepdims=True) + epsilon)
    return centre * scale, scale


def norm_backward(upstream, normed, scale, gain):
    gain_term = jnp.sum(upstream * normed, axis=0)
    bias_term = jnp.sum(upstream, axis=0)
    inner = upstream * gain
    down = scale * (
        inner
        - jnp.mean(inner, axis=-1, keepdims=True)
        - normed * jnp.mean(inner * normed, axis=-1, keepdims=True)
    )
    return down, gain_term, bias_term


def feed_forward(rows, gain, bias, w_up, w_down):
    normed, scale = normalise(rows)
    hidden = (normed * gain + bias).astype(low_type)
    upward = product(hidden, w_up)
    share = 0.5 * (1.0 + lax.erf(upward * (0.5**0.5)))
    slope = share + upward * jnp.exp(-0.5 * upward * upward) * 0.3989422804014327
    active = (upward * share).astype(low_type)
    return rows + product(active, w_down), (hidden, slope, active)


def feed_backward(upstream, low, rows, stored, gain, w_up, w_down):
    hidden, slope, active = stored
    grad_down = product_tn(active, low)
    grad_upward = (product_nt(low, w_down) * slope).astype(low_type)
    grad_up = product_tn(hidden, grad_upward)
    normed, scale = normalise(rows)
    down, gain_term, bias_term = norm_backward(product_nt(grad_upward, w_up), normed, scale, gain)
    return upstream + down, grad_up, grad_down, gain_term, bias_term


def nt(a, b):
    return lax.dot_general(a, b, (((1,), (1,)), ((), ())), preferred_element_type=jnp.float32)


def tn(a, b):
    return lax.dot_general(a, b, (((0,), (0,)), ((), ())), preferred_element_type=jnp.float32)


def params(*semantics):
    return pltpu.CompilerParams(dimension_semantics=semantics, vmem_limit_bytes=VMEM_LIMIT)


def pixel_kernel(micro_ref, pixel_ref, count_ref, out_ref):
    features = pixel_ref.shape[1]
    width = out_ref.shape[3]
    pixels = pixel_ref[0].astype(jnp.float32)
    centre = pixels - jnp.mean(pixels, axis=0, keepdims=True)
    spread = jnp.mean(centre * centre, axis=0, keepdims=True)
    normed = centre * lax.rsqrt(spread + epsilon)
    pad = jnp.zeros((FEATURE_ROWS - features, normed.shape[1]), jnp.float32)
    tall = jnp.concatenate([normed, pad], axis=0)
    row = lax.broadcasted_iota(jnp.int32, (FEATURE_ROWS, width), 0)
    high, rest = count_ref[0][:1, :width], count_ref[0][1:2, :width]
    for part in range(out_ref.shape[0]):
        piece = tall[:, part * width : (part + 1) * width]
        piece = jnp.where(row == features, 1.0, piece)
        piece = jnp.where(row == features + 1, high, jnp.where(row == features + 2, rest, piece))
        out_ref[part, 0] = piece.astype(low_type)


def prepare_pixels(pixels, micro, counts, width):
    routed = micro.shape[0]
    features, slots = pixels.shape[1:]
    step = min(slots, 1024)
    return pl.pallas_call(
        pixel_kernel,
        out_shape=jax.ShapeDtypeStruct((slots // width, routed, FEATURE_ROWS, width), low_type),
        grid_spec=pltpu.PrefetchScalarGridSpec(
            num_scalar_prefetch=1,
            grid=(routed, slots // step),
            in_specs=[
                pl.BlockSpec((1, features, step), lambda i, s, m: (m[i], 0, s)),
                pl.BlockSpec((1, 8, 128), lambda i, s, m: (i, 0, 0)),
            ],
            out_specs=pl.BlockSpec((step // width, 1, FEATURE_ROWS, width), lambda i, s, m: (s, i, 0, 0)),
        ),
        compiler_params=params("arbitrary", "arbitrary"),
        name="prepare_pixels",
    )(micro, pixels, counts)


def side_by_side(ref):
    return jnp.concatenate([ref[tile, 0] for tile in range(ref.shape[0])], axis=1)


def cross_forward_kernel(items, big_ref, query_ref, first_ref, second_ref, mask_ref, out_ref):
    item = pl.program_id(0) // items
    lanes = mask_ref.shape[2] // 2

    def attend(features, mask):
        scores = product(query_ref[...], features) + mask
        top = jnp.max(scores, axis=-1, keepdims=True)
        weights = jnp.exp(scores - top)
        total = jnp.sum(weights, axis=-1, keepdims=True)
        out_ref[...] = nt(weights.astype(low_type), features) / total

    @pl.when(big_ref[item] == 0)
    def small():
        attend(side_by_side(first_ref), mask_ref[0][:1, :lanes])

    @pl.when(big_ref[item] != 0)
    def large():
        both = jnp.concatenate([side_by_side(first_ref), side_by_side(second_ref)], axis=1)
        attend(both, mask_ref[0][:1])


def cross_backward_kernel(items, big_ref, query_ref, grad_ref, first_ref, second_ref, mask_ref, out_ref):
    item = pl.program_id(0) // items
    lanes = mask_ref.shape[2] // 2

    def attend(features, mask):
        scores = product(query_ref[...], features) + mask
        top = jnp.max(scores, axis=-1, keepdims=True)
        weights = jnp.exp(scores - top)
        shares = weights / jnp.sum(weights, axis=-1, keepdims=True)
        grad_shares = product(grad_ref[...], features)
        inner = jnp.sum(shares * grad_shares, axis=-1, keepdims=True)
        grad_scores = (shares * (grad_shares - inner)).astype(low_type)
        out_ref[...] = nt(grad_scores, features)

    @pl.when(big_ref[item] == 0)
    def small():
        attend(side_by_side(first_ref), mask_ref[0][:1, :lanes])

    @pl.when(big_ref[item] != 0)
    def large():
        both = jnp.concatenate([side_by_side(first_ref), side_by_side(second_ref)], axis=1)
        attend(both, mask_ref[0][:1])


def cross_call(kernel, big, rows, first, second, mask, block, per_item):
    count = rows[0].shape[0]
    tiles, width = first.shape[0], first.shape[3]
    row_spec = pl.BlockSpec((block, FEATURE_ROWS), lambda i, big: (i, 0))
    tile_spec = pl.BlockSpec((tiles, 1, FEATURE_ROWS, width), lambda i, big: (0, i // per_item, 0, 0))
    return pl.pallas_call(
        functools.partial(kernel, per_item),
        out_shape=jax.ShapeDtypeStruct((count, FEATURE_ROWS), jnp.float32),
        grid_spec=pltpu.PrefetchScalarGridSpec(
            num_scalar_prefetch=1,
            grid=(count // block,),
            in_specs=[row_spec] * len(rows)
            + [tile_spec, tile_spec]
            + [pl.BlockSpec((1, 8, mask.shape[2]), lambda i, big: (i // per_item, 0, 0))],
            out_specs=row_spec,
        ),
        compiler_params=params("arbitrary"),
        name="cross_attention",
    )(big, *rows, first, second, mask)


def self_forward_kernel(groups, scaling, q_ref, k_ref, v_ref, more_k_ref, more_v_ref, out_ref):
    for q_rows, own, more in groups:
        keys, values = keys_of(own, more, k_ref, v_ref, more_k_ref, more_v_ref)
        scores = nt(q_ref[q_rows], keys) * scaling
        weights = jnp.exp(scores - jnp.max(scores, axis=-1, keepdims=True))
        total = jnp.sum(weights, axis=-1, keepdims=True)
        out_ref[q_rows, :] = (product(weights.astype(low_type), values) / total).astype(low_type)


def keys_of(own, more, k_ref, v_ref, more_k_ref, more_v_ref):
    keys, values = [], []
    if own is not None:
        keys.append(k_ref[own])
        values.append(v_ref[own])
    if more is not None:
        keys.append(more_k_ref[more])
        values.append(more_v_ref[more])
    if len(keys) == 1:
        return keys[0], values[0]
    return jnp.concatenate(keys, axis=0), jnp.concatenate(values, axis=0)


def self_backward_kernel(
    groups,
    scaling,
    q_ref,
    k_ref,
    v_ref,
    more_k_ref,
    more_v_ref,
    grad_ref,
    wide_ref,
    more_ref,
):
    head = q_ref.shape[1]
    model = wide_ref.shape[1] // 3
    column = pl.multiple_of(pl.program_id(0) * head, head)
    at_q, at_k, at_v = (pl.ds(pl.multiple_of(part * model + column, head), head) for part in range(3))
    for q_rows, own, more in groups:
        keys, values = keys_of(own, more, k_ref, v_ref, more_k_ref, more_v_ref)
        queries = q_ref[q_rows]
        grads = grad_ref[q_rows]
        scores = nt(keys, queries) * scaling
        weights = jnp.exp(scores - jnp.max(scores, axis=0, keepdims=True))
        shares = weights / jnp.sum(weights, axis=0, keepdims=True)
        grad_shares = nt(values, grads)
        inner = jnp.sum(shares * grad_shares, axis=0, keepdims=True)
        grad_scores = (shares * (grad_shares - inner)).astype(low_type)
        wide_ref[q_rows, at_q] = (tn(grad_scores, keys) * scaling).astype(low_type)
        dk = (product(grad_scores, queries) * scaling).astype(low_type)
        dv = product(shares.astype(low_type), grads).astype(low_type)
        split = 0
        if own is not None:
            split = own.stop - own.start
            wide_ref[own, at_k] = dk[:split]
            wide_ref[own, at_v] = dv[:split]
        if more is not None:
            more_ref[more, at_q] = dk[split:]
            more_ref[more, at_k] = dv[split:]


def self_specs(triple, more, heads):
    rows, width = triple.shape[0], triple.shape[1] // 3 // heads
    extra = more.shape[0]
    return [
        pl.BlockSpec((rows, width), lambda h: (0, h)),
        pl.BlockSpec((rows, width), lambda h: (0, heads + h)),
        pl.BlockSpec((rows, width), lambda h: (0, 2 * heads + h)),
        pl.BlockSpec((extra, width), lambda h: (0, h)),
        pl.BlockSpec((extra, width), lambda h: (0, heads + h)),
    ]


def self_forward(triple, more, groups):
    rows, model = triple.shape[0], triple.shape[1] // 3
    head = model // HEADS
    return pl.pallas_call(
        functools.partial(self_forward_kernel, groups, head**-0.5),
        out_shape=jax.ShapeDtypeStruct((rows, model), low_type),
        grid=(HEADS,),
        in_specs=self_specs(triple, more, HEADS),
        out_specs=pl.BlockSpec((rows, head), lambda h: (0, h)),
        compiler_params=params("arbitrary"),
        name="self_forward",
    )(triple, triple, triple, more, more)


def self_backward(triple, more, grads, groups):
    rows, model = triple.shape[0], triple.shape[1] // 3
    head = model // HEADS
    extra = more.shape[0]
    return pl.pallas_call(
        functools.partial(self_backward_kernel, groups, head**-0.5),
        out_shape=[
            jax.ShapeDtypeStruct((rows, 3 * model), low_type),
            jax.ShapeDtypeStruct((extra, 2 * model), low_type),
        ],
        grid=(HEADS,),
        in_specs=self_specs(triple, more, HEADS) + [pl.BlockSpec((rows, head), lambda h: (0, h))],
        out_specs=[
            pl.BlockSpec((rows, 3 * model), lambda h: (0, 0)),
            pl.BlockSpec((extra, 2 * model), lambda h: (0, 0)),
        ],
        compiler_params=params("arbitrary"),
        name="self_backward",
    )(triple, triple, triple, more, more, grads)


def widen_kernel(places, core_ref, *refs):
    out_ref = refs[-1]
    count = (len(refs) - 1) // 2
    first = core_ref[0] == 0
    for i, (source, at, size) in enumerate(places):
        own = refs[source][at : at + size]
        other = refs[count + source][at : at + size]
        columns = slice(i * own.shape[1], (i + 1) * own.shape[1])
        out_ref[:size, columns] = jnp.where(first, own, other).astype(jnp.float32)
        out_ref[size:, columns] = jnp.where(first, other, own).astype(jnp.float32)


def widen(core, own, other, places):
    rows, width = 2 * places[0][2], len(places) * own[0].shape[1]
    return pl.pallas_call(
        functools.partial(widen_kernel, tuple(places)),
        out_shape=jax.ShapeDtypeStruct((rows, width), jnp.float32),
        in_specs=[pl.BlockSpec(memory_space=pltpu.SMEM)]
        + [pl.BlockSpec(memory_space=pltpu.VMEM)] * (2 * len(own)),
        out_specs=pl.BlockSpec(memory_space=pltpu.VMEM),
        compiler_params=pltpu.CompilerParams(vmem_limit_bytes=VMEM_LIMIT),
        name="widen",
    )(core.reshape(1).astype(jnp.int32), *own, *other)


def ordered(bit, own, other, axis=0):
    first = jnp.where(bit == 0, own, other)
    last = jnp.where(bit == 0, other, own)
    return jnp.concatenate([first, last], axis=axis)


def half_of(array, bit, axis):
    size = array.shape[axis] // 2
    return lax.dynamic_slice_in_dim(array, bit * size, size, axis)


def swap(array, axis_name, mask):
    size = lax.axis_size(axis_name)
    return lax.ppermute(array, axis_name, [(i, i ^ mask) for i in range(size)])


class Plan:
    def __init__(self, micro_count, rows):
        self.blocks = lax.axis_size("blk")
        self.shards = lax.axis_size("fsdp")
        self.b = lax.axis_index("blk")
        self.x = lax.axis_index("fsdp")
        self.core = self.b & 1
        self.side = (self.b >> 1) & 1
        self.rows = rows
        self.micro_count = micro_count
        self.paired = self.shards == 2 and self.blocks % 4 == 0 and micro_count == 3
        if self.paired:
            self.micro = jnp.stack([self.x, jnp.int32(2)]).astype(jnp.int32)
            self.block_rows = rows
            self.per_item = 2
            self.groups = (
                (slice(0, 2 * rows), slice(0, 2 * rows), None),
                (slice(2 * rows, 3 * rows), slice(2 * rows, 3 * rows), slice(0, rows)),
            )
        else:
            self.micro = jnp.arange(micro_count, dtype=jnp.int32)
            self.block_rows = rows
            self.per_item = 1
            whole = rows * self.shards
            self.groups = tuple(
                (slice(i * rows, (i + 1) * rows), None, slice(i * whole, (i + 1) * whole))
                for i in range(micro_count)
            )

    def same_core(self):
        return [list(range(core, self.blocks, 2)) for core in range(2)]

    def block_of(self, item, device):
        if self.paired and item == 1:
            return (device | 1) - 1 + self.x
        return device

    def turn(self, array):
        places = []
        for x in range(2):
            for b in range(self.blocks):
                core = b % 2
                places.append((b * 2 + x, (b - core + x) * 2 + core))
        return lax.ppermute(array, ("blk", "fsdp"), places)

    def spread(self, array):
        if not self.paired:
            return (array.reshape(-1, array.shape[-1]),)
        own = lax.dynamic_index_in_dim(array, self.x, 0, False)
        away = swap(lax.dynamic_index_in_dim(array, 1 - self.x, 0, False), "fsdp", 1)
        return own, away, self.turn(array[2])

    def send_back(self, array):
        if not self.paired:
            return (array,)
        own, away, shared = (array[i * self.rows : (i + 1) * self.rows] for i in range(3))
        return own, swap(away, "fsdp", 1), self.turn(shared)

    def placed(self, parts):
        if not self.paired:
            return parts[0].reshape(self.micro_count, self.rows, -1)
        own, other, shared = parts
        return jnp.stack([jnp.where(self.x == 0, own, other), jnp.where(self.x == 0, other, own), shared])

    def columns(self, pair, norms):
        if not self.paired:
            return (
                lax.all_gather(pair, "fsdp", axis=1, tiled=True),
                lax.all_gather(norms, "fsdp", axis=1, tiled=True),
            )
        flat = norms.reshape(-1, pair.shape[1])
        return (swap(jnp.concatenate([pair, flat], axis=0), "fsdp", 1),)

    def joined(self, pair, norms, other):
        if not self.paired:
            return other
        rows = pair.shape[0]
        return (
            ordered(self.x, pair, other[0][:rows], 1),
            ordered(self.x, norms, other[0][rows:].reshape(norms.shape), 1),
        )

    def fetch(self, weights, chips):
        if not self.paired:
            return None
        part = self.core if chips == 1 else 2 * self.core + self.side
        size = weights[0].shape[0] // (2 * chips)
        parts = [lax.dynamic_slice_in_dim(weight, part * size, size, 0) for weight in weights]
        return jnp.concatenate(parts, axis=1)

    def whole(self, weights, near, chips):
        if not self.paired:
            return [lax.all_gather(weight, "fsdp", axis=0, tiled=True) for weight in weights]
        if chips == 2:
            near = ordered(self.side, near, swap(near, "blk", 2))
        away = ordered(self.core, near, swap(near, "blk", 1))
        results, at = [], 0
        for weight in weights:
            results.append(ordered(self.x, weight, away[:, at : at + weight.shape[1]]))
            at += weight.shape[1]
        return results

    def partner_rows(self, pairs):
        if self.paired:
            return swap(pairs[2 * self.rows :], "blk", 1)
        wide = pairs.reshape(self.micro_count, self.rows, -1)
        return lax.all_gather(wide, "fsdp", axis=1, tiled=True).reshape(-1, wide.shape[-1])

    def own_pairs(self, wide, more):
        model = wide.shape[1] // 3
        if self.paired:
            back = swap(more, "blk", 1).astype(jnp.float32)
            first = 2 * self.rows
            last = (wide[first:, model:].astype(jnp.float32) + back).astype(low_type)
            return lax.dynamic_update_slice(wide, last, (first, model))
        split = more.reshape(self.micro_count, self.rows * self.shards, -1)
        back = lax.psum_scatter(split, "fsdp", scatter_dimension=1, tiled=True)
        return lax.dynamic_update_slice(wide, back.reshape(-1, back.shape[-1]), (0, model))


def added(kept, received):
    return (kept.astype(jnp.float32) + received.astype(jnp.float32)).astype(low_type)


def after(value, *others):
    return lax.optimization_barrier((value,) + others)[0]


class Group:
    def __init__(self, plan, units):
        self.plan = plan
        self.sizes = [unit.shape[1] // 2 for unit in units]
        core = plan.core
        self.send = jnp.concatenate([half_of(unit, 1 - core, 1) for unit in units], axis=1)
        self.kept = jnp.concatenate([half_of(unit, core, 1) for unit in units], axis=1)

    def over_core(self):
        received = swap(self.send, "blk", 1)
        mask = self.plan.shards // 2
        while mask:
            bit = jnp.where((self.plan.x & mask) > 0, 1, 0)
            self.send = added(half_of(self.kept, 1 - bit, 0), half_of(received, 1 - bit, 0))
            self.kept = added(half_of(self.kept, bit, 0), half_of(received, bit, 0))
            if mask > 1:
                received = swap(self.send, "fsdp", mask)
            mask //= 2
        return self.send

    def over_fsdp(self, *earlier):
        received = swap(self.send, "fsdp", 1)
        if earlier:
            received = after(received, *earlier)
        self.total = added(self.kept, received)[0]
        return self.total

    def over_chips(self, *earlier):
        same_core = self.plan.same_core()
        rows, width = self.total.shape
        parts = lax.all_to_all(
            self.total, "blk", split_axis=0, concat_axis=0, axis_index_groups=same_core, tiled=True
        )
        if earlier:
            parts = after(parts, *earlier)
        count = len(same_core[0])
        parts = parts.reshape(count, rows // count, width).astype(jnp.float32)
        self.held = jnp.sum(parts, axis=0).astype(low_type)
        return self.held

    def finish(self):
        self.other = swap(self.held, "blk", 1)
        results, at = [], 0
        for size in self.sizes:
            own_part, other_part = self.held[at : at + size], self.other[at : at + size]
            results.append(ordered(self.plan.core, own_part, other_part).astype(jnp.float32))
            at += size
        return results


def back_from_chips(groups):
    plan = groups[0].plan
    sizes = [group.held.shape[0] for group in groups]
    held = jnp.concatenate([group.held for group in groups], axis=0)
    held = lax.all_gather(held, "blk", axis_index_groups=plan.same_core())
    at = 0
    for group, size in zip(groups, sizes):
        group.held = held[:, at : at + size].reshape(-1, held.shape[2])
        at += size
    return held


def route_pixels(plan, pixels, segment_ids, pad_ids, block_map, fetch):
    blocks, labels = plan.blocks, block_map.shape[1]
    slots, features = pixels.shape[1:]
    width = slots // blocks
    routed = plan.micro.shape[0]
    label_ids = jnp.arange(labels, dtype=jnp.int32)

    def of_items(array):
        return jnp.stack([lax.dynamic_index_in_dim(array, plan.micro[i], 0, False) for i in range(routed)])

    picked = of_items(segment_ids)
    counts = jnp.sum((picked[:, None, :] == label_ids[None, :, None]).astype(jnp.int32), axis=2)
    counts = jnp.stack([counts >> 4, counts & 15], axis=1).astype(jnp.float32)
    counts = jnp.pad(counts, ((0, 0), (0, 6), (0, 128 - labels)))
    chunks = prepare_pixels(jnp.swapaxes(pixels, 1, 2), plan.micro, counts, width)
    spread = lax.all_to_all(chunks, "blk", split_axis=0, concat_axis=0, tiled=True)
    arrived = spread[:, :, features + 1 : features + 3, :labels].astype(jnp.int32)
    totals = jnp.sum(16 * arrived[:, :, 0] + arrived[:, :, 1], axis=0)
    owners = of_items(block_map)
    images = label_ids[None, :] != of_items(pad_ids)[:, None]
    totals = jnp.where(images, totals, 0)
    earlier = label_ids[None, :] < label_ids[:, None]
    starts = jnp.sum(jnp.where(earlier[None], totals[:, None, :], 0), axis=2)
    devices = jnp.arange(blocks, dtype=jnp.int32)

    def extents(wanted):
        hit = (owners[:, None, :] == wanted[:, :, None]) & images[:, None, :]
        start = jnp.sum(jnp.where(hit, starts[:, None, :], 0), axis=2)
        return start, start + jnp.sum(jnp.where(hit, totals[:, None, :], 0), axis=2)

    def chunk_at(start, place):
        first = start // width
        return first + ((place - first) & (blocks - 1))

    def source_of(chunk):
        return jnp.clip(chunk // blocks, 0, blocks - 1)

    item = jnp.arange(routed, dtype=jnp.int32)
    wanted = jnp.stack([plan.block_of(i, devices) for i in range(routed)])
    start, finish = extents(wanted)
    flat = spread.reshape(blocks * routed, FEATURE_ROWS, width)
    piece_at = source_of(chunk_at(start, plan.b)) * routed + item[:, None]
    pieces = jnp.take(flat, piece_at.T.reshape(-1), axis=0, mode="clip")
    pieces = pieces.reshape(blocks, routed, FEATURE_ROWS, width)
    fetched, sent = fetch(chunks, pieces)
    if sent is not None:
        pieces = after(pieces, sent)
    first = lax.all_to_all(pieces, "blk", split_axis=0, concat_axis=0, tiled=True)
    largest = jnp.argmax(totals, axis=1)
    largest_start = jnp.sum(jnp.where(label_ids[None, :] == largest[:, None], starts, 0), axis=1)
    second_at = source_of(chunk_at(largest_start, plan.b) + blocks) * routed + item
    second = lax.all_gather(jnp.take(flat, second_at, axis=0, mode="clip"), "blk", axis=0, tiled=False)
    mine = jnp.stack([plan.block_of(i, plan.b) for i in range(routed)])[:, None]
    start, finish = extents(mine)
    slot = (width * chunk_at(start, devices[None, :]))[:, :, None] + jnp.arange(width, dtype=jnp.int32)
    slot = slot.reshape(routed, -1)
    slot = jnp.concatenate([slot, slot + width * blocks], axis=1)
    mask = jnp.where((slot >= start) & (slot < finish), 0.0, masked_score)
    mask = jnp.broadcast_to(mask[:, None, :], (routed, 8, mask.shape[1]))
    big = ((finish - 1) // width - start // width >= blocks).astype(jnp.int32)[:, 0]
    if width < 128:
        join = 128 // width

        def merged(array):
            parts = array.reshape(blocks // join, join, routed, FEATURE_ROWS, width)
            return parts.transpose(0, 2, 3, 1, 4).reshape(blocks // join, routed, FEATURE_ROWS, 128)

        first, second = merged(first), merged(second)
    return fetched, first, second, mask, big


def on_device(
    latents,
    pixels,
    segment_ids,
    pad_ids,
    block_map,
    norm_gains,
    norm_biases,
    pixel_gain,
    pixel_bias,
    cross_query,
    cross_kv,
    cross_out,
    cross_up,
    cross_down,
    self_qkv,
    self_out,
    self_up,
    self_down,
    cotangent,
):
    micro_count, unused, rows, model = latents.shape
    features = pixels.shape[2]
    plan = Plan(micro_count, rows)
    scaling = model**-0.5

    norm_rows = jnp.concatenate([norm_gains, norm_biases], axis=0)
    early, middle = [cross_query], [cross_out, cross_up, cross_down]
    late, last = [self_qkv], [self_out, self_up, self_down]

    def fetch(chunks, pieces):
        if not plan.paired:
            return (plan.spread(latents[:, 0]), plan.columns(cross_kv, norm_rows)) + (None,) * 4, None
        latent = plan.spread(after(latents, chunks)[:, 0])
        near_early = swap(plan.fetch([after(cross_query, chunks)], 1), "fsdp", 1)
        other = plan.columns(after(cross_kv, chunks), norm_rows)
        send = plan.fetch([after(middle[0], near_early, *latent[1:], *other)] + middle[1:], 1)
        near_middle = swap(send, "fsdp", 1)
        near_late = swap(plan.fetch([after(late[0], send, pieces)], 2), "fsdp", 1)
        near_last = swap(plan.fetch([after(last[0], send, pieces)] + last[1:], 2), "fsdp", 1)
        latent = (latent[0],) + tuple(after(part, pieces) for part in latent[1:])
        near_early, other = after(near_early, pieces), (after(other[0], pieces),)
        return (latent, other, near_early, near_middle, near_late, near_last), send

    fetched, first, second, mask, big = route_pixels(plan, pixels, segment_ids, pad_ids, block_map, fetch)
    latent, other, near_early, near_middle, near_late, near_last = fetched
    latent = jnp.concatenate(latent, axis=0).astype(jnp.float32)
    w_pair, norms = plan.joined(cross_kv, norm_rows, other)
    norms = norms.astype(jnp.float32)
    gains, biases = norms[:4], norms[4:]
    w_key, w_value = w_pair[:, :model], w_pair[:, model:]
    (w_query,) = plan.whole(early, near_early, 1)
    pixel_scaler = pixel_gain.astype(jnp.float32)
    pixel_offset = pixel_bias.astype(jnp.float32)

    def widened(rows_f32, scale):
        against = jnp.sum(rows_f32 * pixel_offset, axis=-1, keepdims=True)
        wide = jnp.concatenate([rows_f32 * pixel_scaler, against], axis=1) * scale
        return jnp.pad(wide, ((0, 0), (0, FEATURE_ROWS - features - 1))).astype(low_type)

    def narrowed(wide):
        return wide[:, :features] * pixel_scaler + wide[:, features : features + 1] * pixel_offset

    normed, scale = normalise(latent)
    hidden = (normed * gains[0] + biases[0]).astype(low_type)
    queries = product(hidden, w_query).astype(low_type)
    query_features = product_nt(queries, w_key)
    wide_queries = widened(query_features, scaling)
    if plan.paired:
        near_middle, near_late = after(near_middle, wide_queries), after(near_late, first)
    w_out, w_up, w_down = plan.whole(middle, near_middle, 1)
    (w_triple,) = plan.whole(late, near_late, 2)
    summed = cross_call(
        cross_forward_kernel, big, [wide_queries], first, second, mask, plan.block_rows, plan.per_item
    )
    if plan.paired:
        near_last, cotangent = after(near_last, summed), after(cotangent, summed)
    w_self_out, w_self_up, w_self_down = plan.whole(last, near_last, 2)
    upstream = plan.spread(cotangent[:, 0])
    attended_features = narrowed(summed).astype(low_type)
    attended = product(attended_features, w_value).astype(low_type)
    first_sum = latent + product(attended, w_out)
    second_sum, stored_one = feed_forward(first_sum, gains[1], biases[1], w_up, w_down)
    normed_two, scale_two = normalise(second_sum)
    hidden_two = (normed_two * gains[2] + biases[2]).astype(low_type)
    triple = product(hidden_two, w_triple).astype(low_type)
    more = plan.partner_rows(triple[:, model:])
    blended = self_forward(triple, more, plan.groups)
    third_sum = second_sum + product(blended, w_self_out)
    mixed, stored_three = feed_forward(third_sum, gains[3], biases[3], w_self_up, w_self_down)
    mixed = mixed.astype(low_type)

    def unit(grad):
        return grad.astype(low_type).reshape(plan.shards, -1, model)

    if plan.paired:
        upstream = (upstream[0],) + tuple(after(part, third_sum) for part in upstream[1:])
    upstream = jnp.concatenate(upstream, axis=0).astype(jnp.float32)
    low = upstream.astype(low_type)
    upstream, grad_self_up, grad_self_down, gain_three, bias_three = feed_backward(
        upstream, low, third_sum, stored_three, gains[3], w_self_up, w_self_down
    )
    low = upstream.astype(low_type)
    grad_self_out = product_tn(blended, low)
    grad_self_out = product_tn(blended, low)
    one = Group(plan, [unit(grad_self_up), unit(grad_self_down), unit(grad_self_out)])
    grad_blended = product_nt(low, w_self_out).astype(low_type)
    grad_blended = after(grad_blended, one.over_core(), mixed)
    triple_grads, more_grads = self_backward(triple, more, grad_blended, plan.groups)
    triple_grads = plan.own_pairs(triple_grads, more_grads)
    two = Group(
        plan, [unit(product_tn(hidden_two, triple_grads[:, i * model : (i + 1) * model])) for i in range(3)]
    )
    triple_grads = after(triple_grads, two.send, one.over_fsdp())
    grad_hidden = product_nt(triple_grads, w_triple)
    down, gain_two, bias_two = norm_backward(grad_hidden, normed_two, scale_two, gains[2])
    upstream = upstream + down
    low = upstream.astype(low_type)
    grad_down = product_tn(stored_one[2], low)
    low = after(low, two.over_core())
    upstream, grad_up, unused, gain_one, bias_one = feed_backward(
        upstream, low, first_sum, stored_one, gains[1], w_up, w_down
    )
    low = upstream.astype(low_type)
    grad_out = product_tn(attended, low)
    three = Group(plan, [unit(grad_up), unit(grad_down), unit(grad_out)])
    grad_attended = product_nt(low, w_out).astype(low_type)
    grad_value = product_tn(attended_features, grad_attended)
    grad_features = product_nt(grad_attended, w_value)
    wide_grads = after(widened(grad_features, 1.0), three.send, one.over_chips())
    score_sums = cross_call(
        cross_backward_kernel,
        big,
        [wide_queries, wide_grads],
        first,
        second,
        mask,
        plan.block_rows,
        plan.per_item,
    )
    score_sums = after(score_sums, two.over_fsdp(), three.over_core())
    key_sums = (narrowed(score_sums) * scaling).astype(low_type)
    grad_queries = product(key_sums, w_key).astype(low_type)
    grad_key = product_tn(key_sums, queries)
    pixel_gain_term = jnp.sum(
        query_features * score_sums[:, :features] * scaling + grad_features * summed[:, :features], axis=0
    )
    pixel_bias_term = jnp.sum(
        query_features * score_sums[:, features : features + 1] * scaling
        + grad_features * summed[:, features : features + 1],
        axis=0,
    )
    grad_query = product_tn(hidden, grad_queries)
    down, gain_zero, bias_zero = norm_backward(product_nt(grad_queries, w_query), normed, scale, gains[0])
    latents_grad = (upstream + down).astype(low_type)

    shards = plan.shards
    width = 2 * model // shards
    rows_of_pair = jnp.pad(jnp.concatenate([grad_key, grad_value], axis=1), ((0, 264 - features), (0, 0)))
    norm_terms = jnp.stack(
        [gain_zero, gain_one, gain_two, gain_three, bias_zero, bias_one, bias_two, bias_three]
    )
    pixel_terms = jnp.pad(jnp.stack([pixel_gain_term, pixel_bias_term]), ((0, 0), (0, 512 - features)))
    pixel_rows = pixel_terms.reshape(1, -1, width)
    tall = jnp.concatenate(
        [
            rows_of_pair.reshape(264, shards, width).transpose(1, 0, 2),
            norm_terms.reshape(8, shards, model // shards).transpose(1, 0, 2).reshape(shards, 4, width),
            jnp.broadcast_to(pixel_rows, (shards,) + pixel_rows.shape[1:]),
            jnp.zeros((shards, 384 - 268 - pixel_rows.shape[1], width), jnp.float32),
        ],
        axis=1,
    )
    four = Group(plan, [unit(grad_query), tall.astype(low_type).reshape(shards, -1, model)])
    two.over_chips(four.send)
    early_sums = back_from_chips([one, two])
    four.over_core()
    three.over_fsdp(four.send)
    four.over_fsdp(three.total)
    mixed = plan.send_back(after(mixed, four.total))
    latents_grad = plan.send_back(after(latents_grad, four.total))
    three.over_chips(four.total, early_sums)
    four.over_chips(three.held)
    back_from_chips([three, four])
    grad_self_up, grad_self_down, grad_self_out = one.finish()
    two.finish()
    half = two.sizes[0]
    grad_triple = widen(plan.core, [two.held], [two.other], [(0, i * half, half) for i in range(3)])
    latents_grad = plan.placed(latents_grad).astype(jnp.float32)
    grad_up, grad_down, grad_out = three.finish()
    grad_query, tall = four.finish()
    tall = tall.reshape(384, width)
    norm_part = tall[264:268].reshape(8, model // shards)
    pixel_part = tall[268 : 268 + pixel_rows.shape[1]].reshape(2, 512)
    return (
        plan.placed(mixed)[:, None],
        latents_grad[:, None],
        norm_part[:4],
        norm_part[4:],
        pixel_part[0, :features],
        pixel_part[1, :features],
        grad_query,
        tall[:features],
        grad_out,
        grad_up,
        grad_down,
        grad_triple,
        grad_self_out,
        grad_self_up,
        grad_self_down,
    )


def solution(mesh):
    placed = (
        P(None, "blk", "fsdp", None),
        P(None, "blk", None),
        P(None, "blk"),
        P(),
        P(),
        P(None, "fsdp"),
        P(None, "fsdp"),
        P(),
        P(),
        P("fsdp", None),
        P(None, "fsdp"),
        P("fsdp", None),
        P("fsdp", None),
        P("fsdp", None),
        P("fsdp", None),
        P("fsdp", None),
        P("fsdp", None),
        P("fsdp", None),
        P(None, "blk", "fsdp", None),
    )
    return jax.shard_map(
        on_device,
        mesh=mesh,
        in_specs=placed,
        out_specs=(
            P(None, "blk", "fsdp", None),
            P(None, "blk", "fsdp", None),
            P(None, "fsdp"),
            P(None, "fsdp"),
            P(),
            P(),
            P("fsdp", None),
            P(None, "fsdp"),
            P("fsdp", None),
            P("fsdp", None),
            P("fsdp", None),
            P("fsdp", None),
            P("fsdp", None),
            P("fsdp", None),
            P("fsdp", None),
        ),
        check_vma=False,
    )
```

```python
import functools

import jax
import jax.numpy as jnp
from jax import lax
from jax.experimental import pallas as pl
from jax.experimental.pallas import tpu as pltpu
from jax.sharding import PartitionSpec as P

HEADS = 8
FEATURE_ROWS = 272
VMEM_LIMIT = 56 * 1024 * 1024

epsilon = 1e-05
masked_score = -1e30
low_type = jnp.bfloat16


def product(a, b):
    return jnp.dot(a, b, preferred_element_type=jnp.float32)


def product_tn(a, b):
    return lax.dot_general(a, b, (((0,), (0,)), ((), ())), preferred_element_type=jnp.float32)


def product_nt(a, b):
    return lax.dot_general(a, b, (((1,), (1,)), ((), ())), preferred_element_type=jnp.float32)


def normalise(rows):
    centre = rows - jnp.mean(rows, axis=-1, keepdims=True)
    scale = lax.rsqrt(jnp.mean(centre * centre, axis=-1, keepdims=True) + epsilon)
    return centre * scale, scale


def norm_backward(upstream, normed, scale, gain):
    gain_term = jnp.sum(upstream * normed, axis=0)
    bias_term = jnp.sum(upstream, axis=0)
    inner = upstream * gain
    down = scale * (
        inner
        - jnp.mean(inner, axis=-1, keepdims=True)
        - normed * jnp.mean(inner * normed, axis=-1, keepdims=True)
    )
    return down, gain_term, bias_term


def feed_forward(rows, gain, bias, w_up, w_down):
    normed, scale = normalise(rows)
    hidden = (normed * gain + bias).astype(low_type)
    upward = product(hidden, w_up)
    share = 0.5 * (1.0 + lax.erf(upward * (0.5**0.5)))
    slope = share + upward * jnp.exp(-0.5 * upward * upward) * 0.3989422804014327
    active = (upward * share).astype(low_type)
    return rows + product(active, w_down), (hidden, slope, active)


def feed_backward(upstream, low, rows, stored, gain, w_up, w_down):
    hidden, slope, active = stored
    grad_down = product_tn(active, low)
    grad_upward = (product_nt(low, w_down) * slope).astype(low_type)
    grad_up = product_tn(hidden, grad_upward)
    normed, scale = normalise(rows)
    down, gain_term, bias_term = norm_backward(product_nt(grad_upward, w_up), normed, scale, gain)
    return upstream + down, grad_up, grad_down, gain_term, bias_term


def nt(a, b):
    return lax.dot_general(a, b, (((1,), (1,)), ((), ())), preferred_element_type=jnp.float32)


def tn(a, b):
    return lax.dot_general(a, b, (((0,), (0,)), ((), ())), preferred_element_type=jnp.float32)


def params(*semantics):
    return pltpu.CompilerParams(dimension_semantics=semantics, vmem_limit_bytes=VMEM_LIMIT)


def pixel_kernel(micro_ref, pixel_ref, count_ref, out_ref):
    features = pixel_ref.shape[1]
    width = out_ref.shape[3]
    pixels = pixel_ref[0].astype(jnp.float32)
    centre = pixels - jnp.mean(pixels, axis=0, keepdims=True)
    spread = jnp.mean(centre * centre, axis=0, keepdims=True)
    normed = centre * lax.rsqrt(spread + epsilon)
    pad = jnp.zeros((FEATURE_ROWS - features, normed.shape[1]), jnp.float32)
    tall = jnp.concatenate([normed, pad], axis=0)
    row = lax.broadcasted_iota(jnp.int32, (FEATURE_ROWS, width), 0)
    high, rest = count_ref[0][:1, :width], count_ref[0][1:2, :width]
    for part in range(out_ref.shape[0]):
        piece = tall[:, part * width : (part + 1) * width]
        piece = jnp.where(row == features, 1.0, piece)
        piece = jnp.where(row == features + 1, high, jnp.where(row == features + 2, rest, piece))
        out_ref[part, 0] = piece.astype(low_type)


def prepare_pixels(pixels, micro, counts, width):
    routed = micro.shape[0]
    features, slots = pixels.shape[1:]
    step = min(slots, 1024)
    return pl.pallas_call(
        pixel_kernel,
        out_shape=jax.ShapeDtypeStruct((slots // width, routed, FEATURE_ROWS, width), low_type),
        grid_spec=pltpu.PrefetchScalarGridSpec(
            num_scalar_prefetch=1,
            grid=(routed, slots // step),
            in_specs=[
                pl.BlockSpec((1, features, step), lambda i, s, m: (m[i], 0, s)),
                pl.BlockSpec((1, 8, 128), lambda i, s, m: (i, 0, 0)),
            ],
            out_specs=pl.BlockSpec((step // width, 1, FEATURE_ROWS, width), lambda i, s, m: (s, i, 0, 0)),
        ),
        compiler_params=params("arbitrary", "arbitrary"),
        name="prepare_pixels",
    )(micro, pixels, counts)


def side_by_side(ref):
    return jnp.concatenate([ref[tile, 0] for tile in range(ref.shape[0])], axis=1)


def cross_forward_kernel(items, big_ref, query_ref, first_ref, second_ref, mask_ref, out_ref):
    item = pl.program_id(0) // items
    lanes = mask_ref.shape[2] // 2

    def attend(features, mask):
        scores = product(query_ref[...], features) + mask
        top = jnp.max(scores, axis=-1, keepdims=True)
        weights = jnp.exp(scores - top)
        total = jnp.sum(weights, axis=-1, keepdims=True)
        out_ref[...] = nt(weights.astype(low_type), features) / total

    @pl.when(big_ref[item] == 0)
    def small():
        attend(side_by_side(first_ref), mask_ref[0][:1, :lanes])

    @pl.when(big_ref[item] != 0)
    def large():
        both = jnp.concatenate([side_by_side(first_ref), side_by_side(second_ref)], axis=1)
        attend(both, mask_ref[0][:1])


def cross_backward_kernel(items, big_ref, query_ref, grad_ref, first_ref, second_ref, mask_ref, out_ref):
    item = pl.program_id(0) // items
    lanes = mask_ref.shape[2] // 2

    def attend(features, mask):
        scores = product(query_ref[...], features) + mask
        top = jnp.max(scores, axis=-1, keepdims=True)
        weights = jnp.exp(scores - top)
        shares = weights / jnp.sum(weights, axis=-1, keepdims=True)
        grad_shares = product(grad_ref[...], features)
        inner = jnp.sum(shares * grad_shares, axis=-1, keepdims=True)
        grad_scores = (shares * (grad_shares - inner)).astype(low_type)
        out_ref[...] = nt(grad_scores, features)

    @pl.when(big_ref[item] == 0)
    def small():
        attend(side_by_side(first_ref), mask_ref[0][:1, :lanes])

    @pl.when(big_ref[item] != 0)
    def large():
        both = jnp.concatenate([side_by_side(first_ref), side_by_side(second_ref)], axis=1)
        attend(both, mask_ref[0][:1])


def cross_call(kernel, big, rows, first, second, mask, block, per_item):
    count = rows[0].shape[0]
    tiles, width = first.shape[0], first.shape[3]
    row_spec = pl.BlockSpec((block, FEATURE_ROWS), lambda i, big: (i, 0))
    tile_spec = pl.BlockSpec((tiles, 1, FEATURE_ROWS, width), lambda i, big: (0, i // per_item, 0, 0))
    return pl.pallas_call(
        functools.partial(kernel, per_item),
        out_shape=jax.ShapeDtypeStruct((count, FEATURE_ROWS), jnp.float32),
        grid_spec=pltpu.PrefetchScalarGridSpec(
            num_scalar_prefetch=1,
            grid=(count // block,),
            in_specs=[row_spec] * len(rows)
            + [tile_spec, tile_spec]
            + [pl.BlockSpec((1, 8, mask.shape[2]), lambda i, big: (i // per_item, 0, 0))],
            out_specs=row_spec,
        ),
        compiler_params=params("arbitrary"),
        name="cross_attention",
    )(big, *rows, first, second, mask)


def self_forward_kernel(groups, scaling, q_ref, k_ref, v_ref, more_k_ref, more_v_ref, out_ref):
    for q_rows, own, more in groups:
        keys, values = keys_of(own, more, k_ref, v_ref, more_k_ref, more_v_ref)
        scores = nt(q_ref[q_rows], keys) * scaling
        weights = jnp.exp(scores - jnp.max(scores, axis=-1, keepdims=True))
        total = jnp.sum(weights, axis=-1, keepdims=True)
        out_ref[q_rows, :] = (product(weights.astype(low_type), values) / total).astype(low_type)


def keys_of(own, more, k_ref, v_ref, more_k_ref, more_v_ref):
    keys, values = [], []
    if own is not None:
        keys.append(k_ref[own])
        values.append(v_ref[own])
    if more is not None:
        keys.append(more_k_ref[more])
        values.append(more_v_ref[more])
    if len(keys) == 1:
        return keys[0], values[0]
    return jnp.concatenate(keys, axis=0), jnp.concatenate(values, axis=0)


def self_backward_kernel(
    groups,
    scaling,
    q_ref,
    k_ref,
    v_ref,
    more_k_ref,
    more_v_ref,
    grad_ref,
    wide_ref,
    more_ref,
):
    head = q_ref.shape[1]
    model = wide_ref.shape[1] // 3
    column = pl.multiple_of(pl.program_id(0) * head, head)
    at_q, at_k, at_v = (pl.ds(pl.multiple_of(part * model + column, head), head) for part in range(3))
    for q_rows, own, more in groups:
        keys, values = keys_of(own, more, k_ref, v_ref, more_k_ref, more_v_ref)
        queries = q_ref[q_rows]
        grads = grad_ref[q_rows]
        scores = nt(keys, queries) * scaling
        weights = jnp.exp(scores - jnp.max(scores, axis=0, keepdims=True))
        shares = weights / jnp.sum(weights, axis=0, keepdims=True)
        grad_shares = nt(values, grads)
        inner = jnp.sum(shares * grad_shares, axis=0, keepdims=True)
        grad_scores = (shares * (grad_shares - inner)).astype(low_type)
        wide_ref[q_rows, at_q] = (tn(grad_scores, keys) * scaling).astype(low_type)
        dk = (product(grad_scores, queries) * scaling).astype(low_type)
        dv = product(shares.astype(low_type), grads).astype(low_type)
        split = 0
        if own is not None:
            split = own.stop - own.start
            wide_ref[own, at_k] = dk[:split]
            wide_ref[own, at_v] = dv[:split]
        if more is not None:
            more_ref[more, at_q] = dk[split:]
            more_ref[more, at_k] = dv[split:]


def self_specs(triple, more, heads):
    rows, width = triple.shape[0], triple.shape[1] // 3 // heads
    extra = more.shape[0]
    return [
        pl.BlockSpec((rows, width), lambda h: (0, h)),
        pl.BlockSpec((rows, width), lambda h: (0, heads + h)),
        pl.BlockSpec((rows, width), lambda h: (0, 2 * heads + h)),
        pl.BlockSpec((extra, width), lambda h: (0, h)),
        pl.BlockSpec((extra, width), lambda h: (0, heads + h)),
    ]


def self_forward(triple, more, groups):
    rows, model = triple.shape[0], triple.shape[1] // 3
    head = model // HEADS
    return pl.pallas_call(
        functools.partial(self_forward_kernel, groups, head**-0.5),
        out_shape=jax.ShapeDtypeStruct((rows, model), low_type),
        grid=(HEADS,),
        in_specs=self_specs(triple, more, HEADS),
        out_specs=pl.BlockSpec((rows, head), lambda h: (0, h)),
        compiler_params=params("arbitrary"),
        name="self_forward",
    )(triple, triple, triple, more, more)


def self_backward(triple, more, grads, groups):
    rows, model = triple.shape[0], triple.shape[1] // 3
    head = model // HEADS
    extra = more.shape[0]
    return pl.pallas_call(
        functools.partial(self_backward_kernel, groups, head**-0.5),
        out_shape=[
            jax.ShapeDtypeStruct((rows, 3 * model), low_type),
            jax.ShapeDtypeStruct((extra, 2 * model), low_type),
        ],
        grid=(HEADS,),
        in_specs=self_specs(triple, more, HEADS) + [pl.BlockSpec((rows, head), lambda h: (0, h))],
        out_specs=[
            pl.BlockSpec((rows, 3 * model), lambda h: (0, 0)),
            pl.BlockSpec((extra, 2 * model), lambda h: (0, 0)),
        ],
        compiler_params=params("arbitrary"),
        name="self_backward",
    )(triple, triple, triple, more, more, grads)


def widen_kernel(places, core_ref, *refs):
    out_ref = refs[-1]
    count = (len(refs) - 1) // 2
    first = core_ref[0] == 0
    for i, (source, at, size) in enumerate(places):
        own = refs[source][at : at + size]
        other = refs[count + source][at : at + size]
        columns = slice(i * own.shape[1], (i + 1) * own.shape[1])
        out_ref[:size, columns] = jnp.where(first, own, other).astype(jnp.float32)
        out_ref[size:, columns] = jnp.where(first, other, own).astype(jnp.float32)


def widen(core, own, other, places):
    rows, width = 2 * places[0][2], len(places) * own[0].shape[1]
    return pl.pallas_call(
        functools.partial(widen_kernel, tuple(places)),
        out_shape=jax.ShapeDtypeStruct((rows, width), jnp.float32),
        in_specs=[pl.BlockSpec(memory_space=pltpu.SMEM)]
        + [pl.BlockSpec(memory_space=pltpu.VMEM)] * (2 * len(own)),
        out_specs=pl.BlockSpec(memory_space=pltpu.VMEM),
        compiler_params=pltpu.CompilerParams(vmem_limit_bytes=VMEM_LIMIT),
        name="widen",
    )(core.reshape(1).astype(jnp.int32), *own, *other)


def ordered(bit, own, other, axis=0):
    first = jnp.where(bit == 0, own, other)
    last = jnp.where(bit == 0, other, own)
    return jnp.concatenate([first, last], axis=axis)


def half_of(array, bit, axis):
    size = array.shape[axis] // 2
    return lax.dynamic_slice_in_dim(array, bit * size, size, axis)


def swap(array, axis_name, mask):
    size = lax.axis_size(axis_name)
    return lax.ppermute(array, axis_name, [(i, i ^ mask) for i in range(size)])


class Plan:
    def __init__(self, micro_count, rows):
        self.blocks = lax.axis_size("blk")
        self.shards = lax.axis_size("fsdp")
        self.b = lax.axis_index("blk")
        self.x = lax.axis_index("fsdp")
        self.core = self.b & 1
        self.side = (self.b >> 1) & 1
        self.rows = rows
        self.micro_count = micro_count
        self.paired = self.shards == 2 and self.blocks % 4 == 0 and micro_count == 3
        if self.paired:
            self.micro = jnp.stack([self.x, jnp.int32(2)]).astype(jnp.int32)
            self.block_rows = rows
            self.per_item = 2
            self.groups = (
                (slice(0, 2 * rows), slice(0, 2 * rows), None),
                (slice(2 * rows, 3 * rows), slice(2 * rows, 3 * rows), slice(0, rows)),
            )
        else:
            self.micro = jnp.arange(micro_count, dtype=jnp.int32)
            self.block_rows = rows
            self.per_item = 1
            whole = rows * self.shards
            self.groups = tuple(
                (slice(i * rows, (i + 1) * rows), None, slice(i * whole, (i + 1) * whole))
                for i in range(micro_count)
            )

    def same_core(self):
        return [list(range(core, self.blocks, 2)) for core in range(2)]

    def block_of(self, item, device):
        if self.paired and item == 1:
            return (device | 1) - 1 + self.x
        return device

    def turn(self, array):
        places = []
        for x in range(2):
            for b in range(self.blocks):
                core = b % 2
                places.append((b * 2 + x, (b - core + x) * 2 + core))
        return lax.ppermute(array, ("blk", "fsdp"), places)

    def spread(self, array):
        if not self.paired:
            return (array.reshape(-1, array.shape[-1]),)
        own = lax.dynamic_index_in_dim(array, self.x, 0, False)
        away = swap(lax.dynamic_index_in_dim(array, 1 - self.x, 0, False), "fsdp", 1)
        return own, away, self.turn(array[2])

    def send_back(self, array):
        if not self.paired:
            return (array,)
        own, away, shared = (array[i * self.rows : (i + 1) * self.rows] for i in range(3))
        return own, swap(away, "fsdp", 1), self.turn(shared)

    def placed(self, parts):
        if not self.paired:
            return parts[0].reshape(self.micro_count, self.rows, -1)
        own, other, shared = parts
        return jnp.stack([jnp.where(self.x == 0, own, other), jnp.where(self.x == 0, other, own), shared])

    def columns(self, pair, norms):
        if not self.paired:
            return (
                lax.all_gather(pair, "fsdp", axis=1, tiled=True),
                lax.all_gather(norms, "fsdp", axis=1, tiled=True),
            )
        flat = norms.reshape(-1, pair.shape[1])
        return (swap(jnp.concatenate([pair, flat], axis=0), "fsdp", 1),)

    def joined(self, pair, norms, other):
        if not self.paired:
            return other
        rows = pair.shape[0]
        return (
            ordered(self.x, pair, other[0][:rows], 1),
            ordered(self.x, norms, other[0][rows:].reshape(norms.shape), 1),
        )

    def fetch(self, weights, chips):
        if not self.paired:
            return None
        part = self.core if chips == 1 else 2 * self.core + self.side
        size = weights[0].shape[0] // (2 * chips)
        parts = [lax.dynamic_slice_in_dim(weight, part * size, size, 0) for weight in weights]
        return jnp.concatenate(parts, axis=1)

    def whole(self, weights, near, chips):
        if not self.paired:
            return [lax.all_gather(weight, "fsdp", axis=0, tiled=True) for weight in weights]
        if chips == 2:
            near = ordered(self.side, near, swap(near, "blk", 2))
        away = ordered(self.core, near, swap(near, "blk", 1))
        results, at = [], 0
        for weight in weights:
            results.append(ordered(self.x, weight, away[:, at : at + weight.shape[1]]))
            at += weight.shape[1]
        return results

    def partner_rows(self, pairs):
        if self.paired:
            return swap(pairs[2 * self.rows :], "blk", 1)
        wide = pairs.reshape(self.micro_count, self.rows, -1)
        return lax.all_gather(wide, "fsdp", axis=1, tiled=True).reshape(-1, wide.shape[-1])

    def own_pairs(self, wide, more):
        model = wide.shape[1] // 3
        if self.paired:
            back = swap(more, "blk", 1).astype(jnp.float32)
            first = 2 * self.rows
            last = (wide[first:, model:].astype(jnp.float32) + back).astype(low_type)
            return lax.dynamic_update_slice(wide, last, (first, model))
        split = more.reshape(self.micro_count, self.rows * self.shards, -1)
        back = lax.psum_scatter(split, "fsdp", scatter_dimension=1, tiled=True)
        return lax.dynamic_update_slice(wide, back.reshape(-1, back.shape[-1]), (0, model))


def added(kept, received):
    return (kept.astype(jnp.float32) + received.astype(jnp.float32)).astype(low_type)


def after(value, *others):
    return lax.optimization_barrier((value,) + others)[0]


class Group:
    def __init__(self, plan, units):
        self.plan = plan
        self.sizes = [unit.shape[1] // 2 for unit in units]
        core = plan.core
        self.send = jnp.concatenate([half_of(unit, 1 - core, 1) for unit in units], axis=1)
        self.kept = jnp.concatenate([half_of(unit, core, 1) for unit in units], axis=1)

    def over_core(self):
        received = swap(self.send, "blk", 1)
        mask = self.plan.shards // 2
        while mask:
            bit = jnp.where((self.plan.x & mask) > 0, 1, 0)
            self.send = added(half_of(self.kept, 1 - bit, 0), half_of(received, 1 - bit, 0))
            self.kept = added(half_of(self.kept, bit, 0), half_of(received, bit, 0))
            if mask > 1:
                received = swap(self.send, "fsdp", mask)
            mask //= 2
        return self.send

    def over_fsdp(self, *earlier):
        received = swap(self.send, "fsdp", 1)
        if earlier:
            received = after(received, *earlier)
        self.total = added(self.kept, received)[0]
        return received

    def over_chips(self, *earlier):
        same_core = self.plan.same_core()
        rows, width = self.total.shape
        parts = lax.all_to_all(
            self.total, "blk", split_axis=0, concat_axis=0, axis_index_groups=same_core, tiled=True
        )
        if earlier:
            parts = after(parts, *earlier)
        arrived, count = parts, len(same_core[0])
        parts = parts.reshape(count, rows // count, width).astype(jnp.float32)
        self.held = jnp.sum(parts, axis=0).astype(low_type)
        return arrived

    def finish(self):
        self.other = swap(self.held, "blk", 1)
        results, at = [], 0
        for size in self.sizes:
            own_part, other_part = self.held[at : at + size], self.other[at : at + size]
            results.append(ordered(self.plan.core, own_part, other_part).astype(jnp.float32))
            at += size
        return results


def back_from_chips(groups):
    plan = groups[0].plan
    sizes = [group.held.shape[0] for group in groups]
    held = jnp.concatenate([group.held for group in groups], axis=0)
    held = lax.all_gather(held, "blk", axis_index_groups=plan.same_core())
    at = 0
    for group, size in zip(groups, sizes):
        group.held = held[:, at : at + size].reshape(-1, held.shape[2])
        at += size
    return held


def route_pixels(plan, pixels, segment_ids, pad_ids, block_map, fetch):
    blocks, labels = plan.blocks, block_map.shape[1]
    slots, features = pixels.shape[1:]
    width = slots // blocks
    routed = plan.micro.shape[0]
    label_ids = jnp.arange(labels, dtype=jnp.int32)

    def of_items(array):
        return jnp.stack([lax.dynamic_index_in_dim(array, plan.micro[i], 0, False) for i in range(routed)])

    picked = of_items(segment_ids)
    counts = jnp.sum((picked[:, None, :] == label_ids[None, :, None]).astype(jnp.int32), axis=2)
    counts = jnp.stack([counts >> 4, counts & 15], axis=1).astype(jnp.float32)
    counts = jnp.pad(counts, ((0, 0), (0, 6), (0, 128 - labels)))
    chunks = prepare_pixels(jnp.swapaxes(pixels, 1, 2), plan.micro, counts, width)
    spread = lax.all_to_all(chunks, "blk", split_axis=0, concat_axis=0, tiled=True)
    arrived = spread[:, :, features + 1 : features + 3, :labels].astype(jnp.int32)
    totals = jnp.sum(16 * arrived[:, :, 0] + arrived[:, :, 1], axis=0)
    owners = of_items(block_map)
    images = label_ids[None, :] != of_items(pad_ids)[:, None]
    totals = jnp.where(images, totals, 0)
    earlier = label_ids[None, :] < label_ids[:, None]
    starts = jnp.sum(jnp.where(earlier[None], totals[:, None, :], 0), axis=2)
    devices = jnp.arange(blocks, dtype=jnp.int32)

    def extents(wanted):
        hit = (owners[:, None, :] == wanted[:, :, None]) & images[:, None, :]
        start = jnp.sum(jnp.where(hit, starts[:, None, :], 0), axis=2)
        return start, start + jnp.sum(jnp.where(hit, totals[:, None, :], 0), axis=2)

    def chunk_at(start, place):
        first = start // width
        return first + ((place - first) & (blocks - 1))

    def source_of(chunk):
        return jnp.clip(chunk // blocks, 0, blocks - 1)

    item = jnp.arange(routed, dtype=jnp.int32)
    wanted = jnp.stack([plan.block_of(i, devices) for i in range(routed)])
    start, finish = extents(wanted)
    flat = spread.reshape(blocks * routed, FEATURE_ROWS, width)
    piece_at = source_of(chunk_at(start, plan.b)) * routed + item[:, None]
    pieces = jnp.take(flat, piece_at.T.reshape(-1), axis=0, mode="clip")
    pieces = pieces.reshape(blocks, routed, FEATURE_ROWS, width)
    fetched, sent = fetch(chunks, pieces)
    if sent is not None:
        pieces = after(pieces, sent)
    first = lax.all_to_all(pieces, "blk", split_axis=0, concat_axis=0, tiled=True)
    largest = jnp.argmax(totals, axis=1)
    largest_start = jnp.sum(jnp.where(label_ids[None, :] == largest[:, None], starts, 0), axis=1)
    second_at = source_of(chunk_at(largest_start, plan.b) + blocks) * routed + item
    second = lax.all_gather(jnp.take(flat, second_at, axis=0, mode="clip"), "blk", axis=0, tiled=False)
    mine = jnp.stack([plan.block_of(i, plan.b) for i in range(routed)])[:, None]
    start, finish = extents(mine)
    slot = (width * chunk_at(start, devices[None, :]))[:, :, None] + jnp.arange(width, dtype=jnp.int32)
    slot = slot.reshape(routed, -1)
    slot = jnp.concatenate([slot, slot + width * blocks], axis=1)
    mask = jnp.where((slot >= start) & (slot < finish), 0.0, masked_score)
    mask = jnp.broadcast_to(mask[:, None, :], (routed, 8, mask.shape[1]))
    big = ((finish - 1) // width - start // width >= blocks).astype(jnp.int32)[:, 0]
    if width < 128:
        join = 128 // width

        def merged(array):
            parts = array.reshape(blocks // join, join, routed, FEATURE_ROWS, width)
            return parts.transpose(0, 2, 3, 1, 4).reshape(blocks // join, routed, FEATURE_ROWS, 128)

        first, second = merged(first), merged(second)
    return fetched, first, second, mask, big


def on_device(
    latents,
    pixels,
    segment_ids,
    pad_ids,
    block_map,
    norm_gains,
    norm_biases,
    pixel_gain,
    pixel_bias,
    cross_query,
    cross_kv,
    cross_out,
    cross_up,
    cross_down,
    self_qkv,
    self_out,
    self_up,
    self_down,
    cotangent,
):
    micro_count, unused, rows, model = latents.shape
    features = pixels.shape[2]
    plan = Plan(micro_count, rows)
    scaling = model**-0.5

    norm_rows = jnp.concatenate([norm_gains, norm_biases], axis=0)
    early, middle = [cross_query], [cross_out, cross_up, cross_down]
    late, last = [self_qkv], [self_out, self_up, self_down]

    def fetch(chunks, pieces):
        if not plan.paired:
            return (plan.spread(latents[:, 0]), plan.columns(cross_kv, norm_rows)) + (None,) * 4, None
        latent = plan.spread(after(latents, chunks)[:, 0])
        near_early = swap(plan.fetch([after(cross_query, chunks)], 1), "fsdp", 1)
        other = plan.columns(after(cross_kv, chunks), norm_rows)
        send = plan.fetch([after(middle[0], near_early, *latent[1:], *other)] + middle[1:], 1)
        near_middle = swap(send, "fsdp", 1)
        near_late = swap(plan.fetch([after(late[0], send, pieces)], 2), "fsdp", 1)
        near_last = swap(plan.fetch([after(last[0], send, pieces)] + last[1:], 2), "fsdp", 1)
        latent = (latent[0],) + tuple(after(part, pieces) for part in latent[1:])
        near_early, other = after(near_early, pieces), (after(other[0], pieces),)
        return (latent, other, near_early, near_middle, near_late, near_last), send

    fetched, first, second, mask, big = route_pixels(plan, pixels, segment_ids, pad_ids, block_map, fetch)
    latent, other, near_early, near_middle, near_late, near_last = fetched
    latent = jnp.concatenate(latent, axis=0).astype(jnp.float32)
    w_pair, norms = plan.joined(cross_kv, norm_rows, other)
    norms = norms.astype(jnp.float32)
    gains, biases = norms[:4], norms[4:]
    w_key, w_value = w_pair[:, :model], w_pair[:, model:]
    (w_query,) = plan.whole(early, near_early, 1)
    pixel_scaler = pixel_gain.astype(jnp.float32)
    pixel_offset = pixel_bias.astype(jnp.float32)

    def widened(rows_f32, scale):
        against = jnp.sum(rows_f32 * pixel_offset, axis=-1, keepdims=True)
        wide = jnp.concatenate([rows_f32 * pixel_scaler, against], axis=1) * scale
        return jnp.pad(wide, ((0, 0), (0, FEATURE_ROWS - features - 1))).astype(low_type)

    def narrowed(wide):
        return wide[:, :features] * pixel_scaler + wide[:, features : features + 1] * pixel_offset

    normed, scale = normalise(latent)
    hidden = (normed * gains[0] + biases[0]).astype(low_type)
    queries = product(hidden, w_query).astype(low_type)
    query_features = product_nt(queries, w_key)
    wide_queries = widened(query_features, scaling)
    if plan.paired:
        near_middle, near_late = after(near_middle, wide_queries), after(near_late, first)
    w_out, w_up, w_down = plan.whole(middle, near_middle, 1)
    (w_triple,) = plan.whole(late, near_late, 2)
    summed = cross_call(
        cross_forward_kernel, big, [wide_queries], first, second, mask, plan.block_rows, plan.per_item
    )
    if plan.paired:
        near_last, cotangent = after(near_last, summed), after(cotangent, summed)
    w_self_out, w_self_up, w_self_down = plan.whole(last, near_last, 2)
    upstream = plan.spread(cotangent[:, 0])
    attended_features = narrowed(summed).astype(low_type)
    attended = product(attended_features, w_value).astype(low_type)
    first_sum = latent + product(attended, w_out)
    second_sum, stored_one = feed_forward(first_sum, gains[1], biases[1], w_up, w_down)
    normed_two, scale_two = normalise(second_sum)
    hidden_two = (normed_two * gains[2] + biases[2]).astype(low_type)
    triple = product(hidden_two, w_triple).astype(low_type)
    more = plan.partner_rows(triple[:, model:])
    blended = self_forward(triple, more, plan.groups)
    third_sum = second_sum + product(blended, w_self_out)
    mixed, stored_three = feed_forward(third_sum, gains[3], biases[3], w_self_up, w_self_down)
    mixed = mixed.astype(low_type)

    def unit(grad):
        return grad.astype(low_type).reshape(plan.shards, -1, model)

    if plan.paired:
        upstream = (upstream[0],) + tuple(after(part, third_sum) for part in upstream[1:])
    upstream = jnp.concatenate(upstream, axis=0).astype(jnp.float32)
    low = upstream.astype(low_type)
    upstream, grad_self_up, grad_self_down, gain_three, bias_three = feed_backward(
        upstream, low, third_sum, stored_three, gains[3], w_self_up, w_self_down
    )
    low = upstream.astype(low_type)
    grad_self_out = product_tn(blended, low)
    grad_self_out = product_tn(blended, low)
    one = Group(plan, [unit(grad_self_up), unit(grad_self_down)])
    grad_blended = product_nt(low, w_self_out).astype(low_type)
    grad_blended = after(grad_blended, one.over_core(), mixed)
    triple_grads, more_grads = self_backward(triple, more, grad_blended, plan.groups)
    triple_grads, more_grads = after((triple_grads, more_grads), one.over_fsdp())
    triple_grads = plan.own_pairs(triple_grads, more_grads)
    two = Group(
        plan,
        [unit(product_tn(hidden_two, triple_grads[:, i * model : (i + 1) * model])) for i in range(3)]
        + [unit(grad_self_out)],
    )
    triple_grads = after(triple_grads, two.send)
    grad_hidden = product_nt(triple_grads, w_triple)
    down, gain_two, bias_two = norm_backward(grad_hidden, normed_two, scale_two, gains[2])
    upstream = upstream + down
    low = upstream.astype(low_type)
    grad_down = product_tn(stored_one[2], low)
    low = after(low, two.over_core())
    upstream, grad_up, unused, gain_one, bias_one = feed_backward(
        upstream, low, first_sum, stored_one, gains[1], w_up, w_down
    )
    low = after(upstream.astype(low_type), one.over_chips())
    grad_out = product_tn(attended, low)
    three = Group(plan, [unit(grad_up), unit(grad_down), unit(grad_out)])
    grad_attended = product_nt(low, w_out).astype(low_type)
    grad_value = product_tn(attended_features, grad_attended)
    grad_features = product_nt(grad_attended, w_value)
    wide_grads = after(widened(grad_features, 1.0), two.over_fsdp(), three.over_core())
    score_sums = cross_call(
        cross_backward_kernel,
        big,
        [wide_queries, wide_grads],
        first,
        second,
        mask,
        plan.block_rows,
        plan.per_item,
    )
    key_sums = (narrowed(score_sums) * scaling).astype(low_type)
    grad_queries = product(key_sums, w_key).astype(low_type)
    grad_key = product_tn(key_sums, queries)
    pixel_gain_term = jnp.sum(
        query_features * score_sums[:, :features] * scaling + grad_features * summed[:, :features], axis=0
    )
    pixel_bias_term = jnp.sum(
        query_features * score_sums[:, features : features + 1] * scaling
        + grad_features * summed[:, features : features + 1],
        axis=0,
    )
    grad_query = product_tn(hidden, grad_queries)
    down, gain_zero, bias_zero = norm_backward(product_nt(grad_queries, w_query), normed, scale, gains[0])
    latents_grad = (upstream + down).astype(low_type)

    shards = plan.shards
    width = 2 * model // shards
    rows_of_pair = jnp.pad(jnp.concatenate([grad_key, grad_value], axis=1), ((0, 264 - features), (0, 0)))
    norm_terms = jnp.stack(
        [gain_zero, gain_one, gain_two, gain_three, bias_zero, bias_one, bias_two, bias_three]
    )
    pixel_terms = jnp.pad(jnp.stack([pixel_gain_term, pixel_bias_term]), ((0, 0), (0, 512 - features)))
    pixel_rows = pixel_terms.reshape(1, -1, width)
    tall = jnp.concatenate(
        [
            rows_of_pair.reshape(264, shards, width).transpose(1, 0, 2),
            norm_terms.reshape(8, shards, model // shards).transpose(1, 0, 2).reshape(shards, 4, width),
            jnp.broadcast_to(pixel_rows, (shards,) + pixel_rows.shape[1:]),
            jnp.zeros((shards, 384 - 268 - pixel_rows.shape[1], width), jnp.float32),
        ],
        axis=1,
    )
    four = Group(plan, [unit(grad_query), tall.astype(low_type).reshape(shards, -1, model)])
    four.send = after(four.send, three.over_fsdp(), two.over_chips())
    early_sums = back_from_chips([one, two])
    four.over_core()
    arrived = four.over_fsdp(three.total)
    mixed = plan.send_back(after(mixed, arrived))
    latents_grad = plan.send_back(after(latents_grad, arrived))
    arrived = three.over_chips(early_sums)
    four.over_chips(arrived)
    back_from_chips([three, four])
    grad_self_up, grad_self_down = one.finish()
    grad_self_out = two.finish()[3]
    half = two.sizes[0]
    grad_triple = widen(plan.core, [two.held], [two.other], [(0, i * half, half) for i in range(3)])
    latents_grad = plan.placed(latents_grad).astype(jnp.float32)
    grad_up, grad_down, grad_out = three.finish()
    grad_query, tall = four.finish()
    tall = tall.reshape(384, width)
    norm_part = tall[264:268].reshape(8, model // shards)
    pixel_part = tall[268 : 268 + pixel_rows.shape[1]].reshape(2, 512)
    return (
        plan.placed(mixed)[:, None],
        latents_grad[:, None],
        norm_part[:4],
        norm_part[4:],
        pixel_part[0, :features],
        pixel_part[1, :features],
        grad_query,
        tall[:features],
        grad_out,
        grad_up,
        grad_down,
        grad_triple,
        grad_self_out,
        grad_self_up,
        grad_self_down,
    )


def solution(mesh):
    placed = (
        P(None, "blk", "fsdp", None),
        P(None, "blk", None),
        P(None, "blk"),
        P(),
        P(),
        P(None, "fsdp"),
        P(None, "fsdp"),
        P(),
        P(),
        P("fsdp", None),
        P(None, "fsdp"),
        P("fsdp", None),
        P("fsdp", None),
        P("fsdp", None),
        P("fsdp", None),
        P("fsdp", None),
        P("fsdp", None),
        P("fsdp", None),
        P(None, "blk", "fsdp", None),
    )
    return jax.shard_map(
        on_device,
        mesh=mesh,
        in_specs=placed,
        out_specs=(
            P(None, "blk", "fsdp", None),
            P(None, "blk", "fsdp", None),
            P(None, "fsdp"),
            P(None, "fsdp"),
            P(),
            P(),
            P("fsdp", None),
            P(None, "fsdp"),
            P("fsdp", None),
            P("fsdp", None),
            P("fsdp", None),
            P("fsdp", None),
            P("fsdp", None),
            P("fsdp", None),
            P("fsdp", None),
        ),
        check_vma=False,
    )
```

```python
import functools

import jax
import jax.numpy as jnp
from jax import lax
from jax.experimental import pallas as pl
from jax.experimental.pallas import tpu as pltpu
from jax.sharding import PartitionSpec as P

HEADS = 8
FEATURE_ROWS = 272
VMEM_LIMIT = 56 * 1024 * 1024

epsilon = 1e-05
masked_score = -1e30
low_type = jnp.bfloat16


def product(a, b):
    return jnp.dot(a, b, preferred_element_type=jnp.float32)


def product_tn(a, b):
    return lax.dot_general(a, b, (((0,), (0,)), ((), ())), preferred_element_type=jnp.float32)


def product_nt(a, b):
    return lax.dot_general(a, b, (((1,), (1,)), ((), ())), preferred_element_type=jnp.float32)


def normalise(rows):
    centre = rows - jnp.mean(rows, axis=-1, keepdims=True)
    scale = lax.rsqrt(jnp.mean(centre * centre, axis=-1, keepdims=True) + epsilon)
    return centre * scale, scale


def norm_backward(upstream, normed, scale, gain):
    gain_term = jnp.sum(upstream * normed, axis=0)
    bias_term = jnp.sum(upstream, axis=0)
    inner = upstream * gain
    down = scale * (
        inner
        - jnp.mean(inner, axis=-1, keepdims=True)
        - normed * jnp.mean(inner * normed, axis=-1, keepdims=True)
    )
    return down, gain_term, bias_term


def feed_forward(rows, gain, bias, w_up, w_down):
    normed, scale = normalise(rows)
    hidden = (normed * gain + bias).astype(low_type)
    upward = product(hidden, w_up)
    share = 0.5 * (1.0 + lax.erf(upward * (0.5**0.5)))
    slope = share + upward * jnp.exp(-0.5 * upward * upward) * 0.3989422804014327
    active = (upward * share).astype(low_type)
    return rows + product(active, w_down), (hidden, slope, active)


def feed_backward(upstream, low, rows, stored, gain, w_up, w_down):
    hidden, slope, active = stored
    grad_down = product_tn(active, low)
    grad_upward = (product_nt(low, w_down) * slope).astype(low_type)
    grad_up = product_tn(hidden, grad_upward)
    normed, scale = normalise(rows)
    down, gain_term, bias_term = norm_backward(product_nt(grad_upward, w_up), normed, scale, gain)
    return upstream + down, grad_up, grad_down, gain_term, bias_term


def nt(a, b):
    return lax.dot_general(a, b, (((1,), (1,)), ((), ())), preferred_element_type=jnp.float32)


def tn(a, b):
    return lax.dot_general(a, b, (((0,), (0,)), ((), ())), preferred_element_type=jnp.float32)


def params(*semantics):
    return pltpu.CompilerParams(dimension_semantics=semantics, vmem_limit_bytes=VMEM_LIMIT)


def pixel_kernel(micro_ref, pixel_ref, count_ref, out_ref):
    features = pixel_ref.shape[1]
    width = out_ref.shape[3]
    pixels = pixel_ref[0].astype(jnp.float32)
    centre = pixels - jnp.mean(pixels, axis=0, keepdims=True)
    spread = jnp.mean(centre * centre, axis=0, keepdims=True)
    normed = centre * lax.rsqrt(spread + epsilon)
    pad = jnp.zeros((FEATURE_ROWS - features, normed.shape[1]), jnp.float32)
    tall = jnp.concatenate([normed, pad], axis=0)
    row = lax.broadcasted_iota(jnp.int32, (FEATURE_ROWS, width), 0)
    high, rest = count_ref[0][:1, :width], count_ref[0][1:2, :width]
    for part in range(out_ref.shape[0]):
        piece = tall[:, part * width : (part + 1) * width]
        piece = jnp.where(row == features, 1.0, piece)
        piece = jnp.where(row == features + 1, high, jnp.where(row == features + 2, rest, piece))
        out_ref[part, 0] = piece.astype(low_type)


def prepare_pixels(pixels, micro, counts, width):
    routed = micro.shape[0]
    features, slots = pixels.shape[1:]
    step = min(slots, 1024)
    return pl.pallas_call(
        pixel_kernel,
        out_shape=jax.ShapeDtypeStruct((slots // width, routed, FEATURE_ROWS, width), low_type),
        grid_spec=pltpu.PrefetchScalarGridSpec(
            num_scalar_prefetch=1,
            grid=(routed, slots // step),
            in_specs=[
                pl.BlockSpec((1, features, step), lambda i, s, m: (m[i], 0, s)),
                pl.BlockSpec((1, 8, 128), lambda i, s, m: (i, 0, 0)),
            ],
            out_specs=pl.BlockSpec((step // width, 1, FEATURE_ROWS, width), lambda i, s, m: (s, i, 0, 0)),
        ),
        compiler_params=params("arbitrary", "arbitrary"),
        name="prepare_pixels",
    )(micro, pixels, counts)


def side_by_side(ref):
    return jnp.concatenate([ref[tile, 0] for tile in range(ref.shape[0])], axis=1)


def cross_forward_kernel(items, big_ref, query_ref, first_ref, second_ref, mask_ref, out_ref):
    item = pl.program_id(0) // items
    lanes = mask_ref.shape[2] // 2

    def attend(features, mask):
        scores = product(query_ref[...], features) + mask
        top = jnp.max(scores, axis=-1, keepdims=True)
        weights = jnp.exp(scores - top)
        total = jnp.sum(weights, axis=-1, keepdims=True)
        out_ref[...] = nt(weights.astype(low_type), features) / total

    @pl.when(big_ref[item] == 0)
    def small():
        attend(side_by_side(first_ref), mask_ref[0][:1, :lanes])

    @pl.when(big_ref[item] != 0)
    def large():
        both = jnp.concatenate([side_by_side(first_ref), side_by_side(second_ref)], axis=1)
        attend(both, mask_ref[0][:1])


def cross_backward_kernel(items, big_ref, query_ref, grad_ref, first_ref, second_ref, mask_ref, out_ref):
    item = pl.program_id(0) // items
    lanes = mask_ref.shape[2] // 2

    def attend(features, mask):
        scores = product(query_ref[...], features) + mask
        top = jnp.max(scores, axis=-1, keepdims=True)
        weights = jnp.exp(scores - top)
        shares = weights / jnp.sum(weights, axis=-1, keepdims=True)
        grad_shares = product(grad_ref[...], features)
        inner = jnp.sum(shares * grad_shares, axis=-1, keepdims=True)
        grad_scores = (shares * (grad_shares - inner)).astype(low_type)
        out_ref[...] = nt(grad_scores, features)

    @pl.when(big_ref[item] == 0)
    def small():
        attend(side_by_side(first_ref), mask_ref[0][:1, :lanes])

    @pl.when(big_ref[item] != 0)
    def large():
        both = jnp.concatenate([side_by_side(first_ref), side_by_side(second_ref)], axis=1)
        attend(both, mask_ref[0][:1])


def cross_call(kernel, big, rows, first, second, mask, block, per_item):
    count = rows[0].shape[0]
    tiles, width = first.shape[0], first.shape[3]
    row_spec = pl.BlockSpec((block, FEATURE_ROWS), lambda i, big: (i, 0))
    tile_spec = pl.BlockSpec((tiles, 1, FEATURE_ROWS, width), lambda i, big: (0, i // per_item, 0, 0))
    return pl.pallas_call(
        functools.partial(kernel, per_item),
        out_shape=jax.ShapeDtypeStruct((count, FEATURE_ROWS), jnp.float32),
        grid_spec=pltpu.PrefetchScalarGridSpec(
            num_scalar_prefetch=1,
            grid=(count // block,),
            in_specs=[row_spec] * len(rows)
            + [tile_spec, tile_spec]
            + [pl.BlockSpec((1, 8, mask.shape[2]), lambda i, big: (i // per_item, 0, 0))],
            out_specs=row_spec,
        ),
        compiler_params=params("arbitrary"),
        name="cross_attention",
    )(big, *rows, first, second, mask)


def self_forward_kernel(groups, scaling, q_ref, k_ref, v_ref, more_k_ref, more_v_ref, out_ref):
    for q_rows, own, more in groups:
        keys, values = keys_of(own, more, k_ref, v_ref, more_k_ref, more_v_ref)
        scores = nt(q_ref[q_rows], keys) * scaling
        weights = jnp.exp(scores - jnp.max(scores, axis=-1, keepdims=True))
        total = jnp.sum(weights, axis=-1, keepdims=True)
        out_ref[q_rows, :] = (product(weights.astype(low_type), values) / total).astype(low_type)


def keys_of(own, more, k_ref, v_ref, more_k_ref, more_v_ref):
    keys, values = [], []
    if own is not None:
        keys.append(k_ref[own])
        values.append(v_ref[own])
    if more is not None:
        keys.append(more_k_ref[more])
        values.append(more_v_ref[more])
    if len(keys) == 1:
        return keys[0], values[0]
    return jnp.concatenate(keys, axis=0), jnp.concatenate(values, axis=0)


def self_backward_kernel(
    groups,
    scaling,
    q_ref,
    k_ref,
    v_ref,
    more_k_ref,
    more_v_ref,
    grad_ref,
    wide_ref,
    more_ref,
):
    head = q_ref.shape[1]
    model = wide_ref.shape[1] // 3
    column = pl.multiple_of(pl.program_id(0) * head, head)
    at_q, at_k, at_v = (pl.ds(pl.multiple_of(part * model + column, head), head) for part in range(3))
    for q_rows, own, more in groups:
        keys, values = keys_of(own, more, k_ref, v_ref, more_k_ref, more_v_ref)
        queries = q_ref[q_rows]
        grads = grad_ref[q_rows]
        scores = nt(keys, queries) * scaling
        weights = jnp.exp(scores - jnp.max(scores, axis=0, keepdims=True))
        shares = weights / jnp.sum(weights, axis=0, keepdims=True)
        grad_shares = nt(values, grads)
        inner = jnp.sum(shares * grad_shares, axis=0, keepdims=True)
        grad_scores = (shares * (grad_shares - inner)).astype(low_type)
        wide_ref[q_rows, at_q] = (tn(grad_scores, keys) * scaling).astype(low_type)
        dk = (product(grad_scores, queries) * scaling).astype(low_type)
        dv = product(shares.astype(low_type), grads).astype(low_type)
        split = 0
        if own is not None:
            split = own.stop - own.start
            wide_ref[own, at_k] = dk[:split]
            wide_ref[own, at_v] = dv[:split]
        if more is not None:
            more_ref[more, at_q] = dk[split:]
            more_ref[more, at_k] = dv[split:]


def self_specs(triple, more, heads):
    rows, width = triple.shape[0], triple.shape[1] // 3 // heads
    extra = more.shape[0]
    return [
        pl.BlockSpec((rows, width), lambda h: (0, h)),
        pl.BlockSpec((rows, width), lambda h: (0, heads + h)),
        pl.BlockSpec((rows, width), lambda h: (0, 2 * heads + h)),
        pl.BlockSpec((extra, width), lambda h: (0, h)),
        pl.BlockSpec((extra, width), lambda h: (0, heads + h)),
    ]


def self_forward(triple, more, groups):
    rows, model = triple.shape[0], triple.shape[1] // 3
    head = model // HEADS
    return pl.pallas_call(
        functools.partial(self_forward_kernel, groups, head**-0.5),
        out_shape=jax.ShapeDtypeStruct((rows, model), low_type),
        grid=(HEADS,),
        in_specs=self_specs(triple, more, HEADS),
        out_specs=pl.BlockSpec((rows, head), lambda h: (0, h)),
        compiler_params=params("arbitrary"),
        name="self_forward",
    )(triple, triple, triple, more, more)


def self_backward(triple, more, grads, groups):
    rows, model = triple.shape[0], triple.shape[1] // 3
    head = model // HEADS
    extra = more.shape[0]
    return pl.pallas_call(
        functools.partial(self_backward_kernel, groups, head**-0.5),
        out_shape=[
            jax.ShapeDtypeStruct((rows, 3 * model), low_type),
            jax.ShapeDtypeStruct((extra, 2 * model), low_type),
        ],
        grid=(HEADS,),
        in_specs=self_specs(triple, more, HEADS) + [pl.BlockSpec((rows, head), lambda h: (0, h))],
        out_specs=[
            pl.BlockSpec((rows, 3 * model), lambda h: (0, 0)),
            pl.BlockSpec((extra, 2 * model), lambda h: (0, 0)),
        ],
        compiler_params=params("arbitrary"),
        name="self_backward",
    )(triple, triple, triple, more, more, grads)


def widen_kernel(in_ref, out_ref):
    out_ref[...] = in_ref[...].astype(jnp.float32).reshape(out_ref.shape)


def side_by_side_rows(array, first, size, count):
    blocks, unused, width = array.shape
    rows = blocks * size
    if size % 16:
        parts = [array[:, (first + i) * size : (first + i + 1) * size] for i in range(count)]
        return jnp.concatenate([part.reshape(rows, width) for part in parts], axis=1).astype(jnp.float32)
    return pl.pallas_call(
        widen_kernel,
        out_shape=jax.ShapeDtypeStruct((rows, count * width), jnp.float32),
        grid=(count,),
        in_specs=[pl.BlockSpec((blocks, size, width), lambda i: (0, first + i, 0))],
        out_specs=pl.BlockSpec((rows, width), lambda i: (0, i)),
        compiler_params=params("arbitrary"),
        name="widen",
    )(array)


def ordered(bit, own, other, axis=0):
    first = jnp.where(bit == 0, own, other)
    last = jnp.where(bit == 0, other, own)
    return jnp.concatenate([first, last], axis=axis)


def half_of(array, bit, axis):
    size = array.shape[axis] // 2
    return lax.dynamic_slice_in_dim(array, bit * size, size, axis)


def swap(array, axis_name, mask):
    size = lax.axis_size(axis_name)
    return lax.ppermute(array, axis_name, [(i, i ^ mask) for i in range(size)])


class Plan:
    def __init__(self, micro_count, rows):
        self.blocks = lax.axis_size("blk")
        self.shards = lax.axis_size("fsdp")
        self.b = lax.axis_index("blk")
        self.x = lax.axis_index("fsdp")
        self.core = self.b & 1
        self.side = (self.b >> 1) & 1
        self.rows = rows
        self.micro_count = micro_count
        self.paired = self.shards == 2 and self.blocks % 4 == 0 and micro_count == 3
        if self.paired:
            self.micro = jnp.stack([self.x, jnp.int32(2)]).astype(jnp.int32)
            self.block_rows = rows
            self.per_item = 2
            self.groups = (
                (slice(0, 2 * rows), slice(0, 2 * rows), None),
                (slice(2 * rows, 3 * rows), slice(2 * rows, 3 * rows), slice(0, rows)),
            )
        else:
            self.micro = jnp.arange(micro_count, dtype=jnp.int32)
            self.block_rows = rows
            self.per_item = 1
            whole = rows * self.shards
            self.groups = tuple(
                (slice(i * rows, (i + 1) * rows), None, slice(i * whole, (i + 1) * whole))
                for i in range(micro_count)
            )

    def block_of(self, item, device):
        if self.paired and item == 1:
            return (device | 1) - 1 + self.x
        return device

    def turn(self, array):
        places = []
        for x in range(2):
            for b in range(self.blocks):
                core = b % 2
                places.append((b * 2 + x, (b - core + x) * 2 + core))
        return lax.ppermute(array, ("blk", "fsdp"), places)

    def spread(self, array):
        if not self.paired:
            return (array.reshape(-1, array.shape[-1]),)
        own = lax.dynamic_index_in_dim(array, self.x, 0, False)
        away = swap(lax.dynamic_index_in_dim(array, 1 - self.x, 0, False), "fsdp", 1)
        return own, away, self.turn(array[2])

    def send_back(self, array):
        if not self.paired:
            return (array,)
        own, away, shared = (array[i * self.rows : (i + 1) * self.rows] for i in range(3))
        return own, swap(away, "fsdp", 1), self.turn(shared)

    def placed(self, parts):
        if not self.paired:
            return parts[0].reshape(self.micro_count, self.rows, -1)
        own, other, shared = parts
        return jnp.stack([jnp.where(self.x == 0, own, other), jnp.where(self.x == 0, other, own), shared])

    def columns(self, pair, norms):
        if not self.paired:
            return (
                lax.all_gather(pair, "fsdp", axis=1, tiled=True),
                lax.all_gather(norms, "fsdp", axis=1, tiled=True),
            )
        flat = norms.reshape(-1, pair.shape[1])
        return (swap(jnp.concatenate([pair, flat], axis=0), "fsdp", 1),)

    def joined(self, pair, norms, other):
        if not self.paired:
            return other
        rows = pair.shape[0]
        return (
            ordered(self.x, pair, other[0][:rows], 1),
            ordered(self.x, norms, other[0][rows:].reshape(norms.shape), 1),
        )

    def fetch(self, weights, chips):
        if not self.paired:
            return None
        part = self.core if chips == 1 else 2 * self.core + self.side
        size = weights[0].shape[0] // (2 * chips)
        parts = [lax.dynamic_slice_in_dim(weight, part * size, size, 0) for weight in weights]
        return jnp.concatenate(parts, axis=1)

    def whole(self, weights, near, chips):
        if not self.paired:
            return [lax.all_gather(weight, "fsdp", axis=0, tiled=True) for weight in weights]
        if chips == 2:
            near = ordered(self.side, near, swap(near, "blk", 2))
        away = ordered(self.core, near, swap(near, "blk", 1))
        results, at = [], 0
        for weight in weights:
            results.append(ordered(self.x, weight, away[:, at : at + weight.shape[1]]))
            at += weight.shape[1]
        return results

    def partner_rows(self, pairs):
        if self.paired:
            return swap(pairs[2 * self.rows :], "blk", 1)
        wide = pairs.reshape(self.micro_count, self.rows, -1)
        return lax.all_gather(wide, "fsdp", axis=1, tiled=True).reshape(-1, wide.shape[-1])

    def own_pairs(self, wide, more):
        model = wide.shape[1] // 3
        if self.paired:
            back = swap(more, "blk", 1).astype(jnp.float32)
            first = 2 * self.rows
            last = (wide[first:, model:].astype(jnp.float32) + back).astype(low_type)
            return lax.dynamic_update_slice(wide, last, (first, model))
        split = more.reshape(self.micro_count, self.rows * self.shards, -1)
        back = lax.psum_scatter(split, "fsdp", scatter_dimension=1, tiled=True)
        return lax.dynamic_update_slice(wide, back.reshape(-1, back.shape[-1]), (0, model))


def added(kept, received):
    return (kept.astype(jnp.float32) + received.astype(jnp.float32)).astype(low_type)


def after(value, *others):
    return lax.optimization_barrier((value,) + others)[0]


class Group:
    def __init__(self, plan, units):
        self.plan = plan
        count, core = plan.blocks // 2, plan.core
        pieces = [unit.reshape(plan.shards, count, 2, -1, unit.shape[2]) for unit in units]
        self.sizes = [piece.shape[3] for piece in pieces]
        self.send = jnp.concatenate(
            [lax.dynamic_index_in_dim(piece, 1 - core, 2, False) for piece in pieces], axis=2
        )
        self.kept = jnp.concatenate([lax.dynamic_index_in_dim(piece, core, 2, False) for piece in pieces], axis=2)

    def over_core(self):
        received = swap(self.send, "blk", 1)
        mask = self.plan.shards // 2
        while mask:
            bit = jnp.where((self.plan.x & mask) > 0, 1, 0)
            self.send = added(half_of(self.kept, 1 - bit, 0), half_of(received, 1 - bit, 0))
            self.kept = added(half_of(self.kept, bit, 0), half_of(received, bit, 0))
            if mask > 1:
                received = swap(self.send, "fsdp", mask)
            mask //= 2
        return self.send

    def over_fsdp(self):
        received = swap(self.send, "fsdp", 1)
        self.total = added(self.kept, received)[0]
        return received


def over_chips(groups):
    plan = groups[0].plan
    total = jnp.concatenate([group.total for group in groups], axis=1)
    same_core = [list(range(core, plan.blocks, 2)) for core in range(2)]
    arrived = lax.all_to_all(
        total, "blk", split_axis=0, concat_axis=0, axis_index_groups=same_core, tiled=True
    )
    return jnp.sum(arrived.astype(jnp.float32), axis=0).astype(low_type), arrived


def from_all(sums):
    return lax.all_gather(jnp.concatenate(sums, axis=0), "blk", axis=0)


def gathered(array, sizes):
    results, at = [], 0
    for size in sizes:
        part = array[:, at : at + size].astype(jnp.float32)
        results.append(part.reshape(-1, part.shape[2]))
        at += size
    return results


def route_pixels(plan, pixels, segment_ids, pad_ids, block_map, fetch):
    blocks, labels = plan.blocks, block_map.shape[1]
    slots, features = pixels.shape[1:]
    width = slots // blocks
    routed = plan.micro.shape[0]
    label_ids = jnp.arange(labels, dtype=jnp.int32)

    def of_items(array):
        return jnp.stack([lax.dynamic_index_in_dim(array, plan.micro[i], 0, False) for i in range(routed)])

    picked = of_items(segment_ids)
    counts = jnp.sum((picked[:, None, :] == label_ids[None, :, None]).astype(jnp.int32), axis=2)
    counts = jnp.stack([counts >> 4, counts & 15], axis=1).astype(jnp.float32)
    counts = jnp.pad(counts, ((0, 0), (0, 6), (0, 128 - labels)))
    chunks = prepare_pixels(jnp.swapaxes(pixels, 1, 2), plan.micro, counts, width)
    spread = lax.all_to_all(chunks, "blk", split_axis=0, concat_axis=0, tiled=True)
    arrived = spread[:, :, features + 1 : features + 3, :labels].astype(jnp.int32)
    totals = jnp.sum(16 * arrived[:, :, 0] + arrived[:, :, 1], axis=0)
    owners = of_items(block_map)
    images = label_ids[None, :] != of_items(pad_ids)[:, None]
    totals = jnp.where(images, totals, 0)
    earlier = label_ids[None, :] < label_ids[:, None]
    starts = jnp.sum(jnp.where(earlier[None], totals[:, None, :], 0), axis=2)
    devices = jnp.arange(blocks, dtype=jnp.int32)

    def extents(wanted):
        hit = (owners[:, None, :] == wanted[:, :, None]) & images[:, None, :]
        start = jnp.sum(jnp.where(hit, starts[:, None, :], 0), axis=2)
        return start, start + jnp.sum(jnp.where(hit, totals[:, None, :], 0), axis=2)

    def chunk_at(start, place):
        first = start // width
        return first + ((place - first) & (blocks - 1))

    def source_of(chunk):
        return jnp.clip(chunk // blocks, 0, blocks - 1)

    item = jnp.arange(routed, dtype=jnp.int32)
    wanted = jnp.stack([plan.block_of(i, devices) for i in range(routed)])
    start, finish = extents(wanted)
    flat = spread.reshape(blocks * routed, FEATURE_ROWS, width)
    piece_at = source_of(chunk_at(start, plan.b)) * routed + item[:, None]
    pieces = jnp.take(flat, piece_at.T.reshape(-1), axis=0, mode="clip")
    pieces = pieces.reshape(blocks, routed, FEATURE_ROWS, width)
    fetched, sent = fetch(chunks, pieces)
    if sent is not None:
        pieces = after(pieces, sent)
    first = lax.all_to_all(pieces, "blk", split_axis=0, concat_axis=0, tiled=True)
    largest = jnp.argmax(totals, axis=1)
    largest_start = jnp.sum(jnp.where(label_ids[None, :] == largest[:, None], starts, 0), axis=1)
    second_at = source_of(chunk_at(largest_start, plan.b) + blocks) * routed + item
    second = lax.all_gather(jnp.take(flat, second_at, axis=0, mode="clip"), "blk", axis=0, tiled=False)
    mine = jnp.stack([plan.block_of(i, plan.b) for i in range(routed)])[:, None]
    start, finish = extents(mine)
    slot = (width * chunk_at(start, devices[None, :]))[:, :, None] + jnp.arange(width, dtype=jnp.int32)
    slot = slot.reshape(routed, -1)
    slot = jnp.concatenate([slot, slot + width * blocks], axis=1)
    mask = jnp.where((slot >= start) & (slot < finish), 0.0, masked_score)
    mask = jnp.broadcast_to(mask[:, None, :], (routed, 8, mask.shape[1]))
    big = ((finish - 1) // width - start // width >= blocks).astype(jnp.int32)[:, 0]
    if width < 128:
        join = 128 // width

        def merged(array):
            parts = array.reshape(blocks // join, join, routed, FEATURE_ROWS, width)
            return parts.transpose(0, 2, 3, 1, 4).reshape(blocks // join, routed, FEATURE_ROWS, 128)

        first, second = merged(first), merged(second)
    return fetched, first, second, mask, big


def on_device(
    latents,
    pixels,
    segment_ids,
    pad_ids,
    block_map,
    norm_gains,
    norm_biases,
    pixel_gain,
    pixel_bias,
    cross_query,
    cross_kv,
    cross_out,
    cross_up,
    cross_down,
    self_qkv,
    self_out,
    self_up,
    self_down,
    cotangent,
):
    micro_count, unused, rows, model = latents.shape
    features = pixels.shape[2]
    plan = Plan(micro_count, rows)
    scaling = model**-0.5

    norm_rows = jnp.concatenate([norm_gains, norm_biases], axis=0)
    early, middle = [cross_query], [cross_out, cross_up, cross_down]
    late, last = [self_qkv], [self_out, self_up, self_down]

    def fetch(chunks, pieces):
        if not plan.paired:
            return (plan.spread(latents[:, 0]), plan.columns(cross_kv, norm_rows)) + (None,) * 4, None
        latent = plan.spread(after(latents, chunks)[:, 0])
        near_early = swap(plan.fetch([after(cross_query, chunks)], 1), "fsdp", 1)
        other = plan.columns(after(cross_kv, chunks), norm_rows)
        send = plan.fetch([after(middle[0], near_early, *latent[1:], *other)] + middle[1:], 1)
        near_middle = swap(send, "fsdp", 1)
        near_late = swap(plan.fetch([after(late[0], send, pieces)], 2), "fsdp", 1)
        near_last = swap(plan.fetch([after(last[0], send, pieces)] + last[1:], 2), "fsdp", 1)
        latent = (latent[0],) + tuple(after(part, pieces) for part in latent[1:])
        near_early, other = after(near_early, pieces), (after(other[0], pieces),)
        return (latent, other, near_early, near_middle, near_late, near_last), send

    fetched, first, second, mask, big = route_pixels(plan, pixels, segment_ids, pad_ids, block_map, fetch)
    latent, other, near_early, near_middle, near_late, near_last = fetched
    latent = jnp.concatenate(latent, axis=0).astype(jnp.float32)
    w_pair, norms = plan.joined(cross_kv, norm_rows, other)
    norms = norms.astype(jnp.float32)
    gains, biases = norms[:4], norms[4:]
    w_key, w_value = w_pair[:, :model], w_pair[:, model:]
    (w_query,) = plan.whole(early, near_early, 1)
    pixel_scaler = pixel_gain.astype(jnp.float32)
    pixel_offset = pixel_bias.astype(jnp.float32)

    def widened(rows_f32, scale):
        against = jnp.sum(rows_f32 * pixel_offset, axis=-1, keepdims=True)
        wide = jnp.concatenate([rows_f32 * pixel_scaler, against], axis=1) * scale
        return jnp.pad(wide, ((0, 0), (0, FEATURE_ROWS - features - 1))).astype(low_type)

    def narrowed(wide):
        return wide[:, :features] * pixel_scaler + wide[:, features : features + 1] * pixel_offset

    normed, scale = normalise(latent)
    hidden = (normed * gains[0] + biases[0]).astype(low_type)
    queries = product(hidden, w_query).astype(low_type)
    query_features = product_nt(queries, w_key)
    wide_queries = widened(query_features, scaling)
    if plan.paired:
        near_middle, near_late = after(near_middle, wide_queries), after(near_late, first)
    w_out, w_up, w_down = plan.whole(middle, near_middle, 1)
    (w_triple,) = plan.whole(late, near_late, 2)
    summed = cross_call(
        cross_forward_kernel, big, [wide_queries], first, second, mask, plan.block_rows, plan.per_item
    )
    if plan.paired:
        near_last, cotangent = after(near_last, summed), after(cotangent, summed)
    w_self_out, w_self_up, w_self_down = plan.whole(last, near_last, 2)
    upstream = plan.spread(cotangent[:, 0])
    attended_features = narrowed(summed).astype(low_type)
    attended = product(attended_features, w_value).astype(low_type)
    first_sum = latent + product(attended, w_out)
    second_sum, stored_one = feed_forward(first_sum, gains[1], biases[1], w_up, w_down)
    normed_two, scale_two = normalise(second_sum)
    hidden_two = (normed_two * gains[2] + biases[2]).astype(low_type)
    triple = product(hidden_two, w_triple).astype(low_type)
    more = plan.partner_rows(triple[:, model:])
    blended = self_forward(triple, more, plan.groups)
    third_sum = second_sum + product(blended, w_self_out)
    mixed, stored_three = feed_forward(third_sum, gains[3], biases[3], w_self_up, w_self_down)
    mixed = mixed.astype(low_type)

    def unit(grad):
        return grad.astype(low_type).reshape(plan.shards, -1, model)

    if plan.paired:
        upstream = (upstream[0],) + tuple(after(part, third_sum) for part in upstream[1:])
    upstream = jnp.concatenate(upstream, axis=0).astype(jnp.float32)
    low = upstream.astype(low_type)
    upstream, grad_self_up, grad_self_down, gain_three, bias_three = feed_backward(
        upstream, low, third_sum, stored_three, gains[3], w_self_up, w_self_down
    )
    low = upstream.astype(low_type)
    grad_self_out = product_tn(blended, low)
    grad_self_out = product_tn(blended, low)
    one = Group(plan, [unit(grad_self_up), unit(grad_self_down)])
    grad_blended = product_nt(low, w_self_out).astype(low_type)
    grad_blended = after(grad_blended, one.over_core(), mixed)
    triple_grads, more_grads = self_backward(triple, more, grad_blended, plan.groups)
    triple_grads, more_grads = after((triple_grads, more_grads), one.over_fsdp())
    triple_grads = plan.own_pairs(triple_grads, more_grads)
    grad_q, grad_k, grad_v = (
        unit(product_tn(hidden_two, triple_grads[:, i * model : (i + 1) * model])) for i in range(3)
    )
    two, three = Group(plan, [grad_q, grad_k]), Group(plan, [grad_v, unit(grad_self_out)])
    triple_grads = after(triple_grads, two.send, three.send)
    sums_one, arrived_one = over_chips([one])
    grad_hidden = product_nt(triple_grads, w_triple)
    down, gain_two, bias_two = norm_backward(grad_hidden, normed_two, scale_two, gains[2])
    upstream = upstream + down
    low = upstream.astype(low_type)
    grad_down = product_tn(stored_one[2], low)
    low = after(low, two.over_core())
    upstream, grad_up, unused, gain_one, bias_one = feed_backward(
        upstream, low, first_sum, stored_one, gains[1], w_up, w_down
    )
    low = after(upstream.astype(low_type), two.over_fsdp(), three.over_core(), arrived_one)
    grad_out = product_tn(attended, low)
    four = Group(plan, [unit(grad_up), unit(grad_down), unit(grad_out)])
    grad_attended = product_nt(low, w_out).astype(low_type)
    grad_value = product_tn(attended_features, grad_attended)
    grad_features = product_nt(grad_attended, w_value)
    wide_grads = after(widened(grad_features, 1.0), four.send)
    score_sums = cross_call(
        cross_backward_kernel,
        big,
        [wide_queries, wide_grads],
        first,
        second,
        mask,
        plan.block_rows,
        plan.per_item,
    )
    score_sums = after(score_sums, three.over_fsdp(), four.over_core())
    sums_two, arrived_two = over_chips([two, three])
    key_sums = (narrowed(score_sums) * scaling).astype(low_type)
    grad_queries = product(key_sums, w_key).astype(low_type)
    grad_key = product_tn(key_sums, queries)
    pixel_gain_term = jnp.sum(
        query_features * score_sums[:, :features] * scaling + grad_features * summed[:, :features], axis=0
    )
    pixel_bias_term = jnp.sum(
        query_features * score_sums[:, features : features + 1] * scaling
        + grad_features * summed[:, features : features + 1],
        axis=0,
    )
    grad_query = product_tn(hidden, grad_queries)
    down, gain_zero, bias_zero = norm_backward(product_nt(grad_queries, w_query), normed, scale, gains[0])
    latents_grad = (upstream + down).astype(low_type)

    shards = plan.shards
    width = 2 * model // shards
    rows_of_pair = jnp.pad(jnp.concatenate([grad_key, grad_value], axis=1), ((0, 264 - features), (0, 0)))
    norm_terms = jnp.stack(
        [gain_zero, gain_one, gain_two, gain_three, bias_zero, bias_one, bias_two, bias_three]
    )
    pixel_terms = jnp.pad(jnp.stack([pixel_gain_term, pixel_bias_term]), ((0, 0), (0, 512 - features)))
    pixel_rows = pixel_terms.reshape(1, -1, width)
    tall = jnp.concatenate(
        [
            rows_of_pair.reshape(264, shards, width).transpose(1, 0, 2),
            norm_terms.reshape(8, shards, model // shards).transpose(1, 0, 2).reshape(shards, 4, width),
            jnp.broadcast_to(pixel_rows, (shards,) + pixel_rows.shape[1:]),
            jnp.zeros((shards, 384 - 268 - pixel_rows.shape[1], width), jnp.float32),
        ],
        axis=1,
    )
    five = Group(plan, [unit(grad_query), tall.astype(low_type).reshape(shards, -1, model)])
    five.send = after(five.send, four.over_fsdp(), arrived_two)
    early_sums = from_all([sums_one, sums_two])
    sums_four, unused = over_chips([four])
    five.over_core()
    arrived = five.over_fsdp()
    mixed = plan.send_back(after(mixed, arrived))
    latents_grad = plan.send_back(after(latents_grad, arrived))
    sums_five, unused = over_chips([five])
    late_sums = from_all([sums_four, sums_five])
    size = one.sizes[0]
    grad_self_up, grad_self_down = gathered(early_sums, one.sizes)
    grad_triple = side_by_side_rows(early_sums, 2, size, 3)
    (grad_self_out,) = gathered(early_sums[:, 5 * size :], [size])
    latents_grad = plan.placed(latents_grad).astype(jnp.float32)
    grad_up, grad_down, grad_out, grad_query, tall = gathered(late_sums, four.sizes + five.sizes)
    tall = tall.reshape(384, width)
    norm_part = tall[264:268].reshape(8, model // shards)
    pixel_part = tall[268 : 268 + pixel_rows.shape[1]].reshape(2, 512)
    return (
        plan.placed(mixed)[:, None],
        latents_grad[:, None],
        norm_part[:4],
        norm_part[4:],
        pixel_part[0, :features],
        pixel_part[1, :features],
        grad_query,
        tall[:features],
        grad_out,
        grad_up,
        grad_down,
        grad_triple,
        grad_self_out,
        grad_self_up,
        grad_self_down,
    )


def solution(mesh):
    placed = (
        P(None, "blk", "fsdp", None),
        P(None, "blk", None),
        P(None, "blk"),
        P(),
        P(),
        P(None, "fsdp"),
        P(None, "fsdp"),
        P(),
        P(),
        P("fsdp", None),
        P(None, "fsdp"),
        P("fsdp", None),
        P("fsdp", None),
        P("fsdp", None),
        P("fsdp", None),
        P("fsdp", None),
        P("fsdp", None),
        P("fsdp", None),
        P(None, "blk", "fsdp", None),
    )
    return jax.shard_map(
        on_device,
        mesh=mesh,
        in_specs=placed,
        out_specs=(
            P(None, "blk", "fsdp", None),
            P(None, "blk", "fsdp", None),
            P(None, "fsdp"),
            P(None, "fsdp"),
            P(),
            P(),
            P("fsdp", None),
            P(None, "fsdp"),
            P("fsdp", None),
            P("fsdp", None),
            P("fsdp", None),
            P("fsdp", None),
            P("fsdp", None),
            P("fsdp", None),
            P("fsdp", None),
        ),
        check_vma=False,
    )
```

```python
import functools

import jax
import jax.numpy as jnp
from jax import lax
from jax.experimental import pallas as pl
from jax.experimental.pallas import tpu as pltpu
from jax.sharding import PartitionSpec as P

HEADS = 8
FEATURE_ROWS = 272
VMEM_LIMIT = 56 * 1024 * 1024

epsilon = 1e-05
masked_score = -1e30
low_type = jnp.bfloat16


def product(a, b):
    return jnp.dot(a, b, preferred_element_type=jnp.float32)


def product_tn(a, b):
    return lax.dot_general(a, b, (((0,), (0,)), ((), ())), preferred_element_type=jnp.float32)


def product_nt(a, b):
    return lax.dot_general(a, b, (((1,), (1,)), ((), ())), preferred_element_type=jnp.float32)


def normalise(rows):
    centre = rows - jnp.mean(rows, axis=-1, keepdims=True)
    scale = lax.rsqrt(jnp.mean(centre * centre, axis=-1, keepdims=True) + epsilon)
    return centre * scale, scale


def norm_backward(upstream, normed, scale, gain):
    gain_term = jnp.sum(upstream * normed, axis=0)
    bias_term = jnp.sum(upstream, axis=0)
    inner = upstream * gain
    down = scale * (
        inner
        - jnp.mean(inner, axis=-1, keepdims=True)
        - normed * jnp.mean(inner * normed, axis=-1, keepdims=True)
    )
    return down, gain_term, bias_term


def feed_forward(rows, gain, bias, w_up, w_down):
    normed, scale = normalise(rows)
    hidden = (normed * gain + bias).astype(low_type)
    upward = product(hidden, w_up)
    share = 0.5 * (1.0 + lax.erf(upward * (0.5**0.5)))
    slope = share + upward * jnp.exp(-0.5 * upward * upward) * 0.3989422804014327
    active = (upward * share).astype(low_type)
    return rows + product(active, w_down), (hidden, slope, active)


def feed_backward(upstream, low, rows, stored, gain, w_up, w_down):
    hidden, slope, active = stored
    grad_down = product_tn(active, low)
    grad_upward = (product_nt(low, w_down) * slope).astype(low_type)
    grad_up = product_tn(hidden, grad_upward)
    normed, scale = normalise(rows)
    down, gain_term, bias_term = norm_backward(product_nt(grad_upward, w_up), normed, scale, gain)
    return upstream + down, grad_up, grad_down, gain_term, bias_term


def nt(a, b):
    return lax.dot_general(a, b, (((1,), (1,)), ((), ())), preferred_element_type=jnp.float32)


def tn(a, b):
    return lax.dot_general(a, b, (((0,), (0,)), ((), ())), preferred_element_type=jnp.float32)


def params(*semantics):
    return pltpu.CompilerParams(dimension_semantics=semantics, vmem_limit_bytes=VMEM_LIMIT)


def pixel_kernel(micro_ref, pixel_ref, count_ref, out_ref):
    features = pixel_ref.shape[1]
    width = out_ref.shape[3]
    pixels = pixel_ref[0].astype(jnp.float32)
    centre = pixels - jnp.mean(pixels, axis=0, keepdims=True)
    spread = jnp.mean(centre * centre, axis=0, keepdims=True)
    normed = centre * lax.rsqrt(spread + epsilon)
    pad = jnp.zeros((FEATURE_ROWS - features, normed.shape[1]), jnp.float32)
    tall = jnp.concatenate([normed, pad], axis=0)
    row = lax.broadcasted_iota(jnp.int32, (FEATURE_ROWS, width), 0)
    high, rest = count_ref[0][:1, :width], count_ref[0][1:2, :width]
    for part in range(out_ref.shape[0]):
        piece = tall[:, part * width : (part + 1) * width]
        piece = jnp.where(row == features, 1.0, piece)
        piece = jnp.where(row == features + 1, high, jnp.where(row == features + 2, rest, piece))
        out_ref[part, 0] = piece.astype(low_type)


def prepare_pixels(pixels, micro, counts, width):
    routed = micro.shape[0]
    features, slots = pixels.shape[1:]
    step = min(slots, 1024)
    return pl.pallas_call(
        pixel_kernel,
        out_shape=jax.ShapeDtypeStruct((slots // width, routed, FEATURE_ROWS, width), low_type),
        grid_spec=pltpu.PrefetchScalarGridSpec(
            num_scalar_prefetch=1,
            grid=(routed, slots // step),
            in_specs=[
                pl.BlockSpec((1, features, step), lambda i, s, m: (m[i], 0, s)),
                pl.BlockSpec((1, 8, 128), lambda i, s, m: (i, 0, 0)),
            ],
            out_specs=pl.BlockSpec((step // width, 1, FEATURE_ROWS, width), lambda i, s, m: (s, i, 0, 0)),
        ),
        compiler_params=params("arbitrary", "arbitrary"),
        name="prepare_pixels",
    )(micro, pixels, counts)


def side_by_side(ref):
    return jnp.concatenate([ref[tile, 0] for tile in range(ref.shape[0])], axis=1)


def cross_forward_kernel(items, big_ref, query_ref, first_ref, second_ref, mask_ref, out_ref):
    item = pl.program_id(0) // items
    lanes = mask_ref.shape[2] // 2

    def attend(features, mask):
        scores = product(query_ref[...], features) + mask
        top = jnp.max(scores, axis=-1, keepdims=True)
        weights = jnp.exp(scores - top)
        total = jnp.sum(weights, axis=-1, keepdims=True)
        out_ref[...] = nt(weights.astype(low_type), features) / total

    @pl.when(big_ref[item] == 0)
    def small():
        attend(side_by_side(first_ref), mask_ref[0][:1, :lanes])

    @pl.when(big_ref[item] != 0)
    def large():
        both = jnp.concatenate([side_by_side(first_ref), side_by_side(second_ref)], axis=1)
        attend(both, mask_ref[0][:1])


def cross_backward_kernel(items, big_ref, query_ref, grad_ref, first_ref, second_ref, mask_ref, out_ref):
    item = pl.program_id(0) // items
    lanes = mask_ref.shape[2] // 2

    def attend(features, mask):
        scores = product(query_ref[...], features) + mask
        top = jnp.max(scores, axis=-1, keepdims=True)
        weights = jnp.exp(scores - top)
        shares = weights / jnp.sum(weights, axis=-1, keepdims=True)
        grad_shares = product(grad_ref[...], features)
        inner = jnp.sum(shares * grad_shares, axis=-1, keepdims=True)
        grad_scores = (shares * (grad_shares - inner)).astype(low_type)
        out_ref[...] = nt(grad_scores, features)

    @pl.when(big_ref[item] == 0)
    def small():
        attend(side_by_side(first_ref), mask_ref[0][:1, :lanes])

    @pl.when(big_ref[item] != 0)
    def large():
        both = jnp.concatenate([side_by_side(first_ref), side_by_side(second_ref)], axis=1)
        attend(both, mask_ref[0][:1])


def cross_call(kernel, big, rows, first, second, mask, block, per_item):
    count = rows[0].shape[0]
    tiles, width = first.shape[0], first.shape[3]
    row_spec = pl.BlockSpec((block, FEATURE_ROWS), lambda i, big: (i, 0))
    tile_spec = pl.BlockSpec((tiles, 1, FEATURE_ROWS, width), lambda i, big: (0, i // per_item, 0, 0))
    return pl.pallas_call(
        functools.partial(kernel, per_item),
        out_shape=jax.ShapeDtypeStruct((count, FEATURE_ROWS), jnp.float32),
        grid_spec=pltpu.PrefetchScalarGridSpec(
            num_scalar_prefetch=1,
            grid=(count // block,),
            in_specs=[row_spec] * len(rows)
            + [tile_spec, tile_spec]
            + [pl.BlockSpec((1, 8, mask.shape[2]), lambda i, big: (i // per_item, 0, 0))],
            out_specs=row_spec,
        ),
        compiler_params=params("arbitrary"),
        name="cross_attention",
    )(big, *rows, first, second, mask)


def self_forward_kernel(groups, scaling, q_ref, k_ref, v_ref, more_k_ref, more_v_ref, out_ref):
    for q_rows, own, more in groups:
        keys, values = keys_of(own, more, k_ref, v_ref, more_k_ref, more_v_ref)
        scores = nt(q_ref[q_rows], keys) * scaling
        weights = jnp.exp(scores - jnp.max(scores, axis=-1, keepdims=True))
        total = jnp.sum(weights, axis=-1, keepdims=True)
        out_ref[q_rows, :] = (product(weights.astype(low_type), values) / total).astype(low_type)


def keys_of(own, more, k_ref, v_ref, more_k_ref, more_v_ref):
    keys, values = [], []
    if own is not None:
        keys.append(k_ref[own])
        values.append(v_ref[own])
    if more is not None:
        keys.append(more_k_ref[more])
        values.append(more_v_ref[more])
    if len(keys) == 1:
        return keys[0], values[0]
    return jnp.concatenate(keys, axis=0), jnp.concatenate(values, axis=0)


def self_backward_kernel(
    groups,
    scaling,
    q_ref,
    k_ref,
    v_ref,
    more_k_ref,
    more_v_ref,
    grad_ref,
    wide_ref,
    more_ref,
):
    head = q_ref.shape[1]
    model = wide_ref.shape[1] // 3
    column = pl.multiple_of(pl.program_id(0) * head, head)
    at_q, at_k, at_v = (pl.ds(pl.multiple_of(part * model + column, head), head) for part in range(3))
    for q_rows, own, more in groups:
        keys, values = keys_of(own, more, k_ref, v_ref, more_k_ref, more_v_ref)
        queries = q_ref[q_rows]
        grads = grad_ref[q_rows]
        scores = nt(keys, queries) * scaling
        weights = jnp.exp(scores - jnp.max(scores, axis=0, keepdims=True))
        shares = weights / jnp.sum(weights, axis=0, keepdims=True)
        grad_shares = nt(values, grads)
        inner = jnp.sum(shares * grad_shares, axis=0, keepdims=True)
        grad_scores = (shares * (grad_shares - inner)).astype(low_type)
        wide_ref[q_rows, at_q] = (tn(grad_scores, keys) * scaling).astype(low_type)
        dk = (product(grad_scores, queries) * scaling).astype(low_type)
        dv = product(shares.astype(low_type), grads).astype(low_type)
        split = 0
        if own is not None:
            split = own.stop - own.start
            wide_ref[own, at_k] = dk[:split]
            wide_ref[own, at_v] = dv[:split]
        if more is not None:
            more_ref[more, at_q] = dk[split:]
            more_ref[more, at_k] = dv[split:]


def self_specs(triple, more, heads):
    rows, width = triple.shape[0], triple.shape[1] // 3 // heads
    extra = more.shape[0]
    return [
        pl.BlockSpec((rows, width), lambda h: (0, h)),
        pl.BlockSpec((rows, width), lambda h: (0, heads + h)),
        pl.BlockSpec((rows, width), lambda h: (0, 2 * heads + h)),
        pl.BlockSpec((extra, width), lambda h: (0, h)),
        pl.BlockSpec((extra, width), lambda h: (0, heads + h)),
    ]


def self_forward(triple, more, groups):
    rows, model = triple.shape[0], triple.shape[1] // 3
    head = model // HEADS
    return pl.pallas_call(
        functools.partial(self_forward_kernel, groups, head**-0.5),
        out_shape=jax.ShapeDtypeStruct((rows, model), low_type),
        grid=(HEADS,),
        in_specs=self_specs(triple, more, HEADS),
        out_specs=pl.BlockSpec((rows, head), lambda h: (0, h)),
        compiler_params=params("arbitrary"),
        name="self_forward",
    )(triple, triple, triple, more, more)


def self_backward(triple, more, grads, groups):
    rows, model = triple.shape[0], triple.shape[1] // 3
    head = model // HEADS
    extra = more.shape[0]
    return pl.pallas_call(
        functools.partial(self_backward_kernel, groups, head**-0.5),
        out_shape=[
            jax.ShapeDtypeStruct((rows, 3 * model), low_type),
            jax.ShapeDtypeStruct((extra, 2 * model), low_type),
        ],
        grid=(HEADS,),
        in_specs=self_specs(triple, more, HEADS) + [pl.BlockSpec((rows, head), lambda h: (0, h))],
        out_specs=[
            pl.BlockSpec((rows, 3 * model), lambda h: (0, 0)),
            pl.BlockSpec((extra, 2 * model), lambda h: (0, 0)),
        ],
        compiler_params=params("arbitrary"),
        name="self_backward",
    )(triple, triple, triple, more, more, grads)


def widen_kernel(in_ref, out_ref):
    out_ref[...] = in_ref[...].astype(jnp.float32).reshape(out_ref.shape)


def side_by_side_rows(array, first, size, count):
    blocks, unused, width = array.shape
    rows = blocks * size
    if size % 16:
        parts = [array[:, (first + i) * size : (first + i + 1) * size] for i in range(count)]
        return jnp.concatenate([part.reshape(rows, width) for part in parts], axis=1).astype(jnp.float32)
    return pl.pallas_call(
        widen_kernel,
        out_shape=jax.ShapeDtypeStruct((rows, count * width), jnp.float32),
        grid=(count,),
        in_specs=[pl.BlockSpec((blocks, size, width), lambda i: (0, first + i, 0))],
        out_specs=pl.BlockSpec((rows, width), lambda i: (0, i)),
        compiler_params=params("arbitrary"),
        name="widen",
    )(array)


def ordered(bit, own, other, axis=0):
    first = jnp.where(bit == 0, own, other)
    last = jnp.where(bit == 0, other, own)
    return jnp.concatenate([first, last], axis=axis)


def half_of(array, bit, axis):
    size = array.shape[axis] // 2
    return lax.dynamic_slice_in_dim(array, bit * size, size, axis)


def swap(array, axis_name, mask):
    size = lax.axis_size(axis_name)
    return lax.ppermute(array, axis_name, [(i, i ^ mask) for i in range(size)])


class Plan:
    def __init__(self, micro_count, rows):
        self.blocks = lax.axis_size("blk")
        self.shards = lax.axis_size("fsdp")
        self.b = lax.axis_index("blk")
        self.x = lax.axis_index("fsdp")
        self.core = self.b & 1
        self.side = (self.b >> 1) & 1
        self.rows = rows
        self.micro_count = micro_count
        self.paired = self.shards == 2 and self.blocks % 4 == 0 and micro_count == 3
        if self.paired:
            self.micro = jnp.stack([self.x, jnp.int32(2)]).astype(jnp.int32)
            self.block_rows = rows
            self.per_item = 2
            self.groups = (
                (slice(0, 2 * rows), slice(0, 2 * rows), None),
                (slice(2 * rows, 3 * rows), slice(2 * rows, 3 * rows), slice(0, rows)),
            )
        else:
            self.micro = jnp.arange(micro_count, dtype=jnp.int32)
            self.block_rows = rows
            self.per_item = 1
            whole = rows * self.shards
            self.groups = tuple(
                (slice(i * rows, (i + 1) * rows), None, slice(i * whole, (i + 1) * whole))
                for i in range(micro_count)
            )

    def block_of(self, item, device):
        if self.paired and item == 1:
            return (device | 1) - 1 + self.x
        return device

    def turn(self, array):
        places = []
        for x in range(2):
            for b in range(self.blocks):
                core = b % 2
                places.append((b * 2 + x, (b - core + x) * 2 + core))
        return lax.ppermute(array, ("blk", "fsdp"), places)

    def spread(self, array):
        if not self.paired:
            return (array.reshape(-1, array.shape[-1]),)
        own = lax.dynamic_index_in_dim(array, self.x, 0, False)
        away = swap(lax.dynamic_index_in_dim(array, 1 - self.x, 0, False), "fsdp", 1)
        return own, away, self.turn(array[2])

    def send_back(self, array):
        if not self.paired:
            return (array,)
        own, away, shared = (array[i * self.rows : (i + 1) * self.rows] for i in range(3))
        return own, swap(away, "fsdp", 1), self.turn(shared)

    def placed(self, parts):
        if not self.paired:
            return parts[0].reshape(self.micro_count, self.rows, -1)
        own, other, shared = parts
        return jnp.stack([jnp.where(self.x == 0, own, other), jnp.where(self.x == 0, other, own), shared])

    def columns(self, pair, norms):
        if not self.paired:
            return (
                lax.all_gather(pair, "fsdp", axis=1, tiled=True),
                lax.all_gather(norms, "fsdp", axis=1, tiled=True),
            )
        flat = norms.reshape(-1, pair.shape[1])
        return (swap(jnp.concatenate([pair, flat], axis=0), "fsdp", 1),)

    def joined(self, pair, norms, other):
        if not self.paired:
            return other
        rows = pair.shape[0]
        return (
            ordered(self.x, pair, other[0][:rows], 1),
            ordered(self.x, norms, other[0][rows:].reshape(norms.shape), 1),
        )

    def fetch(self, weights, chips):
        if not self.paired:
            return None
        part = self.core if chips == 1 else 2 * self.core + self.side
        size = weights[0].shape[0] // (2 * chips)
        parts = [lax.dynamic_slice_in_dim(weight, part * size, size, 0) for weight in weights]
        return jnp.concatenate(parts, axis=1)

    def whole(self, weights, near, chips):
        if not self.paired:
            return [lax.all_gather(weight, "fsdp", axis=0, tiled=True) for weight in weights]
        if chips == 2:
            near = ordered(self.side, near, swap(near, "blk", 2))
        away = ordered(self.core, near, swap(near, "blk", 1))
        results, at = [], 0
        for weight in weights:
            results.append(ordered(self.x, weight, away[:, at : at + weight.shape[1]]))
            at += weight.shape[1]
        return results

    def partner_rows(self, pairs):
        if self.paired:
            return swap(pairs[2 * self.rows :], "blk", 1)
        wide = pairs.reshape(self.micro_count, self.rows, -1)
        return lax.all_gather(wide, "fsdp", axis=1, tiled=True).reshape(-1, wide.shape[-1])

    def own_pairs(self, wide, more):
        model = wide.shape[1] // 3
        if self.paired:
            back = swap(more, "blk", 1).astype(jnp.float32)
            first = 2 * self.rows
            last = (wide[first:, model:].astype(jnp.float32) + back).astype(low_type)
            return lax.dynamic_update_slice(wide, last, (first, model))
        split = more.reshape(self.micro_count, self.rows * self.shards, -1)
        back = lax.psum_scatter(split, "fsdp", scatter_dimension=1, tiled=True)
        return lax.dynamic_update_slice(wide, back.reshape(-1, back.shape[-1]), (0, model))


def added(kept, received):
    return (kept.astype(jnp.float32) + received.astype(jnp.float32)).astype(low_type)


def after(value, *others):
    if not others:
        return value
    return lax.optimization_barrier((value,) + others)[0]


class Group:
    def __init__(self, plan, units):
        self.plan = plan
        count, core = plan.blocks // 2, plan.core
        pieces = [unit.reshape(plan.shards, count, 2, -1, unit.shape[2]) for unit in units]
        self.sizes = [piece.shape[3] for piece in pieces]
        self.send = jnp.concatenate(
            [lax.dynamic_index_in_dim(piece, 1 - core, 2, False) for piece in pieces], axis=2
        )
        self.kept = jnp.concatenate([lax.dynamic_index_in_dim(piece, core, 2, False) for piece in pieces], axis=2)

    def over_core(self, *earlier):
        received = after(swap(self.send, "blk", 1), *earlier)
        mask = self.plan.shards // 2
        while mask:
            bit = jnp.where((self.plan.x & mask) > 0, 1, 0)
            self.send = added(half_of(self.kept, 1 - bit, 0), half_of(received, 1 - bit, 0))
            self.kept = added(half_of(self.kept, bit, 0), half_of(received, bit, 0))
            if mask > 1:
                received = swap(self.send, "fsdp", mask)
            mask //= 2
        return self.send

    def over_fsdp(self, *earlier):
        received = after(swap(self.send, "fsdp", 1), *earlier)
        self.total = added(self.kept, received)[0]
        return received


def over_chips(groups, *earlier):
    plan = groups[0].plan
    total = jnp.concatenate([group.total for group in groups], axis=1)
    same_core = [list(range(core, plan.blocks, 2)) for core in range(2)]
    arrived = lax.all_to_all(
        total, "blk", split_axis=0, concat_axis=0, axis_index_groups=same_core, tiled=True
    )
    arrived = after(arrived, *earlier)
    return jnp.sum(arrived.astype(jnp.float32), axis=0).astype(low_type), arrived


def from_all(sums):
    return lax.all_gather(jnp.concatenate(sums, axis=0), "blk", axis=0)


def gathered(array, sizes):
    results, at = [], 0
    for size in sizes:
        part = array[:, at : at + size].astype(jnp.float32)
        results.append(part.reshape(-1, part.shape[2]))
        at += size
    return results


def route_pixels(plan, pixels, segment_ids, pad_ids, block_map, fetch):
    blocks, labels = plan.blocks, block_map.shape[1]
    slots, features = pixels.shape[1:]
    width = slots // blocks
    routed = plan.micro.shape[0]
    label_ids = jnp.arange(labels, dtype=jnp.int32)

    def of_items(array):
        return jnp.stack([lax.dynamic_index_in_dim(array, plan.micro[i], 0, False) for i in range(routed)])

    picked = of_items(segment_ids)
    counts = jnp.sum((picked[:, None, :] == label_ids[None, :, None]).astype(jnp.int32), axis=2)
    counts = jnp.stack([counts >> 4, counts & 15], axis=1).astype(jnp.float32)
    counts = jnp.pad(counts, ((0, 0), (0, 6), (0, 128 - labels)))
    chunks = prepare_pixels(jnp.swapaxes(pixels, 1, 2), plan.micro, counts, width)
    spread = lax.all_to_all(chunks, "blk", split_axis=0, concat_axis=0, tiled=True)
    arrived = spread[:, :, features + 1 : features + 3, :labels].astype(jnp.int32)
    totals = jnp.sum(16 * arrived[:, :, 0] + arrived[:, :, 1], axis=0)
    owners = of_items(block_map)
    images = label_ids[None, :] != of_items(pad_ids)[:, None]
    totals = jnp.where(images, totals, 0)
    earlier = label_ids[None, :] < label_ids[:, None]
    starts = jnp.sum(jnp.where(earlier[None], totals[:, None, :], 0), axis=2)
    devices = jnp.arange(blocks, dtype=jnp.int32)

    def extents(wanted):
        hit = (owners[:, None, :] == wanted[:, :, None]) & images[:, None, :]
        start = jnp.sum(jnp.where(hit, starts[:, None, :], 0), axis=2)
        return start, start + jnp.sum(jnp.where(hit, totals[:, None, :], 0), axis=2)

    def chunk_at(start, place):
        first = start // width
        return first + ((place - first) & (blocks - 1))

    def source_of(chunk):
        return jnp.clip(chunk // blocks, 0, blocks - 1)

    item = jnp.arange(routed, dtype=jnp.int32)
    wanted = jnp.stack([plan.block_of(i, devices) for i in range(routed)])
    start, finish = extents(wanted)
    flat = spread.reshape(blocks * routed, FEATURE_ROWS, width)
    piece_at = source_of(chunk_at(start, plan.b)) * routed + item[:, None]
    pieces = jnp.take(flat, piece_at.T.reshape(-1), axis=0, mode="clip")
    pieces = pieces.reshape(blocks, routed, FEATURE_ROWS, width)
    fetched, sent = fetch(chunks, pieces)
    if sent is not None:
        pieces = after(pieces, sent)
    first = lax.all_to_all(pieces, "blk", split_axis=0, concat_axis=0, tiled=True)
    largest = jnp.argmax(totals, axis=1)
    largest_start = jnp.sum(jnp.where(label_ids[None, :] == largest[:, None], starts, 0), axis=1)
    second_at = source_of(chunk_at(largest_start, plan.b) + blocks) * routed + item
    second = lax.all_gather(jnp.take(flat, second_at, axis=0, mode="clip"), "blk", axis=0, tiled=False)
    mine = jnp.stack([plan.block_of(i, plan.b) for i in range(routed)])[:, None]
    start, finish = extents(mine)
    slot = (width * chunk_at(start, devices[None, :]))[:, :, None] + jnp.arange(width, dtype=jnp.int32)
    slot = slot.reshape(routed, -1)
    slot = jnp.concatenate([slot, slot + width * blocks], axis=1)
    mask = jnp.where((slot >= start) & (slot < finish), 0.0, masked_score)
    mask = jnp.broadcast_to(mask[:, None, :], (routed, 8, mask.shape[1]))
    big = ((finish - 1) // width - start // width >= blocks).astype(jnp.int32)[:, 0]
    if width < 128:
        join = 128 // width

        def merged(array):
            parts = array.reshape(blocks // join, join, routed, FEATURE_ROWS, width)
            return parts.transpose(0, 2, 3, 1, 4).reshape(blocks // join, routed, FEATURE_ROWS, 128)

        first, second = merged(first), merged(second)
    return fetched, first, second, mask, big


def on_device(
    latents,
    pixels,
    segment_ids,
    pad_ids,
    block_map,
    norm_gains,
    norm_biases,
    pixel_gain,
    pixel_bias,
    cross_query,
    cross_kv,
    cross_out,
    cross_up,
    cross_down,
    self_qkv,
    self_out,
    self_up,
    self_down,
    cotangent,
):
    micro_count, unused, rows, model = latents.shape
    features = pixels.shape[2]
    plan = Plan(micro_count, rows)
    scaling = model**-0.5

    norm_rows = jnp.concatenate([norm_gains, norm_biases], axis=0)
    early, middle = [cross_query], [cross_out, cross_up, cross_down]
    late, last = [self_qkv], [self_out, self_up, self_down]

    def fetch(chunks, pieces):
        if not plan.paired:
            return (plan.spread(latents[:, 0]), plan.columns(cross_kv, norm_rows)) + (None,) * 4, None
        latent = plan.spread(after(latents, chunks)[:, 0])
        near_early = swap(plan.fetch([after(cross_query, chunks)], 1), "fsdp", 1)
        other = plan.columns(after(cross_kv, chunks), norm_rows)
        send = plan.fetch([after(middle[0], near_early, *latent[1:], *other)] + middle[1:], 1)
        near_middle = swap(send, "fsdp", 1)
        near_late = swap(plan.fetch([after(late[0], send, pieces)], 2), "fsdp", 1)
        near_last = swap(plan.fetch([after(last[0], send, pieces)] + last[1:], 2), "fsdp", 1)
        latent = (latent[0],) + tuple(after(part, pieces) for part in latent[1:])
        near_early, other = after(near_early, pieces), (after(other[0], pieces),)
        return (latent, other, near_early, near_middle, near_late, near_last), send

    fetched, first, second, mask, big = route_pixels(plan, pixels, segment_ids, pad_ids, block_map, fetch)
    latent, other, near_early, near_middle, near_late, near_last = fetched
    latent = jnp.concatenate(latent, axis=0).astype(jnp.float32)
    w_pair, norms = plan.joined(cross_kv, norm_rows, other)
    norms = norms.astype(jnp.float32)
    gains, biases = norms[:4], norms[4:]
    w_key, w_value = w_pair[:, :model], w_pair[:, model:]
    (w_query,) = plan.whole(early, near_early, 1)
    pixel_scaler = pixel_gain.astype(jnp.float32)
    pixel_offset = pixel_bias.astype(jnp.float32)

    def widened(rows_f32, scale):
        against = jnp.sum(rows_f32 * pixel_offset, axis=-1, keepdims=True)
        wide = jnp.concatenate([rows_f32 * pixel_scaler, against], axis=1) * scale
        return jnp.pad(wide, ((0, 0), (0, FEATURE_ROWS - features - 1))).astype(low_type)

    def narrowed(wide):
        return wide[:, :features] * pixel_scaler + wide[:, features : features + 1] * pixel_offset

    normed, scale = normalise(latent)
    hidden = (normed * gains[0] + biases[0]).astype(low_type)
    queries = product(hidden, w_query).astype(low_type)
    query_features = product_nt(queries, w_key)
    wide_queries = widened(query_features, scaling)
    if plan.paired:
        near_middle, near_late = after(near_middle, wide_queries), after(near_late, first)
    w_out, w_up, w_down = plan.whole(middle, near_middle, 1)
    (w_triple,) = plan.whole(late, near_late, 2)
    summed = cross_call(
        cross_forward_kernel, big, [wide_queries], first, second, mask, plan.block_rows, plan.per_item
    )
    if plan.paired:
        near_last, cotangent = after(near_last, summed), after(cotangent, summed)
    w_self_out, w_self_up, w_self_down = plan.whole(last, near_last, 2)
    upstream = plan.spread(cotangent[:, 0])
    attended_features = narrowed(summed).astype(low_type)
    attended = product(attended_features, w_value).astype(low_type)
    first_sum = latent + product(attended, w_out)
    second_sum, stored_one = feed_forward(first_sum, gains[1], biases[1], w_up, w_down)
    normed_two, scale_two = normalise(second_sum)
    hidden_two = (normed_two * gains[2] + biases[2]).astype(low_type)
    triple = product(hidden_two, w_triple).astype(low_type)
    more = plan.partner_rows(triple[:, model:])
    blended = self_forward(triple, more, plan.groups)
    third_sum = second_sum + product(blended, w_self_out)
    mixed, stored_three = feed_forward(third_sum, gains[3], biases[3], w_self_up, w_self_down)
    mixed = mixed.astype(low_type)

    def unit(grad):
        return grad.astype(low_type).reshape(plan.shards, -1, model)

    if plan.paired:
        upstream = (upstream[0],) + tuple(after(part, third_sum) for part in upstream[1:])
    upstream = jnp.concatenate(upstream, axis=0).astype(jnp.float32)
    low = upstream.astype(low_type)
    upstream, grad_self_up, grad_self_down, gain_three, bias_three = feed_backward(
        upstream, low, third_sum, stored_three, gains[3], w_self_up, w_self_down
    )
    low = upstream.astype(low_type)
    grad_self_out = product_tn(blended, low)
    grad_self_out = product_tn(blended, low)
    one = Group(plan, [unit(grad_self_up), unit(grad_self_down)])
    grad_blended = product_nt(low, w_self_out).astype(low_type)
    grad_blended = after(grad_blended, one.over_core(), mixed)
    triple_grads, more_grads = self_backward(triple, more, grad_blended, plan.groups)
    triple_grads, more_grads = after((triple_grads, more_grads), one.over_fsdp())
    triple_grads = plan.own_pairs(triple_grads, more_grads)
    grad_q, grad_k, grad_v = (
        unit(product_tn(hidden_two, triple_grads[:, i * model : (i + 1) * model])) for i in range(3)
    )
    two, three = Group(plan, [grad_q, grad_k]), Group(plan, [grad_v, unit(grad_self_out)])
    triple_grads = after(triple_grads, two.send, three.send)
    sums_one, arrived_one = over_chips([one])
    grad_hidden = product_nt(triple_grads, w_triple)
    down, gain_two, bias_two = norm_backward(grad_hidden, normed_two, scale_two, gains[2])
    upstream = upstream + down
    low = upstream.astype(low_type)
    grad_down = product_tn(stored_one[2], low)
    low = after(low, two.over_core())
    upstream, grad_up, unused, gain_one, bias_one = feed_backward(
        upstream, low, first_sum, stored_one, gains[1], w_up, w_down
    )
    grad_up, grad_down = unit(grad_up), unit(grad_down)
    low = upstream.astype(low_type)
    low = after(low, grad_up, grad_down, two.over_fsdp(low), three.over_core(low), arrived_one)
    grad_out = product_tn(attended, low)
    four = Group(plan, [grad_up, grad_down, unit(grad_out)])
    grad_attended = product_nt(low, w_out).astype(low_type)
    grad_value = product_tn(attended_features, grad_attended)
    grad_features = product_nt(grad_attended, w_value)
    wide_grads = after(widened(grad_features, 1.0), four.send)
    score_sums = cross_call(
        cross_backward_kernel,
        big,
        [wide_queries, wide_grads],
        first,
        second,
        mask,
        plan.block_rows,
        plan.per_item,
    )
    score_sums = after(score_sums, three.over_fsdp(score_sums), four.over_core(score_sums))
    key_sums = (narrowed(score_sums) * scaling).astype(low_type)
    grad_queries = product(key_sums, w_key).astype(low_type)
    grad_key = product_tn(key_sums, queries)
    pixel_gain_term = jnp.sum(
        query_features * score_sums[:, :features] * scaling + grad_features * summed[:, :features], axis=0
    )
    pixel_bias_term = jnp.sum(
        query_features * score_sums[:, features : features + 1] * scaling
        + grad_features * summed[:, features : features + 1],
        axis=0,
    )
    grad_query = product_tn(hidden, grad_queries)
    down, gain_zero, bias_zero = norm_backward(product_nt(grad_queries, w_query), normed, scale, gains[0])
    latents_grad = (upstream + down).astype(low_type)

    shards = plan.shards
    width = 2 * model // shards
    if shards == 2:
        rows_of_pair = jnp.stack([grad_key, grad_value]).astype(low_type)
    else:
        rows_of_pair = jnp.concatenate([grad_key, grad_value], axis=1).astype(low_type)
        rows_of_pair = rows_of_pair.reshape(features, shards, width).transpose(1, 0, 2)
    norm_terms = jnp.stack(
        [gain_zero, gain_one, gain_two, gain_three, bias_zero, bias_one, bias_two, bias_three]
    )
    pixel_terms = jnp.pad(jnp.stack([pixel_gain_term, pixel_bias_term]), ((0, 0), (0, 512 - features)))
    pixel_rows = pixel_terms.reshape(1, -1, width)
    small = jnp.concatenate(
        [
            norm_terms.reshape(8, shards, model // shards).transpose(1, 0, 2).reshape(shards, 4, width),
            jnp.broadcast_to(pixel_rows, (shards,) + pixel_rows.shape[1:]),
        ],
        axis=1,
    )
    tall = jnp.pad(rows_of_pair, ((0, 0), (0, 384 - features), (0, 0)))
    tall = lax.dynamic_update_slice(tall, small.astype(low_type), (0, 264, 0))
    grad_query = unit(grad_query)
    sums_two, arrived_two = over_chips([two, three], grad_query)
    five = Group(plan, [grad_query, tall.reshape(shards, -1, model)])
    five.send = after(five.send, four.over_fsdp(grad_query), arrived_two)
    early_sums = from_all([sums_one, sums_two])
    sums_four, unused = over_chips([four])
    five.over_core()
    arrived = five.over_fsdp()
    mixed = plan.send_back(after(mixed, arrived))
    latents_grad = plan.send_back(after(latents_grad, arrived))
    sums_five, unused = over_chips([five])
    late_sums = from_all([sums_four, sums_five])
    size = one.sizes[0]
    grad_self_up, grad_self_down = gathered(early_sums, one.sizes)
    grad_triple = side_by_side_rows(early_sums, 2, size, 3)
    (grad_self_out,) = gathered(early_sums[:, 5 * size :], [size])
    latents_grad = plan.placed(latents_grad).astype(jnp.float32)
    grad_up, grad_down, grad_out, grad_query, tall = gathered(late_sums, four.sizes + five.sizes)
    tall = tall.reshape(384, width)
    norm_part = tall[264:268].reshape(8, model // shards)
    pixel_part = tall[268 : 268 + pixel_rows.shape[1]].reshape(2, 512)
    return (
        plan.placed(mixed)[:, None],
        latents_grad[:, None],
        norm_part[:4],
        norm_part[4:],
        pixel_part[0, :features],
        pixel_part[1, :features],
        grad_query,
        tall[:features],
        grad_out,
        grad_up,
        grad_down,
        grad_triple,
        grad_self_out,
        grad_self_up,
        grad_self_down,
    )


def solution(mesh):
    placed = (
        P(None, "blk", "fsdp", None),
        P(None, "blk", None),
        P(None, "blk"),
        P(),
        P(),
        P(None, "fsdp"),
        P(None, "fsdp"),
        P(),
        P(),
        P("fsdp", None),
        P(None, "fsdp"),
        P("fsdp", None),
        P("fsdp", None),
        P("fsdp", None),
        P("fsdp", None),
        P("fsdp", None),
        P("fsdp", None),
        P("fsdp", None),
        P(None, "blk", "fsdp", None),
    )
    return jax.shard_map(
        on_device,
        mesh=mesh,
        in_specs=placed,
        out_specs=(
            P(None, "blk", "fsdp", None),
            P(None, "blk", "fsdp", None),
            P(None, "fsdp"),
            P(None, "fsdp"),
            P(),
            P(),
            P("fsdp", None),
            P(None, "fsdp"),
            P("fsdp", None),
            P("fsdp", None),
            P("fsdp", None),
            P("fsdp", None),
            P("fsdp", None),
            P("fsdp", None),
            P("fsdp", None),
        ),
        check_vma=False,
    )
```

```python
import functools

import jax
import jax.numpy as jnp
from jax import lax
from jax.experimental import pallas as pl
from jax.experimental.pallas import tpu as pltpu
from jax.sharding import PartitionSpec as P

HEADS = 8
FEATURE_ROWS = 272
VMEM_LIMIT = 56 * 1024 * 1024

epsilon = 1e-05
masked_score = -1e30
low_type = jnp.bfloat16


def product(a, b):
    return jnp.dot(a, b, preferred_element_type=jnp.float32)


def product_tn(a, b):
    return lax.dot_general(a, b, (((0,), (0,)), ((), ())), preferred_element_type=jnp.float32)


def product_nt(a, b):
    return lax.dot_general(a, b, (((1,), (1,)), ((), ())), preferred_element_type=jnp.float32)


def normalise(rows):
    centre = rows - jnp.mean(rows, axis=-1, keepdims=True)
    scale = lax.rsqrt(jnp.mean(centre * centre, axis=-1, keepdims=True) + epsilon)
    return centre * scale, scale


def norm_backward(upstream, normed, scale, gain):
    gain_term = jnp.sum(upstream * normed, axis=0)
    bias_term = jnp.sum(upstream, axis=0)
    inner = upstream * gain
    down = scale * (
        inner
        - jnp.mean(inner, axis=-1, keepdims=True)
        - normed * jnp.mean(inner * normed, axis=-1, keepdims=True)
    )
    return down, gain_term, bias_term


def feed_forward(rows, gain, bias, w_up, w_down):
    normed, scale = normalise(rows)
    hidden = (normed * gain + bias).astype(low_type)
    upward = product(hidden, w_up)
    share = 0.5 * (1.0 + lax.erf(upward * (0.5**0.5)))
    slope = share + upward * jnp.exp(-0.5 * upward * upward) * 0.3989422804014327
    active = (upward * share).astype(low_type)
    return rows + product(active, w_down), (hidden, slope, active)


def feed_backward(upstream, low, rows, stored, gain, w_up, w_down):
    hidden, slope, active = stored
    grad_down = product_tn(active, low)
    grad_upward = (product_nt(low, w_down) * slope).astype(low_type)
    grad_up = product_tn(hidden, grad_upward)
    normed, scale = normalise(rows)
    down, gain_term, bias_term = norm_backward(product_nt(grad_upward, w_up), normed, scale, gain)
    return upstream + down, grad_up, grad_down, gain_term, bias_term


def nt(a, b):
    return lax.dot_general(a, b, (((1,), (1,)), ((), ())), preferred_element_type=jnp.float32)


def tn(a, b):
    return lax.dot_general(a, b, (((0,), (0,)), ((), ())), preferred_element_type=jnp.float32)


def params(*semantics):
    return pltpu.CompilerParams(dimension_semantics=semantics, vmem_limit_bytes=VMEM_LIMIT)


def pixel_kernel(micro_ref, pixel_ref, out_ref):
    features = pixel_ref.shape[1]
    width = out_ref.shape[3]
    pixels = pixel_ref[0].astype(jnp.float32)
    centre = pixels - jnp.mean(pixels, axis=0, keepdims=True)
    spread = jnp.mean(centre * centre, axis=0, keepdims=True)
    normed = centre * lax.rsqrt(spread + epsilon)
    pad = jnp.zeros((FEATURE_ROWS - features, normed.shape[1]), jnp.float32)
    tall = jnp.concatenate([normed, pad], axis=0)
    row = lax.broadcasted_iota(jnp.int32, (FEATURE_ROWS, width), 0)
    for part in range(out_ref.shape[0]):
        piece = tall[:, part * width : (part + 1) * width]
        out_ref[part, 0] = jnp.where(row == features, 1.0, piece).astype(low_type)


def prepare_pixels(pixels, micro, width):
    routed = micro.shape[0]
    features, slots = pixels.shape[1:]
    step = min(slots, 1024)
    return pl.pallas_call(
        pixel_kernel,
        out_shape=jax.ShapeDtypeStruct((slots // width, routed, FEATURE_ROWS, width), low_type),
        grid_spec=pltpu.PrefetchScalarGridSpec(
            num_scalar_prefetch=1,
            grid=(routed, slots // step),
            in_specs=[pl.BlockSpec((1, features, step), lambda i, s, m: (m[i], 0, s))],
            out_specs=pl.BlockSpec((step // width, 1, FEATURE_ROWS, width), lambda i, s, m: (s, i, 0, 0)),
        ),
        compiler_params=params("arbitrary", "arbitrary"),
        name="prepare_pixels",
    )(micro, pixels)


def side_by_side(ref):
    return jnp.concatenate([ref[tile, 0] for tile in range(ref.shape[0])], axis=1)


def cross_forward_kernel(items, big_ref, query_ref, first_ref, second_ref, mask_ref, out_ref):
    item = pl.program_id(0) // items
    lanes = mask_ref.shape[2] // 2

    def attend(features, mask):
        scores = product(query_ref[...], features) + mask
        top = jnp.max(scores, axis=-1, keepdims=True)
        weights = jnp.exp(scores - top)
        total = jnp.sum(weights, axis=-1, keepdims=True)
        out_ref[...] = nt(weights.astype(low_type), features) / total

    @pl.when(big_ref[item] == 0)
    def small():
        attend(side_by_side(first_ref), mask_ref[0][:1, :lanes])

    @pl.when(big_ref[item] != 0)
    def large():
        both = jnp.concatenate([side_by_side(first_ref), side_by_side(second_ref)], axis=1)
        attend(both, mask_ref[0][:1])


def cross_backward_kernel(items, big_ref, query_ref, grad_ref, first_ref, second_ref, mask_ref, out_ref):
    item = pl.program_id(0) // items
    lanes = mask_ref.shape[2] // 2

    def attend(features, mask):
        scores = product(query_ref[...], features) + mask
        top = jnp.max(scores, axis=-1, keepdims=True)
        weights = jnp.exp(scores - top)
        shares = weights / jnp.sum(weights, axis=-1, keepdims=True)
        grad_shares = product(grad_ref[...], features)
        inner = jnp.sum(shares * grad_shares, axis=-1, keepdims=True)
        grad_scores = (shares * (grad_shares - inner)).astype(low_type)
        out_ref[...] = nt(grad_scores, features)

    @pl.when(big_ref[item] == 0)
    def small():
        attend(side_by_side(first_ref), mask_ref[0][:1, :lanes])

    @pl.when(big_ref[item] != 0)
    def large():
        both = jnp.concatenate([side_by_side(first_ref), side_by_side(second_ref)], axis=1)
        attend(both, mask_ref[0][:1])


def cross_call(kernel, big, rows, first, second, mask, block, per_item):
    count = rows[0].shape[0]
    tiles, width = first.shape[0], first.shape[3]
    row_spec = pl.BlockSpec((block, FEATURE_ROWS), lambda i, big: (i, 0))
    tile_spec = pl.BlockSpec((tiles, 1, FEATURE_ROWS, width), lambda i, big: (0, i // per_item, 0, 0))
    return pl.pallas_call(
        functools.partial(kernel, per_item),
        out_shape=jax.ShapeDtypeStruct((count, FEATURE_ROWS), jnp.float32),
        grid_spec=pltpu.PrefetchScalarGridSpec(
            num_scalar_prefetch=1,
            grid=(count // block,),
            in_specs=[row_spec] * len(rows)
            + [tile_spec, tile_spec]
            + [pl.BlockSpec((1, 8, mask.shape[2]), lambda i, big: (i // per_item, 0, 0))],
            out_specs=row_spec,
        ),
        compiler_params=params("arbitrary"),
        name="cross_attention",
    )(big, *rows, first, second, mask)


def self_forward_kernel(groups, scaling, q_ref, k_ref, v_ref, more_k_ref, more_v_ref, out_ref):
    for q_rows, own, more in groups:
        keys, values = keys_of(own, more, k_ref, v_ref, more_k_ref, more_v_ref)
        scores = nt(q_ref[q_rows], keys) * scaling
        weights = jnp.exp(scores - jnp.max(scores, axis=-1, keepdims=True))
        total = jnp.sum(weights, axis=-1, keepdims=True)
        out_ref[q_rows, :] = (product(weights.astype(low_type), values) / total).astype(low_type)


def keys_of(own, more, k_ref, v_ref, more_k_ref, more_v_ref):
    keys, values = [], []
    if own is not None:
        keys.append(k_ref[own])
        values.append(v_ref[own])
    if more is not None:
        keys.append(more_k_ref[more])
        values.append(more_v_ref[more])
    if len(keys) == 1:
        return keys[0], values[0]
    return jnp.concatenate(keys, axis=0), jnp.concatenate(values, axis=0)


def self_backward_kernel(
    groups,
    scaling,
    q_ref,
    k_ref,
    v_ref,
    more_k_ref,
    more_v_ref,
    grad_ref,
    wide_ref,
    more_ref,
):
    head = q_ref.shape[1]
    model = wide_ref.shape[1] // 3
    column = pl.multiple_of(pl.program_id(0) * head, head)
    at_q, at_k, at_v = (pl.ds(pl.multiple_of(part * model + column, head), head) for part in range(3))
    for q_rows, own, more in groups:
        keys, values = keys_of(own, more, k_ref, v_ref, more_k_ref, more_v_ref)
        queries = q_ref[q_rows]
        grads = grad_ref[q_rows]
        scores = nt(keys, queries) * scaling
        weights = jnp.exp(scores - jnp.max(scores, axis=0, keepdims=True))
        shares = weights / jnp.sum(weights, axis=0, keepdims=True)
        grad_shares = nt(values, grads)
        inner = jnp.sum(shares * grad_shares, axis=0, keepdims=True)
        grad_scores = (shares * (grad_shares - inner)).astype(low_type)
        wide_ref[q_rows, at_q] = (tn(grad_scores, keys) * scaling).astype(low_type)
        dk = (product(grad_scores, queries) * scaling).astype(low_type)
        dv = product(shares.astype(low_type), grads).astype(low_type)
        split = 0
        if own is not None:
            split = own.stop - own.start
            wide_ref[own, at_k] = dk[:split]
            wide_ref[own, at_v] = dv[:split]
        if more is not None:
            more_ref[more, at_q] = dk[split:]
            more_ref[more, at_k] = dv[split:]


def self_specs(triple, more, heads):
    rows, width = triple.shape[0], triple.shape[1] // 3 // heads
    extra = more.shape[0]
    return [
        pl.BlockSpec((rows, width), lambda h: (0, h)),
        pl.BlockSpec((rows, width), lambda h: (0, heads + h)),
        pl.BlockSpec((rows, width), lambda h: (0, 2 * heads + h)),
        pl.BlockSpec((extra, width), lambda h: (0, h)),
        pl.BlockSpec((extra, width), lambda h: (0, heads + h)),
    ]


def self_forward(triple, more, groups):
    rows, model = triple.shape[0], triple.shape[1] // 3
    head = model // HEADS
    return pl.pallas_call(
        functools.partial(self_forward_kernel, groups, head**-0.5),
        out_shape=jax.ShapeDtypeStruct((rows, model), low_type),
        grid=(HEADS,),
        in_specs=self_specs(triple, more, HEADS),
        out_specs=pl.BlockSpec((rows, head), lambda h: (0, h)),
        compiler_params=params("arbitrary"),
        name="self_forward",
    )(triple, triple, triple, more, more)


def self_backward(triple, more, grads, groups):
    rows, model = triple.shape[0], triple.shape[1] // 3
    head = model // HEADS
    extra = more.shape[0]
    return pl.pallas_call(
        functools.partial(self_backward_kernel, groups, head**-0.5),
        out_shape=[
            jax.ShapeDtypeStruct((rows, 3 * model), low_type),
            jax.ShapeDtypeStruct((extra, 2 * model), low_type),
        ],
        grid=(HEADS,),
        in_specs=self_specs(triple, more, HEADS) + [pl.BlockSpec((rows, head), lambda h: (0, h))],
        out_specs=[
            pl.BlockSpec((rows, 3 * model), lambda h: (0, 0)),
            pl.BlockSpec((extra, 2 * model), lambda h: (0, 0)),
        ],
        compiler_params=params("arbitrary"),
        name="self_backward",
    )(triple, triple, triple, more, more, grads)


def widen_kernel(in_ref, out_ref):
    out_ref[...] = in_ref[...].astype(jnp.float32).reshape(out_ref.shape)


def side_by_side_rows(array, first, size, count):
    blocks, unused, width = array.shape
    rows = blocks * size
    if size % 16:
        parts = [array[:, (first + i) * size : (first + i + 1) * size] for i in range(count)]
        return jnp.concatenate([part.reshape(rows, width) for part in parts], axis=1).astype(jnp.float32)
    return pl.pallas_call(
        widen_kernel,
        out_shape=jax.ShapeDtypeStruct((rows, count * width), jnp.float32),
        grid=(count,),
        in_specs=[pl.BlockSpec((blocks, size, width), lambda i: (0, first + i, 0))],
        out_specs=pl.BlockSpec((rows, width), lambda i: (0, i)),
        compiler_params=params("arbitrary"),
        name="widen",
    )(array)


def ordered(bit, own, other, axis=0):
    first = jnp.where(bit == 0, own, other)
    last = jnp.where(bit == 0, other, own)
    return jnp.concatenate([first, last], axis=axis)


def half_of(array, bit, axis):
    size = array.shape[axis] // 2
    return lax.dynamic_slice_in_dim(array, bit * size, size, axis)


def swap(array, axis_name, mask):
    size = lax.axis_size(axis_name)
    return lax.ppermute(array, axis_name, [(i, i ^ mask) for i in range(size)])


class Plan:
    def __init__(self, micro_count, rows):
        self.blocks = lax.axis_size("blk")
        self.shards = lax.axis_size("fsdp")
        self.b = lax.axis_index("blk")
        self.x = lax.axis_index("fsdp")
        self.core = self.b & 1
        self.side = (self.b >> 1) & 1
        self.rows = rows
        self.micro_count = micro_count
        self.paired = self.shards == 2 and self.blocks % 4 == 0 and micro_count == 3
        if self.paired:
            self.micro = jnp.stack([self.x, jnp.int32(2)]).astype(jnp.int32)
            self.block_rows = rows
            self.per_item = 2
            self.groups = (
                (slice(0, 2 * rows), slice(0, 2 * rows), None),
                (slice(2 * rows, 3 * rows), slice(2 * rows, 3 * rows), slice(0, rows)),
            )
        else:
            self.micro = jnp.arange(micro_count, dtype=jnp.int32)
            self.block_rows = rows
            self.per_item = 1
            whole = rows * self.shards
            self.groups = tuple(
                (slice(i * rows, (i + 1) * rows), None, slice(i * whole, (i + 1) * whole))
                for i in range(micro_count)
            )

    def block_of(self, item, device):
        if self.paired and item == 1:
            return (device | 1) - 1 + self.x
        return device

    def turn(self, array):
        places = []
        for x in range(2):
            for b in range(self.blocks):
                core = b % 2
                places.append((b * 2 + x, (b - core + x) * 2 + core))
        return lax.ppermute(array, ("blk", "fsdp"), places)

    def spread(self, array):
        if not self.paired:
            return (array.reshape(-1, array.shape[-1]),)
        own = lax.dynamic_index_in_dim(array, self.x, 0, False)
        away = swap(lax.dynamic_index_in_dim(array, 1 - self.x, 0, False), "fsdp", 1)
        return own, away, self.turn(array[2])

    def send_back(self, array):
        if not self.paired:
            return (array,)
        own, away, shared = (array[i * self.rows : (i + 1) * self.rows] for i in range(3))
        return own, swap(away, "fsdp", 1), self.turn(shared)

    def placed(self, parts):
        if not self.paired:
            return parts[0].reshape(self.micro_count, self.rows, -1)
        own, other, shared = parts
        return jnp.stack([jnp.where(self.x == 0, own, other), jnp.where(self.x == 0, other, own), shared])

    def columns(self, pair, norms):
        if not self.paired:
            return (
                lax.all_gather(pair, "fsdp", axis=1, tiled=True),
                lax.all_gather(norms, "fsdp", axis=1, tiled=True),
            )
        flat = norms.reshape(-1, pair.shape[1])
        return (swap(jnp.concatenate([pair, flat], axis=0), "fsdp", 1),)

    def joined(self, pair, norms, other):
        if not self.paired:
            return other
        rows = pair.shape[0]
        return (
            ordered(self.x, pair, other[0][:rows], 1),
            ordered(self.x, norms, other[0][rows:].reshape(norms.shape), 1),
        )

    def fetch(self, weights, chips):
        if not self.paired:
            return None
        part = self.core if chips == 1 else 2 * self.core + self.side
        size = weights[0].shape[0] // (2 * chips)
        parts = [lax.dynamic_slice_in_dim(weight, part * size, size, 0) for weight in weights]
        return jnp.concatenate(parts, axis=1)

    def whole(self, weights, near, chips):
        if not self.paired:
            return [lax.all_gather(weight, "fsdp", axis=0, tiled=True) for weight in weights]
        if chips == 2:
            near = ordered(self.side, near, swap(near, "blk", 2))
        away = ordered(self.core, near, swap(near, "blk", 1))
        results, at = [], 0
        for weight in weights:
            results.append(ordered(self.x, weight, away[:, at : at + weight.shape[1]]))
            at += weight.shape[1]
        return results

    def partner_rows(self, pairs):
        if self.paired:
            return swap(pairs[2 * self.rows :], "blk", 1)
        wide = pairs.reshape(self.micro_count, self.rows, -1)
        return lax.all_gather(wide, "fsdp", axis=1, tiled=True).reshape(-1, wide.shape[-1])

    def own_pairs(self, wide, more):
        model = wide.shape[1] // 3
        if self.paired:
            back = swap(more, "blk", 1).astype(jnp.float32)
            first = 2 * self.rows
            last = (wide[first:, model:].astype(jnp.float32) + back).astype(low_type)
            return lax.dynamic_update_slice(wide, last, (first, model))
        split = more.reshape(self.micro_count, self.rows * self.shards, -1)
        back = lax.psum_scatter(split, "fsdp", scatter_dimension=1, tiled=True)
        return lax.dynamic_update_slice(wide, back.reshape(-1, back.shape[-1]), (0, model))


def added(kept, received):
    return (kept.astype(jnp.float32) + received.astype(jnp.float32)).astype(low_type)


def after(value, *others):
    if not others:
        return value
    return lax.optimization_barrier((value,) + others)[0]


class Group:
    def __init__(self, plan, units):
        self.plan = plan
        count, core = plan.blocks // 2, plan.core
        pieces = [unit.reshape(plan.shards, count, 2, -1, unit.shape[2]) for unit in units]
        self.sizes = [piece.shape[3] for piece in pieces]
        self.send = jnp.concatenate(
            [lax.dynamic_index_in_dim(piece, 1 - core, 2, False) for piece in pieces], axis=2
        )
        self.kept = jnp.concatenate([lax.dynamic_index_in_dim(piece, core, 2, False) for piece in pieces], axis=2)

    def over_core(self, *earlier):
        received = after(swap(self.send, "blk", 1), *earlier)
        mask = self.plan.shards // 2
        while mask:
            bit = jnp.where((self.plan.x & mask) > 0, 1, 0)
            self.send = added(half_of(self.kept, 1 - bit, 0), half_of(received, 1 - bit, 0))
            self.kept = added(half_of(self.kept, bit, 0), half_of(received, bit, 0))
            if mask > 1:
                received = swap(self.send, "fsdp", mask)
            mask //= 2
        return self.send

    def over_fsdp(self, *earlier):
        received = after(swap(self.send, "fsdp", 1), *earlier)
        self.total = added(self.kept, received)[0]
        return received


def over_chips(groups, *earlier):
    plan = groups[0].plan
    total = jnp.concatenate([group.total for group in groups], axis=1)
    same_core = [list(range(core, plan.blocks, 2)) for core in range(2)]
    arrived = lax.all_to_all(
        total, "blk", split_axis=0, concat_axis=0, axis_index_groups=same_core, tiled=True
    )
    arrived = after(arrived, *earlier)
    return jnp.sum(arrived.astype(jnp.float32), axis=0).astype(low_type), arrived


def from_all(sums):
    return lax.all_gather(jnp.concatenate(sums, axis=0), "blk", axis=0)


def gathered(array, sizes):
    results, at = [], 0
    for size in sizes:
        part = array[:, at : at + size].astype(jnp.float32)
        results.append(part.reshape(-1, part.shape[2]))
        at += size
    return results


def route_pixels(plan, pixels, segment_ids, pad_ids, block_map, fetch):
    blocks, labels = plan.blocks, block_map.shape[1]
    slots, features = pixels.shape[1:]
    width = slots // blocks
    routed = plan.micro.shape[0]
    label_ids = jnp.arange(labels, dtype=jnp.int32)

    def of_items(array):
        return jnp.stack([lax.dynamic_index_in_dim(array, plan.micro[i], 0, False) for i in range(routed)])

    picked = of_items(segment_ids)
    counts = jnp.sum((picked[:, None, :] == label_ids[None, :, None]).astype(jnp.float32), axis=2)
    chunks = prepare_pixels(jnp.swapaxes(pixels, 1, 2), plan.micro, width)
    spread = lax.all_to_all(chunks, "blk", split_axis=0, concat_axis=0, tiled=True)
    totals = jnp.sum(lax.all_gather(counts, "blk", axis=0), axis=0).astype(jnp.int32)
    owners = of_items(block_map)
    images = label_ids[None, :] != of_items(pad_ids)[:, None]
    totals = jnp.where(images, totals, 0)
    earlier = label_ids[None, :] < label_ids[:, None]
    starts = jnp.sum(jnp.where(earlier[None], totals[:, None, :], 0), axis=2)
    devices = jnp.arange(blocks, dtype=jnp.int32)

    def extents(wanted):
        hit = (owners[:, None, :] == wanted[:, :, None]) & images[:, None, :]
        start = jnp.sum(jnp.where(hit, starts[:, None, :], 0), axis=2)
        return start, start + jnp.sum(jnp.where(hit, totals[:, None, :], 0), axis=2)

    def chunk_at(start, place):
        first = start // width
        return first + ((place - first) & (blocks - 1))

    def source_of(chunk):
        return jnp.clip(chunk // blocks, 0, blocks - 1)

    item = jnp.arange(routed, dtype=jnp.int32)
    wanted = jnp.stack([plan.block_of(i, devices) for i in range(routed)])
    start, finish = extents(wanted)
    flat = spread.reshape(blocks * routed, FEATURE_ROWS, width)
    piece_at = source_of(chunk_at(start, plan.b)) * routed + item[:, None]
    pieces = jnp.take(flat, piece_at.T.reshape(-1), axis=0, mode="clip")
    pieces = pieces.reshape(blocks, routed, FEATURE_ROWS, width)
    fetched, sent = fetch(chunks, pieces)
    if sent is not None:
        pieces = after(pieces, sent)
    first = lax.all_to_all(pieces, "blk", split_axis=0, concat_axis=0, tiled=True)
    largest = jnp.argmax(totals, axis=1)
    largest_start = jnp.sum(jnp.where(label_ids[None, :] == largest[:, None], starts, 0), axis=1)
    second_at = source_of(chunk_at(largest_start, plan.b) + blocks) * routed + item
    second = lax.all_gather(jnp.take(flat, second_at, axis=0, mode="clip"), "blk", axis=0, tiled=False)
    mine = jnp.stack([plan.block_of(i, plan.b) for i in range(routed)])[:, None]
    start, finish = extents(mine)
    slot = (width * chunk_at(start, devices[None, :]))[:, :, None] + jnp.arange(width, dtype=jnp.int32)
    slot = slot.reshape(routed, -1)
    slot = jnp.concatenate([slot, slot + width * blocks], axis=1)
    mask = jnp.where((slot >= start) & (slot < finish), 0.0, masked_score)
    mask = jnp.broadcast_to(mask[:, None, :], (routed, 8, mask.shape[1]))
    big = ((finish - 1) // width - start // width >= blocks).astype(jnp.int32)[:, 0]
    if width < 128:
        join = 128 // width

        def merged(array):
            parts = array.reshape(blocks // join, join, routed, FEATURE_ROWS, width)
            return parts.transpose(0, 2, 3, 1, 4).reshape(blocks // join, routed, FEATURE_ROWS, 128)

        first, second = merged(first), merged(second)
    return fetched, first, second, mask, big


def on_device(
    latents,
    pixels,
    segment_ids,
    pad_ids,
    block_map,
    norm_gains,
    norm_biases,
    pixel_gain,
    pixel_bias,
    cross_query,
    cross_kv,
    cross_out,
    cross_up,
    cross_down,
    self_qkv,
    self_out,
    self_up,
    self_down,
    cotangent,
):
    micro_count, unused, rows, model = latents.shape
    features = pixels.shape[2]
    plan = Plan(micro_count, rows)
    scaling = model**-0.5

    norm_rows = jnp.concatenate([norm_gains, norm_biases], axis=0)
    early, middle = [cross_query], [cross_out, cross_up, cross_down]
    late, last = [self_qkv], [self_out, self_up, self_down]

    def fetch(chunks, pieces):
        if not plan.paired:
            return (plan.spread(latents[:, 0]), plan.columns(cross_kv, norm_rows)) + (None,) * 4, None
        latent = plan.spread(after(latents, chunks)[:, 0])
        near_early = swap(plan.fetch([after(cross_query, chunks)], 1), "fsdp", 1)
        other = plan.columns(after(cross_kv, chunks), norm_rows)
        send = plan.fetch([after(middle[0], near_early, *latent[1:], *other)] + middle[1:], 1)
        near_middle = swap(send, "fsdp", 1)
        near_late = swap(plan.fetch([after(late[0], send, pieces)], 2), "fsdp", 1)
        near_last = swap(plan.fetch([after(last[0], send, pieces)] + last[1:], 2), "fsdp", 1)
        latent = (latent[0],) + tuple(after(part, pieces) for part in latent[1:])
        near_early, other = after(near_early, pieces), (after(other[0], pieces),)
        return (latent, other, near_early, near_middle, near_late, near_last), send

    fetched, first, second, mask, big = route_pixels(plan, pixels, segment_ids, pad_ids, block_map, fetch)
    latent, other, near_early, near_middle, near_late, near_last = fetched
    latent = jnp.concatenate(latent, axis=0).astype(jnp.float32)
    w_pair, norms = plan.joined(cross_kv, norm_rows, other)
    norms = norms.astype(jnp.float32)
    gains, biases = norms[:4], norms[4:]
    w_key, w_value = w_pair[:, :model], w_pair[:, model:]
    (w_query,) = plan.whole(early, near_early, 1)
    pixel_scaler = pixel_gain.astype(jnp.float32)
    pixel_offset = pixel_bias.astype(jnp.float32)

    def widened(rows_f32, scale):
        against = jnp.sum(rows_f32 * pixel_offset, axis=-1, keepdims=True)
        wide = jnp.concatenate([rows_f32 * pixel_scaler, against], axis=1) * scale
        return jnp.pad(wide, ((0, 0), (0, FEATURE_ROWS - features - 1))).astype(low_type)

    def narrowed(wide):
        return wide[:, :features] * pixel_scaler + wide[:, features : features + 1] * pixel_offset

    normed, scale = normalise(latent)
    hidden = (normed * gains[0] + biases[0]).astype(low_type)
    queries = product(hidden, w_query).astype(low_type)
    query_features = product_nt(queries, w_key)
    wide_queries = widened(query_features, scaling)
    if plan.paired:
        near_middle, near_late = after(near_middle, wide_queries), after(near_late, first)
    w_out, w_up, w_down = plan.whole(middle, near_middle, 1)
    (w_triple,) = plan.whole(late, near_late, 2)
    summed = cross_call(
        cross_forward_kernel, big, [wide_queries], first, second, mask, plan.block_rows, plan.per_item
    )
    if plan.paired:
        near_last, cotangent = after(near_last, summed), after(cotangent, summed)
    w_self_out, w_self_up, w_self_down = plan.whole(last, near_last, 2)
    upstream = plan.spread(cotangent[:, 0])
    attended_features = narrowed(summed).astype(low_type)
    attended = product(attended_features, w_value).astype(low_type)
    first_sum = latent + product(attended, w_out)
    second_sum, stored_one = feed_forward(first_sum, gains[1], biases[1], w_up, w_down)
    normed_two, scale_two = normalise(second_sum)
    hidden_two = (normed_two * gains[2] + biases[2]).astype(low_type)
    triple = product(hidden_two, w_triple).astype(low_type)
    more = plan.partner_rows(triple[:, model:])
    blended = self_forward(triple, more, plan.groups)
    third_sum = second_sum + product(blended, w_self_out)
    mixed, stored_three = feed_forward(third_sum, gains[3], biases[3], w_self_up, w_self_down)
    mixed = mixed.astype(low_type)

    def unit(grad):
        return grad.astype(low_type).reshape(plan.shards, -1, model)

    if plan.paired:
        upstream = (upstream[0],) + tuple(after(part, third_sum) for part in upstream[1:])
    upstream = jnp.concatenate(upstream, axis=0).astype(jnp.float32)
    low = upstream.astype(low_type)
    upstream, grad_self_up, grad_self_down, gain_three, bias_three = feed_backward(
        upstream, low, third_sum, stored_three, gains[3], w_self_up, w_self_down
    )
    low = upstream.astype(low_type)
    grad_self_out = product_tn(blended, low)
    grad_self_out = product_tn(blended, low)
    one = Group(plan, [unit(grad_self_up), unit(grad_self_down)])
    grad_blended = product_nt(low, w_self_out).astype(low_type)
    grad_blended = after(grad_blended, one.over_core(), mixed)
    triple_grads, more_grads = self_backward(triple, more, grad_blended, plan.groups)
    triple_grads, more_grads = after((triple_grads, more_grads), one.over_fsdp())
    triple_grads = plan.own_pairs(triple_grads, more_grads)
    grad_q, grad_k, grad_v = (
        unit(product_tn(hidden_two, triple_grads[:, i * model : (i + 1) * model])) for i in range(3)
    )
    two, three = Group(plan, [grad_q, grad_k]), Group(plan, [grad_v, unit(grad_self_out)])
    triple_grads = after(triple_grads, two.send, three.send)
    sums_one, arrived_one = over_chips([one])
    grad_hidden = product_nt(triple_grads, w_triple)
    down, gain_two, bias_two = norm_backward(grad_hidden, normed_two, scale_two, gains[2])
    upstream = upstream + down
    low = upstream.astype(low_type)
    grad_down = product_tn(stored_one[2], low)
    low = after(low, two.over_core())
    upstream, grad_up, unused, gain_one, bias_one = feed_backward(
        upstream, low, first_sum, stored_one, gains[1], w_up, w_down
    )
    grad_up, grad_down = unit(grad_up), unit(grad_down)
    low = upstream.astype(low_type)
    low = after(low, grad_up, grad_down, two.over_fsdp(low), three.over_core(low), arrived_one)
    grad_out = product_tn(attended, low)
    four = Group(plan, [grad_up, grad_down, unit(grad_out)])
    grad_attended = product_nt(low, w_out).astype(low_type)
    grad_value = product_tn(attended_features, grad_attended)
    grad_features = product_nt(grad_attended, w_value)
    wide_grads = after(widened(grad_features, 1.0), four.send)
    score_sums = cross_call(
        cross_backward_kernel,
        big,
        [wide_queries, wide_grads],
        first,
        second,
        mask,
        plan.block_rows,
        plan.per_item,
    )
    score_sums = after(score_sums, three.over_fsdp(score_sums), four.over_core(score_sums))
    key_sums = (narrowed(score_sums) * scaling).astype(low_type)
    grad_queries = product(key_sums, w_key).astype(low_type)
    grad_key = product_tn(key_sums, queries)
    pixel_gain_term = jnp.sum(
        query_features * score_sums[:, :features] * scaling + grad_features * summed[:, :features], axis=0
    )
    pixel_bias_term = jnp.sum(
        query_features * score_sums[:, features : features + 1] * scaling
        + grad_features * summed[:, features : features + 1],
        axis=0,
    )
    grad_query = product_tn(hidden, grad_queries)
    down, gain_zero, bias_zero = norm_backward(product_nt(grad_queries, w_query), normed, scale, gains[0])
    latents_grad = (upstream + down).astype(low_type)

    shards = plan.shards
    width = 2 * model // shards
    if shards == 2:
        rows_of_pair = jnp.stack([grad_key, grad_value]).astype(low_type)
    else:
        rows_of_pair = jnp.concatenate([grad_key, grad_value], axis=1).astype(low_type)
        rows_of_pair = rows_of_pair.reshape(features, shards, width).transpose(1, 0, 2)
    norm_terms = jnp.stack(
        [gain_zero, gain_one, gain_two, gain_three, bias_zero, bias_one, bias_two, bias_three]
    )
    pixel_terms = jnp.pad(jnp.stack([pixel_gain_term, pixel_bias_term]), ((0, 0), (0, 512 - features)))
    pixel_rows = pixel_terms.reshape(1, -1, width)
    small = jnp.concatenate(
        [
            norm_terms.reshape(8, shards, model // shards).transpose(1, 0, 2).reshape(shards, 4, width),
            jnp.broadcast_to(pixel_rows, (shards,) + pixel_rows.shape[1:]),
        ],
        axis=1,
    )
    tall = jnp.pad(rows_of_pair, ((0, 0), (0, 384 - features), (0, 0)))
    tall = lax.dynamic_update_slice(tall, small.astype(low_type), (0, 264, 0))
    grad_query = unit(grad_query)
    five = Group(plan, [grad_query, tall.reshape(shards, -1, model)])
    five.send = after(five.send, four.over_fsdp(grad_query))
    sums_two, arrived_two = over_chips([two, three], five.send)
    early_sums = from_all([sums_one, sums_two])
    sums_four, unused = over_chips([four])
    five.over_core()
    arrived = five.over_fsdp()
    mixed = plan.send_back(after(mixed, arrived))
    latents_grad = plan.send_back(after(latents_grad, arrived))
    sums_five, unused = over_chips([five])
    late_sums = from_all([sums_four, sums_five])
    size = one.sizes[0]
    grad_self_up, grad_self_down = gathered(early_sums, one.sizes)
    grad_triple = side_by_side_rows(early_sums, 2, size, 3)
    (grad_self_out,) = gathered(early_sums[:, 5 * size :], [size])
    latents_grad = plan.placed(latents_grad).astype(jnp.float32)
    grad_up, grad_down, grad_out, grad_query, tall = gathered(late_sums, four.sizes + five.sizes)
    tall = tall.reshape(384, width)
    norm_part = tall[264:268].reshape(8, model // shards)
    pixel_part = tall[268 : 268 + pixel_rows.shape[1]].reshape(2, 512)
    return (
        plan.placed(mixed)[:, None],
        latents_grad[:, None],
        norm_part[:4],
        norm_part[4:],
        pixel_part[0, :features],
        pixel_part[1, :features],
        grad_query,
        tall[:features],
        grad_out,
        grad_up,
        grad_down,
        grad_triple,
        grad_self_out,
        grad_self_up,
        grad_self_down,
    )


def solution(mesh):
    placed = (
        P(None, "blk", "fsdp", None),
        P(None, "blk", None),
        P(None, "blk"),
        P(),
        P(),
        P(None, "fsdp"),
        P(None, "fsdp"),
        P(),
        P(),
        P("fsdp", None),
        P(None, "fsdp"),
        P("fsdp", None),
        P("fsdp", None),
        P("fsdp", None),
        P("fsdp", None),
        P("fsdp", None),
        P("fsdp", None),
        P("fsdp", None),
        P(None, "blk", "fsdp", None),
    )
    return jax.shard_map(
        on_device,
        mesh=mesh,
        in_specs=placed,
        out_specs=(
            P(None, "blk", "fsdp", None),
            P(None, "blk", "fsdp", None),
            P(None, "fsdp"),
            P(None, "fsdp"),
            P(),
            P(),
            P("fsdp", None),
            P(None, "fsdp"),
            P("fsdp", None),
            P("fsdp", None),
            P("fsdp", None),
            P("fsdp", None),
            P("fsdp", None),
            P("fsdp", None),
            P("fsdp", None),
        ),
        check_vma=False,
    )
```

```python
import functools

import jax
import jax.numpy as jnp
from jax import lax
from jax.experimental import pallas as pl
from jax.experimental.pallas import tpu as pltpu
from jax.sharding import PartitionSpec as P

HEADS = 8
FEATURE_ROWS = 272
VMEM_LIMIT = 56 * 1024 * 1024

epsilon = 1e-05
masked_score = -1e30
low_type = jnp.bfloat16


def product(a, b):
    return jnp.dot(a, b, preferred_element_type=jnp.float32)


def product_tn(a, b):
    return lax.dot_general(a, b, (((0,), (0,)), ((), ())), preferred_element_type=jnp.float32)


def product_nt(a, b):
    return lax.dot_general(a, b, (((1,), (1,)), ((), ())), preferred_element_type=jnp.float32)


def normalise(rows):
    centre = rows - jnp.mean(rows, axis=-1, keepdims=True)
    scale = lax.rsqrt(jnp.mean(centre * centre, axis=-1, keepdims=True) + epsilon)
    return centre * scale, scale


def norm_backward(upstream, normed, scale, gain):
    gain_term = jnp.sum(upstream * normed, axis=0)
    bias_term = jnp.sum(upstream, axis=0)
    inner = upstream * gain
    down = scale * (
        inner
        - jnp.mean(inner, axis=-1, keepdims=True)
        - normed * jnp.mean(inner * normed, axis=-1, keepdims=True)
    )
    return down, gain_term, bias_term


def feed_forward(rows, gain, bias, w_up, w_down):
    normed, scale = normalise(rows)
    hidden = (normed * gain + bias).astype(low_type)
    upward = product(hidden, w_up)
    share = 0.5 * (1.0 + lax.erf(upward * (0.5**0.5)))
    slope = share + upward * jnp.exp(-0.5 * upward * upward) * 0.3989422804014327
    active = (upward * share).astype(low_type)
    return rows + product(active, w_down), (hidden, slope, active)


def feed_backward(upstream, low, rows, stored, gain, w_up, w_down):
    hidden, slope, active = stored
    grad_down = product_tn(active, low)
    grad_upward = (product_nt(low, w_down) * slope).astype(low_type)
    grad_up = product_tn(hidden, grad_upward)
    normed, scale = normalise(rows)
    down, gain_term, bias_term = norm_backward(product_nt(grad_upward, w_up), normed, scale, gain)
    return upstream + down, grad_up, grad_down, gain_term, bias_term


def nt(a, b):
    return lax.dot_general(a, b, (((1,), (1,)), ((), ())), preferred_element_type=jnp.float32)


def tn(a, b):
    return lax.dot_general(a, b, (((0,), (0,)), ((), ())), preferred_element_type=jnp.float32)


def params(*semantics):
    return pltpu.CompilerParams(dimension_semantics=semantics, vmem_limit_bytes=VMEM_LIMIT)


def pixel_kernel(micro_ref, pixel_ref, out_ref):
    features = pixel_ref.shape[1]
    width = out_ref.shape[3]
    pixels = pixel_ref[0].astype(jnp.float32)
    centre = pixels - jnp.mean(pixels, axis=0, keepdims=True)
    spread = jnp.mean(centre * centre, axis=0, keepdims=True)
    normed = centre * lax.rsqrt(spread + epsilon)
    pad = jnp.zeros((FEATURE_ROWS - features, normed.shape[1]), jnp.float32)
    tall = jnp.concatenate([normed, pad], axis=0)
    row = lax.broadcasted_iota(jnp.int32, (FEATURE_ROWS, width), 0)
    for part in range(out_ref.shape[0]):
        piece = tall[:, part * width : (part + 1) * width]
        out_ref[part, 0] = jnp.where(row == features, 1.0, piece).astype(low_type)


def prepare_pixels(pixels, micro, width):
    routed = micro.shape[0]
    features, slots = pixels.shape[1:]
    step = min(slots, 1024)
    return pl.pallas_call(
        pixel_kernel,
        out_shape=jax.ShapeDtypeStruct((slots // width, routed, FEATURE_ROWS, width), low_type),
        grid_spec=pltpu.PrefetchScalarGridSpec(
            num_scalar_prefetch=1,
            grid=(routed, slots // step),
            in_specs=[pl.BlockSpec((1, features, step), lambda i, s, m: (m[i], 0, s))],
            out_specs=pl.BlockSpec((step // width, 1, FEATURE_ROWS, width), lambda i, s, m: (s, i, 0, 0)),
        ),
        compiler_params=params("arbitrary", "arbitrary"),
        name="prepare_pixels",
    )(micro, pixels)


def side_by_side(ref):
    return jnp.concatenate([ref[tile, 0] for tile in range(ref.shape[0])], axis=1)


def cross_forward_kernel(items, big_ref, query_ref, first_ref, second_ref, mask_ref, out_ref):
    item = pl.program_id(0) // items
    lanes = mask_ref.shape[2] // 2

    def attend(features, mask):
        scores = product(query_ref[...], features) + mask
        top = jnp.max(scores, axis=-1, keepdims=True)
        weights = jnp.exp(scores - top)
        total = jnp.sum(weights, axis=-1, keepdims=True)
        out_ref[...] = nt(weights.astype(low_type), features) / total

    @pl.when(big_ref[item] == 0)
    def small():
        attend(side_by_side(first_ref), mask_ref[0][:1, :lanes])

    @pl.when(big_ref[item] != 0)
    def large():
        both = jnp.concatenate([side_by_side(first_ref), side_by_side(second_ref)], axis=1)
        attend(both, mask_ref[0][:1])


def cross_backward_kernel(items, big_ref, query_ref, grad_ref, first_ref, second_ref, mask_ref, out_ref):
    item = pl.program_id(0) // items
    lanes = mask_ref.shape[2] // 2

    def attend(features, mask):
        scores = product(query_ref[...], features) + mask
        top = jnp.max(scores, axis=-1, keepdims=True)
        weights = jnp.exp(scores - top)
        shares = weights * (1.0 / jnp.sum(weights, axis=-1, keepdims=True))
        grad_shares = product(grad_ref[...], features)
        inner = jnp.sum(shares * grad_shares, axis=-1, keepdims=True)
        grad_scores = (shares * (grad_shares - inner)).astype(low_type)
        out_ref[...] = nt(grad_scores, features)

    @pl.when(big_ref[item] == 0)
    def small():
        attend(side_by_side(first_ref), mask_ref[0][:1, :lanes])

    @pl.when(big_ref[item] != 0)
    def large():
        both = jnp.concatenate([side_by_side(first_ref), side_by_side(second_ref)], axis=1)
        attend(both, mask_ref[0][:1])


def cross_call(kernel, big, rows, first, second, mask, block, per_item):
    count = rows[0].shape[0]
    tiles, width = first.shape[0], first.shape[3]
    row_spec = pl.BlockSpec((block, FEATURE_ROWS), lambda i, big: (i, 0))
    tile_spec = pl.BlockSpec((tiles, 1, FEATURE_ROWS, width), lambda i, big: (0, i // per_item, 0, 0))
    return pl.pallas_call(
        functools.partial(kernel, per_item),
        out_shape=jax.ShapeDtypeStruct((count, FEATURE_ROWS), jnp.float32),
        grid_spec=pltpu.PrefetchScalarGridSpec(
            num_scalar_prefetch=1,
            grid=(count // block,),
            in_specs=[row_spec] * len(rows)
            + [tile_spec, tile_spec]
            + [pl.BlockSpec((1, 8, mask.shape[2]), lambda i, big: (i // per_item, 0, 0))],
            out_specs=row_spec,
        ),
        compiler_params=params("arbitrary"),
        name="cross_attention",
    )(big, *rows, first, second, mask)


def self_forward_kernel(groups, scaling, q_ref, k_ref, v_ref, more_k_ref, more_v_ref, out_ref):
    for q_rows, own, more in groups:
        keys, values = keys_of(own, more, k_ref, v_ref, more_k_ref, more_v_ref)
        scores = nt(q_ref[q_rows], keys) * scaling
        weights = jnp.exp(scores - jnp.max(scores, axis=-1, keepdims=True))
        total = jnp.sum(weights, axis=-1, keepdims=True)
        out_ref[q_rows, :] = (product(weights.astype(low_type), values) / total).astype(low_type)


def keys_of(own, more, k_ref, v_ref, more_k_ref, more_v_ref):
    keys, values = [], []
    if own is not None:
        keys.append(k_ref[own])
        values.append(v_ref[own])
    if more is not None:
        keys.append(more_k_ref[more])
        values.append(more_v_ref[more])
    if len(keys) == 1:
        return keys[0], values[0]
    return jnp.concatenate(keys, axis=0), jnp.concatenate(values, axis=0)


def self_backward_kernel(
    groups,
    scaling,
    q_ref,
    k_ref,
    v_ref,
    more_k_ref,
    more_v_ref,
    grad_ref,
    wide_ref,
    more_ref,
):
    head = q_ref.shape[1]
    model = wide_ref.shape[1] // 3
    column = pl.multiple_of(pl.program_id(0) * head, head)
    at_q, at_k, at_v = (pl.ds(pl.multiple_of(part * model + column, head), head) for part in range(3))
    for q_rows, own, more in groups:
        keys, values = keys_of(own, more, k_ref, v_ref, more_k_ref, more_v_ref)
        queries = q_ref[q_rows]
        grads = grad_ref[q_rows]
        scores = nt(keys, queries) * scaling
        weights = jnp.exp(scores - jnp.max(scores, axis=0, keepdims=True))
        shares = weights * (1.0 / jnp.sum(weights, axis=0, keepdims=True))
        grad_shares = nt(values, grads)
        inner = jnp.sum(shares * grad_shares, axis=0, keepdims=True)
        grad_scores = (shares * (grad_shares - inner)).astype(low_type)
        wide_ref[q_rows, at_q] = (tn(grad_scores, keys) * scaling).astype(low_type)
        dk = (product(grad_scores, queries) * scaling).astype(low_type)
        dv = product(shares.astype(low_type), grads).astype(low_type)
        split = 0
        if own is not None:
            split = own.stop - own.start
            wide_ref[own, at_k] = dk[:split]
            wide_ref[own, at_v] = dv[:split]
        if more is not None:
            more_ref[more, at_q] = dk[split:]
            more_ref[more, at_k] = dv[split:]


def self_specs(triple, more, heads):
    rows, width = triple.shape[0], triple.shape[1] // 3 // heads
    extra = more.shape[0]
    return [
        pl.BlockSpec((rows, width), lambda h: (0, h)),
        pl.BlockSpec((rows, width), lambda h: (0, heads + h)),
        pl.BlockSpec((rows, width), lambda h: (0, 2 * heads + h)),
        pl.BlockSpec((extra, width), lambda h: (0, h)),
        pl.BlockSpec((extra, width), lambda h: (0, heads + h)),
    ]


def self_forward(triple, more, groups):
    rows, model = triple.shape[0], triple.shape[1] // 3
    head = model // HEADS
    return pl.pallas_call(
        functools.partial(self_forward_kernel, groups, head**-0.5),
        out_shape=jax.ShapeDtypeStruct((rows, model), low_type),
        grid=(HEADS,),
        in_specs=self_specs(triple, more, HEADS),
        out_specs=pl.BlockSpec((rows, head), lambda h: (0, h)),
        compiler_params=params("arbitrary"),
        name="self_forward",
    )(triple, triple, triple, more, more)


def self_backward(triple, more, grads, groups):
    rows, model = triple.shape[0], triple.shape[1] // 3
    head = model // HEADS
    extra = more.shape[0]
    return pl.pallas_call(
        functools.partial(self_backward_kernel, groups, head**-0.5),
        out_shape=[
            jax.ShapeDtypeStruct((rows, 3 * model), low_type),
            jax.ShapeDtypeStruct((extra, 2 * model), low_type),
        ],
        grid=(HEADS,),
        in_specs=self_specs(triple, more, HEADS) + [pl.BlockSpec((rows, head), lambda h: (0, h))],
        out_specs=[
            pl.BlockSpec((rows, 3 * model), lambda h: (0, 0)),
            pl.BlockSpec((extra, 2 * model), lambda h: (0, 0)),
        ],
        compiler_params=params("arbitrary"),
        name="self_backward",
    )(triple, triple, triple, more, more, grads)


def widen_kernel(in_ref, out_ref):
    out_ref[...] = in_ref[...].astype(jnp.float32).reshape(out_ref.shape)


def side_by_side_rows(array, first, size, count):
    blocks, unused, width = array.shape
    rows = blocks * size
    if size % 16:
        parts = [array[:, (first + i) * size : (first + i + 1) * size] for i in range(count)]
        return jnp.concatenate([part.reshape(rows, width) for part in parts], axis=1).astype(jnp.float32)
    return pl.pallas_call(
        widen_kernel,
        out_shape=jax.ShapeDtypeStruct((rows, count * width), jnp.float32),
        grid=(count,),
        in_specs=[pl.BlockSpec((blocks, size, width), lambda i: (0, first + i, 0))],
        out_specs=pl.BlockSpec((rows, width), lambda i: (0, i)),
        compiler_params=params("arbitrary"),
        name="widen",
    )(array)


def ordered(bit, own, other, axis=0):
    first = jnp.where(bit == 0, own, other)
    last = jnp.where(bit == 0, other, own)
    return jnp.concatenate([first, last], axis=axis)


def half_of(array, bit, axis):
    size = array.shape[axis] // 2
    return lax.dynamic_slice_in_dim(array, bit * size, size, axis)


def swap(array, axis_name, mask):
    size = lax.axis_size(axis_name)
    return lax.ppermute(array, axis_name, [(i, i ^ mask) for i in range(size)])


class Plan:
    def __init__(self, micro_count, rows):
        self.blocks = lax.axis_size("blk")
        self.shards = lax.axis_size("fsdp")
        self.b = lax.axis_index("blk")
        self.x = lax.axis_index("fsdp")
        self.core = self.b & 1
        self.side = (self.b >> 1) & 1
        self.rows = rows
        self.micro_count = micro_count
        self.paired = self.shards == 2 and self.blocks % 4 == 0 and micro_count == 3
        if self.paired:
            self.micro = jnp.stack([self.x, jnp.int32(2)]).astype(jnp.int32)
            self.block_rows = rows
            self.per_item = 2
            self.groups = (
                (slice(0, 2 * rows), slice(0, 2 * rows), None),
                (slice(2 * rows, 3 * rows), slice(2 * rows, 3 * rows), slice(0, rows)),
            )
        else:
            self.micro = jnp.arange(micro_count, dtype=jnp.int32)
            self.block_rows = rows
            self.per_item = 1
            whole = rows * self.shards
            self.groups = tuple(
                (slice(i * rows, (i + 1) * rows), None, slice(i * whole, (i + 1) * whole))
                for i in range(micro_count)
            )

    def block_of(self, item, device):
        if self.paired and item == 1:
            return (device | 1) - 1 + self.x
        return device

    def turn(self, array):
        places = []
        for x in range(2):
            for b in range(self.blocks):
                core = b % 2
                places.append((b * 2 + x, (b - core + x) * 2 + core))
        return lax.ppermute(array, ("blk", "fsdp"), places)

    def spread(self, array):
        if not self.paired:
            return (array.reshape(-1, array.shape[-1]),)
        own = lax.dynamic_index_in_dim(array, self.x, 0, False)
        away = swap(lax.dynamic_index_in_dim(array, 1 - self.x, 0, False), "fsdp", 1)
        return own, away, self.turn(array[2])

    def send_back(self, array):
        if not self.paired:
            return (array,)
        own, away, shared = (array[i * self.rows : (i + 1) * self.rows] for i in range(3))
        return own, swap(away, "fsdp", 1), self.turn(shared)

    def placed(self, parts):
        if not self.paired:
            return parts[0].reshape(self.micro_count, self.rows, -1)
        own, other, shared = parts
        return jnp.stack([jnp.where(self.x == 0, own, other), jnp.where(self.x == 0, other, own), shared])

    def columns(self, pair, norms):
        if not self.paired:
            return (
                lax.all_gather(pair, "fsdp", axis=1, tiled=True),
                lax.all_gather(norms, "fsdp", axis=1, tiled=True),
            )
        flat = norms.reshape(-1, pair.shape[1])
        return (swap(jnp.concatenate([pair, flat], axis=0), "fsdp", 1),)

    def joined(self, pair, norms, other):
        if not self.paired:
            return other
        rows = pair.shape[0]
        return (
            ordered(self.x, pair, other[0][:rows], 1),
            ordered(self.x, norms, other[0][rows:].reshape(norms.shape), 1),
        )

    def fetch(self, weights, chips):
        if not self.paired:
            return None
        part = self.core if chips == 1 else 2 * self.core + self.side
        size = weights[0].shape[0] // (2 * chips)
        parts = [lax.dynamic_slice_in_dim(weight, part * size, size, 0) for weight in weights]
        return jnp.concatenate(parts, axis=1)

    def whole(self, weights, near, chips):
        if not self.paired:
            return [lax.all_gather(weight, "fsdp", axis=0, tiled=True) for weight in weights]
        if chips == 2:
            near = ordered(self.side, near, swap(near, "blk", 2))
        away = ordered(self.core, near, swap(near, "blk", 1))
        results, at = [], 0
        for weight in weights:
            results.append(ordered(self.x, weight, away[:, at : at + weight.shape[1]]))
            at += weight.shape[1]
        return results

    def partner_rows(self, pairs):
        if self.paired:
            return swap(pairs[2 * self.rows :], "blk", 1)
        wide = pairs.reshape(self.micro_count, self.rows, -1)
        return lax.all_gather(wide, "fsdp", axis=1, tiled=True).reshape(-1, wide.shape[-1])

    def own_pairs(self, wide, more):
        model = wide.shape[1] // 3
        if self.paired:
            back = swap(more, "blk", 1).astype(jnp.float32)
            first = 2 * self.rows
            last = (wide[first:, model:].astype(jnp.float32) + back).astype(low_type)
            return lax.dynamic_update_slice(wide, last, (first, model))
        split = more.reshape(self.micro_count, self.rows * self.shards, -1)
        back = lax.psum_scatter(split, "fsdp", scatter_dimension=1, tiled=True)
        return lax.dynamic_update_slice(wide, back.reshape(-1, back.shape[-1]), (0, model))


def added(kept, received):
    return (kept.astype(jnp.float32) + received.astype(jnp.float32)).astype(low_type)


def after(value, *others):
    if not others:
        return value
    return lax.optimization_barrier((value,) + others)[0]


class Group:
    def __init__(self, plan, units):
        self.plan = plan
        count, core = plan.blocks // 2, plan.core
        pieces = [unit.reshape(plan.shards, count, 2, -1, unit.shape[2]) for unit in units]
        self.sizes = [piece.shape[3] for piece in pieces]
        self.send = jnp.concatenate(
            [lax.dynamic_index_in_dim(piece, 1 - core, 2, False) for piece in pieces], axis=2
        )
        self.kept = jnp.concatenate([lax.dynamic_index_in_dim(piece, core, 2, False) for piece in pieces], axis=2)

    def over_core(self, *earlier):
        received = after(swap(self.send, "blk", 1), *earlier)
        mask = self.plan.shards // 2
        while mask:
            bit = jnp.where((self.plan.x & mask) > 0, 1, 0)
            self.send = added(half_of(self.kept, 1 - bit, 0), half_of(received, 1 - bit, 0))
            self.kept = added(half_of(self.kept, bit, 0), half_of(received, bit, 0))
            if mask > 1:
                received = swap(self.send, "fsdp", mask)
            mask //= 2
        return self.send

    def over_fsdp(self, *earlier):
        received = after(swap(self.send, "fsdp", 1), *earlier)
        self.total = added(self.kept, received)[0]
        return received


def over_chips(groups, *earlier):
    plan = groups[0].plan
    total = jnp.concatenate([group.total for group in groups], axis=1)
    same_core = [list(range(core, plan.blocks, 2)) for core in range(2)]
    arrived = lax.all_to_all(
        total, "blk", split_axis=0, concat_axis=0, axis_index_groups=same_core, tiled=True
    )
    arrived = after(arrived, *earlier)
    return jnp.sum(arrived.astype(jnp.float32), axis=0).astype(low_type), arrived


def from_all(sums):
    return lax.all_gather(jnp.concatenate(sums, axis=0), "blk", axis=0)


def gathered(array, sizes):
    results, at = [], 0
    for size in sizes:
        part = array[:, at : at + size].astype(jnp.float32)
        results.append(part.reshape(-1, part.shape[2]))
        at += size
    return results


def route_pixels(plan, pixels, segment_ids, pad_ids, block_map, fetch):
    blocks, labels = plan.blocks, block_map.shape[1]
    slots, features = pixels.shape[1:]
    width = slots // blocks
    routed = plan.micro.shape[0]
    label_ids = jnp.arange(labels, dtype=jnp.int32)

    def of_items(array):
        return jnp.stack([lax.dynamic_index_in_dim(array, plan.micro[i], 0, False) for i in range(routed)])

    picked = of_items(segment_ids)
    counts = jnp.sum((picked[:, None, :] == label_ids[None, :, None]).astype(jnp.float32), axis=2)
    chunks = prepare_pixels(jnp.swapaxes(pixels, 1, 2), plan.micro, width)
    spread = lax.all_to_all(chunks, "blk", split_axis=0, concat_axis=0, tiled=True)
    mask = 1
    while mask < blocks:
        counts = counts + swap(counts, "blk", mask)
        mask *= 2
    totals = counts.astype(jnp.int32)
    owners = of_items(block_map)
    images = label_ids[None, :] != of_items(pad_ids)[:, None]
    totals = jnp.where(images, totals, 0)
    earlier = label_ids[None, :] < label_ids[:, None]
    starts = jnp.sum(jnp.where(earlier[None], totals[:, None, :], 0), axis=2)
    devices = jnp.arange(blocks, dtype=jnp.int32)

    def extents(wanted):
        hit = (owners[:, None, :] == wanted[:, :, None]) & images[:, None, :]
        start = jnp.sum(jnp.where(hit, starts[:, None, :], 0), axis=2)
        return start, start + jnp.sum(jnp.where(hit, totals[:, None, :], 0), axis=2)

    def chunk_at(start, place):
        first = start // width
        return first + ((place - first) & (blocks - 1))

    def source_of(chunk):
        return jnp.clip(chunk // blocks, 0, blocks - 1)

    item = jnp.arange(routed, dtype=jnp.int32)
    wanted = jnp.stack([plan.block_of(i, devices) for i in range(routed)])
    start, finish = extents(wanted)
    flat = spread.reshape(blocks * routed, FEATURE_ROWS, width)
    piece_at = source_of(chunk_at(start, plan.b)) * routed + item[:, None]
    pieces = jnp.take(flat, piece_at.T.reshape(-1), axis=0, mode="clip")
    pieces = pieces.reshape(blocks, routed, FEATURE_ROWS, width)
    fetched, sent = fetch(chunks, pieces)
    if sent is not None:
        pieces = after(pieces, sent)
    first = lax.all_to_all(pieces, "blk", split_axis=0, concat_axis=0, tiled=True)
    largest = jnp.argmax(totals, axis=1)
    largest_start = jnp.sum(jnp.where(label_ids[None, :] == largest[:, None], starts, 0), axis=1)
    second_at = source_of(chunk_at(largest_start, plan.b) + blocks) * routed + item
    second = lax.all_gather(jnp.take(flat, second_at, axis=0, mode="clip"), "blk", axis=0, tiled=False)
    mine = jnp.stack([plan.block_of(i, plan.b) for i in range(routed)])[:, None]
    start, finish = extents(mine)
    slot = (width * chunk_at(start, devices[None, :]))[:, :, None] + jnp.arange(width, dtype=jnp.int32)
    slot = slot.reshape(routed, -1)
    slot = jnp.concatenate([slot, slot + width * blocks], axis=1)
    mask = jnp.where((slot >= start) & (slot < finish), 0.0, masked_score)
    mask = jnp.broadcast_to(mask[:, None, :], (routed, 8, mask.shape[1]))
    big = ((finish - 1) // width - start // width >= blocks).astype(jnp.int32)[:, 0]
    if width < 128:
        join = 128 // width

        def merged(array):
            parts = array.reshape(blocks // join, join, routed, FEATURE_ROWS, width)
            return parts.transpose(0, 2, 3, 1, 4).reshape(blocks // join, routed, FEATURE_ROWS, 128)

        first, second = merged(first), merged(second)
    return fetched, first, second, mask, big


def on_device(
    latents,
    pixels,
    segment_ids,
    pad_ids,
    block_map,
    norm_gains,
    norm_biases,
    pixel_gain,
    pixel_bias,
    cross_query,
    cross_kv,
    cross_out,
    cross_up,
    cross_down,
    self_qkv,
    self_out,
    self_up,
    self_down,
    cotangent,
):
    micro_count, unused, rows, model = latents.shape
    features = pixels.shape[2]
    plan = Plan(micro_count, rows)
    scaling = model**-0.5

    norm_rows = jnp.concatenate([norm_gains, norm_biases], axis=0)
    early, middle = [cross_query], [cross_out, cross_up, cross_down]
    late, last = [self_qkv], [self_out, self_up, self_down]

    def fetch(chunks, pieces):
        if not plan.paired:
            return (plan.spread(latents[:, 0]), plan.columns(cross_kv, norm_rows)) + (None,) * 4, None
        latent = plan.spread(after(latents, chunks)[:, 0])
        near_early = swap(plan.fetch([after(cross_query, chunks)], 1), "fsdp", 1)
        other = plan.columns(after(cross_kv, chunks), norm_rows)
        send = plan.fetch([after(middle[0], near_early, *latent[1:], *other)] + middle[1:], 1)
        near_middle = swap(send, "fsdp", 1)
        near_late = swap(plan.fetch([after(late[0], send, pieces)], 2), "fsdp", 1)
        near_last = swap(plan.fetch([after(last[0], send, pieces)] + last[1:], 2), "fsdp", 1)
        latent = (latent[0],) + tuple(after(part, pieces) for part in latent[1:])
        near_early, other = after(near_early, pieces), (after(other[0], pieces),)
        return (latent, other, near_early, near_middle, near_late, near_last), send

    fetched, first, second, mask, big = route_pixels(plan, pixels, segment_ids, pad_ids, block_map, fetch)
    latent, other, near_early, near_middle, near_late, near_last = fetched
    latent = jnp.concatenate(latent, axis=0).astype(jnp.float32)
    w_pair, norms = plan.joined(cross_kv, norm_rows, other)
    norms = norms.astype(jnp.float32)
    gains, biases = norms[:4], norms[4:]
    w_key, w_value = w_pair[:, :model], w_pair[:, model:]
    (w_query,) = plan.whole(early, near_early, 1)
    pixel_scaler = pixel_gain.astype(jnp.float32)
    pixel_offset = pixel_bias.astype(jnp.float32)

    def widened(rows_f32, scale):
        against = jnp.sum(rows_f32 * pixel_offset, axis=-1, keepdims=True)
        wide = jnp.concatenate([rows_f32 * pixel_scaler, against], axis=1) * scale
        return jnp.pad(wide, ((0, 0), (0, FEATURE_ROWS - features - 1))).astype(low_type)

    def narrowed(wide):
        return wide[:, :features] * pixel_scaler + wide[:, features : features + 1] * pixel_offset

    normed, scale = normalise(latent)
    hidden = (normed * gains[0] + biases[0]).astype(low_type)
    queries = product(hidden, w_query).astype(low_type)
    query_features = product_nt(queries, w_key)
    wide_queries = widened(query_features, scaling)
    if plan.paired:
        near_middle, near_late = after(near_middle, wide_queries), after(near_late, first)
    w_out, w_up, w_down = plan.whole(middle, near_middle, 1)
    (w_triple,) = plan.whole(late, near_late, 2)
    summed = cross_call(
        cross_forward_kernel, big, [wide_queries], first, second, mask, plan.block_rows, plan.per_item
    )
    if plan.paired:
        near_last, cotangent = after(near_last, summed), after(cotangent, summed)
    w_self_out, w_self_up, w_self_down = plan.whole(last, near_last, 2)
    upstream = plan.spread(cotangent[:, 0])
    attended_features = narrowed(summed).astype(low_type)
    attended = product(attended_features, w_value).astype(low_type)
    first_sum = latent + product(attended, w_out)
    second_sum, stored_one = feed_forward(first_sum, gains[1], biases[1], w_up, w_down)
    normed_two, scale_two = normalise(second_sum)
    hidden_two = (normed_two * gains[2] + biases[2]).astype(low_type)
    triple = product(hidden_two, w_triple).astype(low_type)
    more = plan.partner_rows(triple[:, model:])
    blended = self_forward(triple, more, plan.groups)
    third_sum = second_sum + product(blended, w_self_out)
    mixed, stored_three = feed_forward(third_sum, gains[3], biases[3], w_self_up, w_self_down)
    mixed = mixed.astype(low_type)

    def unit(grad):
        return grad.astype(low_type).reshape(plan.shards, -1, model)

    if plan.paired:
        upstream = (upstream[0],) + tuple(after(part, third_sum) for part in upstream[1:])
    upstream = jnp.concatenate(upstream, axis=0).astype(jnp.float32)
    low = upstream.astype(low_type)
    upstream, grad_self_up, grad_self_down, gain_three, bias_three = feed_backward(
        upstream, low, third_sum, stored_three, gains[3], w_self_up, w_self_down
    )
    low = upstream.astype(low_type)
    grad_self_out = product_tn(blended, low)
    grad_self_out = product_tn(blended, low)
    one = Group(plan, [unit(grad_self_up), unit(grad_self_down)])
    grad_blended = product_nt(low, w_self_out).astype(low_type)
    grad_blended = after(grad_blended, one.over_core(), mixed)
    triple_grads, more_grads = self_backward(triple, more, grad_blended, plan.groups)
    triple_grads, more_grads = after((triple_grads, more_grads), one.over_fsdp())
    triple_grads = plan.own_pairs(triple_grads, more_grads)
    grad_q, grad_k, grad_v = (
        unit(product_tn(hidden_two, triple_grads[:, i * model : (i + 1) * model])) for i in range(3)
    )
    two, three = Group(plan, [grad_q, grad_k]), Group(plan, [grad_v, unit(grad_self_out)])
    triple_grads = after(triple_grads, two.send, three.send)
    sums_one, arrived_one = over_chips([one])
    grad_hidden = product_nt(triple_grads, w_triple)
    down, gain_two, bias_two = norm_backward(grad_hidden, normed_two, scale_two, gains[2])
    upstream = upstream + down
    low = upstream.astype(low_type)
    grad_down = product_tn(stored_one[2], low)
    low = after(low, two.over_core())
    upstream, grad_up, unused, gain_one, bias_one = feed_backward(
        upstream, low, first_sum, stored_one, gains[1], w_up, w_down
    )
    grad_up, grad_down = unit(grad_up), unit(grad_down)
    low = upstream.astype(low_type)
    low = after(low, grad_up, grad_down, two.over_fsdp(low), three.over_core(low), arrived_one)
    grad_out = product_tn(attended, low)
    four = Group(plan, [grad_up, grad_down, unit(grad_out)])
    grad_attended = product_nt(low, w_out).astype(low_type)
    grad_value = product_tn(attended_features, grad_attended)
    grad_features = product_nt(grad_attended, w_value)
    wide_grads = after(widened(grad_features, 1.0), four.send)
    score_sums = cross_call(
        cross_backward_kernel,
        big,
        [wide_queries, wide_grads],
        first,
        second,
        mask,
        plan.block_rows,
        plan.per_item,
    )
    score_sums = after(score_sums, three.over_fsdp(score_sums), four.over_core(score_sums))
    key_sums = (narrowed(score_sums) * scaling).astype(low_type)
    grad_queries = product(key_sums, w_key).astype(low_type)
    grad_key = product_tn(key_sums, queries)
    pixel_gain_term = jnp.sum(
        query_features * score_sums[:, :features] * scaling + grad_features * summed[:, :features], axis=0
    )
    pixel_bias_term = jnp.sum(
        query_features * score_sums[:, features : features + 1] * scaling
        + grad_features * summed[:, features : features + 1],
        axis=0,
    )
    grad_query = product_tn(hidden, grad_queries)
    down, gain_zero, bias_zero = norm_backward(product_nt(grad_queries, w_query), normed, scale, gains[0])
    latents_grad = (upstream + down).astype(low_type)

    shards = plan.shards
    width = 2 * model // shards
    if shards == 2:
        rows_of_pair = jnp.stack([grad_key, grad_value]).astype(low_type)
    else:
        rows_of_pair = jnp.concatenate([grad_key, grad_value], axis=1).astype(low_type)
        rows_of_pair = rows_of_pair.reshape(features, shards, width).transpose(1, 0, 2)
    norm_terms = jnp.stack(
        [gain_zero, gain_one, gain_two, gain_three, bias_zero, bias_one, bias_two, bias_three]
    )
    pixel_terms = jnp.pad(jnp.stack([pixel_gain_term, pixel_bias_term]), ((0, 0), (0, 512 - features)))
    pixel_rows = pixel_terms.reshape(1, -1, width)
    small = jnp.concatenate(
        [
            norm_terms.reshape(8, shards, model // shards).transpose(1, 0, 2).reshape(shards, 4, width),
            jnp.broadcast_to(pixel_rows, (shards,) + pixel_rows.shape[1:]),
        ],
        axis=1,
    )
    tall = jnp.pad(rows_of_pair, ((0, 0), (0, 384 - features), (0, 0)))
    tall = lax.dynamic_update_slice(tall, small.astype(low_type), (0, 264, 0))
    grad_query = unit(grad_query)
    five = Group(plan, [grad_query, tall.reshape(shards, -1, model)])
    five.send = after(five.send, four.over_fsdp(grad_query))
    sums_two, arrived_two = over_chips([two, three], five.send)
    early_sums = from_all([sums_one, sums_two])
    sums_four, unused = over_chips([four])
    five.over_core()
    arrived = five.over_fsdp()
    mixed = plan.send_back(after(mixed, arrived))
    latents_grad = plan.send_back(after(latents_grad, arrived))
    sums_five, unused = over_chips([five])
    late_sums = from_all([sums_four, sums_five])
    size = one.sizes[0]
    grad_self_up, grad_self_down = gathered(early_sums, one.sizes)
    grad_triple = side_by_side_rows(early_sums, 2, size, 3)
    (grad_self_out,) = gathered(early_sums[:, 5 * size :], [size])
    latents_grad = plan.placed(latents_grad).astype(jnp.float32)
    grad_up, grad_down, grad_out, grad_query, tall = gathered(late_sums, four.sizes + five.sizes)
    tall = tall.reshape(384, width)
    norm_part = tall[264:268].reshape(8, model // shards)
    pixel_part = tall[268 : 268 + pixel_rows.shape[1]].reshape(2, 512)
    return (
        plan.placed(mixed)[:, None],
        latents_grad[:, None],
        norm_part[:4],
        norm_part[4:],
        pixel_part[0, :features],
        pixel_part[1, :features],
        grad_query,
        tall[:features],
        grad_out,
        grad_up,
        grad_down,
        grad_triple,
        grad_self_out,
        grad_self_up,
        grad_self_down,
    )


def solution(mesh):
    placed = (
        P(None, "blk", "fsdp", None),
        P(None, "blk", None),
        P(None, "blk"),
        P(),
        P(),
        P(None, "fsdp"),
        P(None, "fsdp"),
        P(),
        P(),
        P("fsdp", None),
        P(None, "fsdp"),
        P("fsdp", None),
        P("fsdp", None),
        P("fsdp", None),
        P("fsdp", None),
        P("fsdp", None),
        P("fsdp", None),
        P("fsdp", None),
        P(None, "blk", "fsdp", None),
    )
    return jax.shard_map(
        on_device,
        mesh=mesh,
        in_specs=placed,
        out_specs=(
            P(None, "blk", "fsdp", None),
            P(None, "blk", "fsdp", None),
            P(None, "fsdp"),
            P(None, "fsdp"),
            P(),
            P(),
            P("fsdp", None),
            P(None, "fsdp"),
            P("fsdp", None),
            P("fsdp", None),
            P("fsdp", None),
            P("fsdp", None),
            P("fsdp", None),
            P("fsdp", None),
            P("fsdp", None),
        ),
        check_vma=False,
    )
```

```python
import functools

import jax
import jax.numpy as jnp
from jax import lax
from jax.experimental import pallas as pl
from jax.experimental.pallas import tpu as pltpu
from jax.sharding import PartitionSpec as P

HEADS = 8
FEATURE_ROWS = 272
VMEM_LIMIT = 56 * 1024 * 1024

epsilon = 1e-05
masked_score = -1e30
low_type = jnp.bfloat16


def product(a, b):
    return jnp.dot(a, b, preferred_element_type=jnp.float32)


def product_tn(a, b):
    return lax.dot_general(a, b, (((0,), (0,)), ((), ())), preferred_element_type=jnp.float32)


def product_nt(a, b):
    return lax.dot_general(a, b, (((1,), (1,)), ((), ())), preferred_element_type=jnp.float32)


def normalise(rows):
    centre = rows - jnp.mean(rows, axis=-1, keepdims=True)
    scale = lax.rsqrt(jnp.mean(centre * centre, axis=-1, keepdims=True) + epsilon)
    return centre * scale, scale


def norm_backward(upstream, normed, scale, gain):
    gain_term = jnp.sum(upstream * normed, axis=0)
    bias_term = jnp.sum(upstream, axis=0)
    inner = upstream * gain
    down = scale * (
        inner
        - jnp.mean(inner, axis=-1, keepdims=True)
        - normed * jnp.mean(inner * normed, axis=-1, keepdims=True)
    )
    return down, gain_term, bias_term


def feed_forward(rows, gain, bias, w_up, w_down):
    normed, scale = normalise(rows)
    hidden = (normed * gain + bias).astype(low_type)
    upward = product(hidden, w_up)
    share = 0.5 * (1.0 + lax.erf(upward * (0.5**0.5)))
    slope = share + upward * jnp.exp(-0.5 * upward * upward) * 0.3989422804014327
    active = (upward * share).astype(low_type)
    return rows + product(active, w_down), (hidden, slope, active)


def feed_backward(upstream, low, rows, stored, gain, w_up, w_down):
    hidden, slope, active = stored
    grad_down = product_tn(active, low)
    grad_upward = (product_nt(low, w_down) * slope).astype(low_type)
    grad_up = product_tn(hidden, grad_upward)
    normed, scale = normalise(rows)
    down, gain_term, bias_term = norm_backward(product_nt(grad_upward, w_up), normed, scale, gain)
    return upstream + down, grad_up, grad_down, gain_term, bias_term


def nt(a, b):
    return lax.dot_general(a, b, (((1,), (1,)), ((), ())), preferred_element_type=jnp.float32)


def tn(a, b):
    return lax.dot_general(a, b, (((0,), (0,)), ((), ())), preferred_element_type=jnp.float32)


def params(*semantics):
    return pltpu.CompilerParams(dimension_semantics=semantics, vmem_limit_bytes=VMEM_LIMIT)


def pixel_kernel(micro_ref, pixel_ref, count_ref, out_ref):
    features = pixel_ref.shape[1]
    width = out_ref.shape[3]
    pixels = pixel_ref[0].astype(jnp.float32)
    centre = pixels - jnp.mean(pixels, axis=0, keepdims=True)
    spread = jnp.mean(centre * centre, axis=0, keepdims=True)
    normed = centre * lax.rsqrt(spread + epsilon)
    pad = jnp.zeros((FEATURE_ROWS - features, normed.shape[1]), jnp.float32)
    tall = jnp.concatenate([normed, pad], axis=0)
    row = lax.broadcasted_iota(jnp.int32, (FEATURE_ROWS, width), 0)
    high, rest = count_ref[0][:1, :width], count_ref[0][1:2, :width]
    for part in range(out_ref.shape[0]):
        piece = tall[:, part * width : (part + 1) * width]
        piece = jnp.where(row == features, 1.0, piece)
        piece = jnp.where(row == features + 1, high, jnp.where(row == features + 2, rest, piece))
        out_ref[part, 0] = piece.astype(low_type)


def prepare_pixels(pixels, micro, counts, width):
    routed = micro.shape[0]
    features, slots = pixels.shape[1:]
    step = min(slots, 1024)
    return pl.pallas_call(
        pixel_kernel,
        out_shape=jax.ShapeDtypeStruct((slots // width, routed, FEATURE_ROWS, width), low_type),
        grid_spec=pltpu.PrefetchScalarGridSpec(
            num_scalar_prefetch=1,
            grid=(routed, slots // step),
            in_specs=[
                pl.BlockSpec((1, features, step), lambda i, s, m: (m[i], 0, s)),
                pl.BlockSpec((1, 8, 128), lambda i, s, m: (i, 0, 0)),
            ],
            out_specs=pl.BlockSpec((step // width, 1, FEATURE_ROWS, width), lambda i, s, m: (s, i, 0, 0)),
        ),
        compiler_params=params("arbitrary", "arbitrary"),
        name="prepare_pixels",
    )(micro, pixels, counts)


def side_by_side(ref):
    return jnp.concatenate([ref[tile, 0] for tile in range(ref.shape[0])], axis=1)


def cross_forward_kernel(items, big_ref, query_ref, first_ref, second_ref, mask_ref, out_ref):
    item = pl.program_id(0) // items
    lanes = mask_ref.shape[2] // 2

    def attend(features, mask):
        scores = product(query_ref[...], features) + mask
        top = jnp.max(scores, axis=-1, keepdims=True)
        weights = jnp.exp(scores - top)
        total = jnp.sum(weights, axis=-1, keepdims=True)
        out_ref[...] = nt(weights.astype(low_type), features) / total

    @pl.when(big_ref[item] == 0)
    def small():
        attend(side_by_side(first_ref), mask_ref[0][:1, :lanes])

    @pl.when(big_ref[item] != 0)
    def large():
        both = jnp.concatenate([side_by_side(first_ref), side_by_side(second_ref)], axis=1)
        attend(both, mask_ref[0][:1])


def cross_backward_kernel(items, big_ref, query_ref, grad_ref, first_ref, second_ref, mask_ref, out_ref):
    item = pl.program_id(0) // items
    lanes = mask_ref.shape[2] // 2

    def attend(features, mask):
        scores = product(query_ref[...], features) + mask
        top = jnp.max(scores, axis=-1, keepdims=True)
        weights = jnp.exp(scores - top)
        shares = weights * (1.0 / jnp.sum(weights, axis=-1, keepdims=True))
        grad_shares = product(grad_ref[...], features)
        inner = jnp.sum(shares * grad_shares, axis=-1, keepdims=True)
        grad_scores = (shares * (grad_shares - inner)).astype(low_type)
        out_ref[...] = nt(grad_scores, features)

    @pl.when(big_ref[item] == 0)
    def small():
        attend(side_by_side(first_ref), mask_ref[0][:1, :lanes])

    @pl.when(big_ref[item] != 0)
    def large():
        both = jnp.concatenate([side_by_side(first_ref), side_by_side(second_ref)], axis=1)
        attend(both, mask_ref[0][:1])


def cross_call(kernel, big, rows, first, second, mask, block, per_item):
    count = rows[0].shape[0]
    tiles, width = first.shape[0], first.shape[3]
    row_spec = pl.BlockSpec((block, FEATURE_ROWS), lambda i, big: (i, 0))
    tile_spec = pl.BlockSpec((tiles, 1, FEATURE_ROWS, width), lambda i, big: (0, i // per_item, 0, 0))
    return pl.pallas_call(
        functools.partial(kernel, per_item),
        out_shape=jax.ShapeDtypeStruct((count, FEATURE_ROWS), jnp.float32),
        grid_spec=pltpu.PrefetchScalarGridSpec(
            num_scalar_prefetch=1,
            grid=(count // block,),
            in_specs=[row_spec] * len(rows)
            + [tile_spec, tile_spec]
            + [pl.BlockSpec((1, 8, mask.shape[2]), lambda i, big: (i // per_item, 0, 0))],
            out_specs=row_spec,
        ),
        compiler_params=params("arbitrary"),
        name="cross_attention",
    )(big, *rows, first, second, mask)


def self_forward_kernel(groups, scaling, q_ref, k_ref, v_ref, more_k_ref, more_v_ref, out_ref):
    for q_rows, own, more in groups:
        keys, values = keys_of(own, more, k_ref, v_ref, more_k_ref, more_v_ref)
        scores = nt(q_ref[q_rows], keys) * scaling
        weights = jnp.exp(scores - jnp.max(scores, axis=-1, keepdims=True))
        total = jnp.sum(weights, axis=-1, keepdims=True)
        out_ref[q_rows, :] = (product(weights.astype(low_type), values) / total).astype(low_type)


def keys_of(own, more, k_ref, v_ref, more_k_ref, more_v_ref):
    keys, values = [], []
    if own is not None:
        keys.append(k_ref[own])
        values.append(v_ref[own])
    if more is not None:
        keys.append(more_k_ref[more])
        values.append(more_v_ref[more])
    if len(keys) == 1:
        return keys[0], values[0]
    return jnp.concatenate(keys, axis=0), jnp.concatenate(values, axis=0)


def self_backward_kernel(
    groups,
    scaling,
    q_ref,
    k_ref,
    v_ref,
    more_k_ref,
    more_v_ref,
    grad_ref,
    wide_ref,
    more_ref,
):
    head = q_ref.shape[1]
    model = wide_ref.shape[1] // 3
    column = pl.multiple_of(pl.program_id(0) * head, head)
    at_q, at_k, at_v = (pl.ds(pl.multiple_of(part * model + column, head), head) for part in range(3))
    for q_rows, own, more in groups:
        keys, values = keys_of(own, more, k_ref, v_ref, more_k_ref, more_v_ref)
        queries = q_ref[q_rows]
        grads = grad_ref[q_rows]
        scores = nt(keys, queries) * scaling
        weights = jnp.exp(scores - jnp.max(scores, axis=0, keepdims=True))
        shares = weights * (1.0 / jnp.sum(weights, axis=0, keepdims=True))
        grad_shares = nt(values, grads)
        inner = jnp.sum(shares * grad_shares, axis=0, keepdims=True)
        grad_scores = (shares * (grad_shares - inner)).astype(low_type)
        wide_ref[q_rows, at_q] = (tn(grad_scores, keys) * scaling).astype(low_type)
        dk = (product(grad_scores, queries) * scaling).astype(low_type)
        dv = product(shares.astype(low_type), grads).astype(low_type)
        split = 0
        if own is not None:
            split = own.stop - own.start
            wide_ref[own, at_k] = dk[:split]
            wide_ref[own, at_v] = dv[:split]
        if more is not None:
            more_ref[more, at_q] = dk[split:]
            more_ref[more, at_k] = dv[split:]


def self_specs(triple, more, heads):
    rows, width = triple.shape[0], triple.shape[1] // 3 // heads
    extra = more.shape[0]
    return [
        pl.BlockSpec((rows, width), lambda h: (0, h)),
        pl.BlockSpec((rows, width), lambda h: (0, heads + h)),
        pl.BlockSpec((rows, width), lambda h: (0, 2 * heads + h)),
        pl.BlockSpec((extra, width), lambda h: (0, h)),
        pl.BlockSpec((extra, width), lambda h: (0, heads + h)),
    ]


def self_forward(triple, more, groups):
    rows, model = triple.shape[0], triple.shape[1] // 3
    head = model // HEADS
    return pl.pallas_call(
        functools.partial(self_forward_kernel, groups, head**-0.5),
        out_shape=jax.ShapeDtypeStruct((rows, model), low_type),
        grid=(HEADS,),
        in_specs=self_specs(triple, more, HEADS),
        out_specs=pl.BlockSpec((rows, head), lambda h: (0, h)),
        compiler_params=params("arbitrary"),
        name="self_forward",
    )(triple, triple, triple, more, more)


def self_backward(triple, more, grads, groups):
    rows, model = triple.shape[0], triple.shape[1] // 3
    head = model // HEADS
    extra = more.shape[0]
    return pl.pallas_call(
        functools.partial(self_backward_kernel, groups, head**-0.5),
        out_shape=[
            jax.ShapeDtypeStruct((rows, 3 * model), low_type),
            jax.ShapeDtypeStruct((extra, 2 * model), low_type),
        ],
        grid=(HEADS,),
        in_specs=self_specs(triple, more, HEADS) + [pl.BlockSpec((rows, head), lambda h: (0, h))],
        out_specs=[
            pl.BlockSpec((rows, 3 * model), lambda h: (0, 0)),
            pl.BlockSpec((extra, 2 * model), lambda h: (0, 0)),
        ],
        compiler_params=params("arbitrary"),
        name="self_backward",
    )(triple, triple, triple, more, more, grads)


def widen_kernel(in_ref, out_ref):
    out_ref[...] = in_ref[...].astype(jnp.float32).reshape(out_ref.shape)


def side_by_side_rows(array, first, size, count):
    blocks, unused, width = array.shape
    rows = blocks * size
    if size % 16:
        parts = [array[:, (first + i) * size : (first + i + 1) * size] for i in range(count)]
        return jnp.concatenate([part.reshape(rows, width) for part in parts], axis=1).astype(jnp.float32)
    return pl.pallas_call(
        widen_kernel,
        out_shape=jax.ShapeDtypeStruct((rows, count * width), jnp.float32),
        grid=(count,),
        in_specs=[pl.BlockSpec((blocks, size, width), lambda i: (0, first + i, 0))],
        out_specs=pl.BlockSpec((rows, width), lambda i: (0, i)),
        compiler_params=params("arbitrary"),
        name="widen",
    )(array)


def widen_each_kernel(in_ref, *out_refs):
    size = out_refs[0].shape[0] // in_ref.shape[0]
    for i, out_ref in enumerate(out_refs):
        part = in_ref[:, i * size : (i + 1) * size].astype(jnp.float32)
        out_ref[...] = part.reshape(out_ref.shape)


def rows_of_each(array, size, count):
    blocks, unused, width = array.shape
    if size % 16:
        parts = [array[:, i * size : (i + 1) * size].astype(jnp.float32) for i in range(count)]
        return [part.reshape(blocks * size, width) for part in parts]
    half = width // 2
    return pl.pallas_call(
        widen_each_kernel,
        out_shape=[jax.ShapeDtypeStruct((blocks * size, width), jnp.float32)] * count,
        grid=(2,),
        in_specs=[pl.BlockSpec((blocks, array.shape[1], half), lambda i: (0, 0, i))],
        out_specs=[pl.BlockSpec((blocks * size, half), lambda i: (0, i))] * count,
        compiler_params=params("arbitrary"),
        name="widen_each",
    )(array)


def ordered(bit, own, other, axis=0):
    first = jnp.where(bit == 0, own, other)
    last = jnp.where(bit == 0, other, own)
    return jnp.concatenate([first, last], axis=axis)


def half_of(array, bit, axis):
    size = array.shape[axis] // 2
    return lax.dynamic_slice_in_dim(array, bit * size, size, axis)


def swap(array, axis_name, mask):
    size = lax.axis_size(axis_name)
    return lax.ppermute(array, axis_name, [(i, i ^ mask) for i in range(size)])


class Plan:
    def __init__(self, micro_count, rows):
        self.blocks = lax.axis_size("blk")
        self.shards = lax.axis_size("fsdp")
        self.b = lax.axis_index("blk")
        self.x = lax.axis_index("fsdp")
        self.core = self.b & 1
        self.side = (self.b >> 1) & 1
        self.rows = rows
        self.micro_count = micro_count
        self.paired = self.shards == 2 and self.blocks % 4 == 0 and micro_count == 3
        if self.paired:
            self.micro = jnp.stack([self.x, jnp.int32(2)]).astype(jnp.int32)
            self.block_rows = rows
            self.per_item = 2
            self.groups = (
                (slice(0, 2 * rows), slice(0, 2 * rows), None),
                (slice(2 * rows, 3 * rows), slice(2 * rows, 3 * rows), slice(0, rows)),
            )
        else:
            self.micro = jnp.arange(micro_count, dtype=jnp.int32)
            self.block_rows = rows
            self.per_item = 1
            whole = rows * self.shards
            self.groups = tuple(
                (slice(i * rows, (i + 1) * rows), None, slice(i * whole, (i + 1) * whole))
                for i in range(micro_count)
            )

    def block_of(self, item, device):
        if self.paired and item == 1:
            return (device | 1) - 1 + self.x
        return device

    def turn(self, array):
        places = []
        for x in range(2):
            for b in range(self.blocks):
                core = b % 2
                places.append((b * 2 + x, (b - core + x) * 2 + core))
        return lax.ppermute(array, ("blk", "fsdp"), places)

    def spread(self, array):
        if not self.paired:
            return (array.reshape(-1, array.shape[-1]),)
        own = lax.dynamic_index_in_dim(array, self.x, 0, False)
        away = swap(lax.dynamic_index_in_dim(array, 1 - self.x, 0, False), "fsdp", 1)
        return own, away, self.turn(array[2])

    def send_back(self, array):
        if not self.paired:
            return (array,)
        own, away, shared = (array[i * self.rows : (i + 1) * self.rows] for i in range(3))
        return own, swap(away, "fsdp", 1), self.turn(shared)

    def placed(self, parts):
        if not self.paired:
            return parts[0].reshape(self.micro_count, self.rows, -1)
        own, other, shared = parts
        return jnp.stack([jnp.where(self.x == 0, own, other), jnp.where(self.x == 0, other, own), shared])

    def columns(self, pair, norms):
        if not self.paired:
            return (
                lax.all_gather(pair, "fsdp", axis=1, tiled=True),
                lax.all_gather(norms, "fsdp", axis=1, tiled=True),
            )
        flat = norms.reshape(-1, pair.shape[1])
        return (swap(jnp.concatenate([pair, flat], axis=0), "fsdp", 1),)

    def joined(self, pair, norms, other):
        if not self.paired:
            return other
        rows = pair.shape[0]
        return (
            ordered(self.x, pair, other[0][:rows], 1),
            ordered(self.x, norms, other[0][rows:].reshape(norms.shape), 1),
        )

    def fetch(self, weights, chips):
        if not self.paired:
            return None
        part = self.core if chips == 1 else 2 * self.core + self.side
        size = weights[0].shape[0] // (2 * chips)
        parts = [lax.dynamic_slice_in_dim(weight, part * size, size, 0) for weight in weights]
        return jnp.concatenate(parts, axis=1)

    def whole(self, weights, near, chips):
        if not self.paired:
            return [lax.all_gather(weight, "fsdp", axis=0, tiled=True) for weight in weights]
        if chips == 2:
            near = ordered(self.side, near, swap(near, "blk", 2))
        away = ordered(self.core, near, swap(near, "blk", 1))
        results, at = [], 0
        for weight in weights:
            results.append(ordered(self.x, weight, away[:, at : at + weight.shape[1]]))
            at += weight.shape[1]
        return results

    def partner_rows(self, pairs):
        if self.paired:
            return swap(pairs[2 * self.rows :], "blk", 1)
        wide = pairs.reshape(self.micro_count, self.rows, -1)
        return lax.all_gather(wide, "fsdp", axis=1, tiled=True).reshape(-1, wide.shape[-1])

    def own_pairs(self, wide, more):
        model = wide.shape[1] // 3
        if self.paired:
            back = swap(more, "blk", 1).astype(jnp.float32)
            first = 2 * self.rows
            last = (wide[first:, model:].astype(jnp.float32) + back).astype(low_type)
            return lax.dynamic_update_slice(wide, last, (first, model))
        split = more.reshape(self.micro_count, self.rows * self.shards, -1)
        back = lax.psum_scatter(split, "fsdp", scatter_dimension=1, tiled=True)
        return lax.dynamic_update_slice(wide, back.reshape(-1, back.shape[-1]), (0, model))


def added(kept, received):
    return (kept.astype(jnp.float32) + received.astype(jnp.float32)).astype(low_type)


def after(value, *others):
    if not others:
        return value
    return lax.optimization_barrier((value,) + others)[0]


class Group:
    def __init__(self, plan, units):
        self.plan = plan
        count, core = plan.blocks // 2, plan.core
        pieces = [unit.reshape(plan.shards, count, 2, -1, unit.shape[2]) for unit in units]
        self.sizes = [piece.shape[3] for piece in pieces]
        self.send = jnp.concatenate(
            [lax.dynamic_index_in_dim(piece, 1 - core, 2, False) for piece in pieces], axis=2
        )
        self.kept = jnp.concatenate([lax.dynamic_index_in_dim(piece, core, 2, False) for piece in pieces], axis=2)

    def over_core(self, *earlier):
        received = after(swap(self.send, "blk", 1), *earlier)
        mask = self.plan.shards // 2
        while mask:
            bit = jnp.where((self.plan.x & mask) > 0, 1, 0)
            self.send = added(half_of(self.kept, 1 - bit, 0), half_of(received, 1 - bit, 0))
            self.kept = added(half_of(self.kept, bit, 0), half_of(received, bit, 0))
            if mask > 1:
                received = swap(self.send, "fsdp", mask)
            mask //= 2
        return self.send

    def over_fsdp(self, *earlier):
        received = after(swap(self.send, "fsdp", 1), *earlier)
        self.total = added(self.kept, received)[0]
        return received


def over_chips(groups, *earlier):
    plan = groups[0].plan
    total = jnp.concatenate([group.total for group in groups], axis=1)
    same_core = [list(range(core, plan.blocks, 2)) for core in range(2)]
    arrived = lax.all_to_all(
        total, "blk", split_axis=0, concat_axis=0, axis_index_groups=same_core, tiled=True
    )
    arrived = after(arrived, *earlier)
    return jnp.sum(arrived.astype(jnp.float32), axis=0).astype(low_type), arrived


def from_all(sums):
    return lax.all_gather(jnp.concatenate(sums, axis=0), "blk", axis=0)


def gathered(array, sizes):
    results, at = [], 0
    for size in sizes:
        part = array[:, at : at + size].astype(jnp.float32)
        results.append(part.reshape(-1, part.shape[2]))
        at += size
    return results


def route_pixels(plan, pixels, segment_ids, pad_ids, block_map, fetch):
    blocks, labels = plan.blocks, block_map.shape[1]
    slots, features = pixels.shape[1:]
    width = slots // blocks
    routed = plan.micro.shape[0]
    label_ids = jnp.arange(labels, dtype=jnp.int32)

    def of_items(array):
        return jnp.stack([lax.dynamic_index_in_dim(array, plan.micro[i], 0, False) for i in range(routed)])

    picked = of_items(segment_ids)
    counts = jnp.sum((picked[:, None, :] == label_ids[None, :, None]).astype(jnp.int32), axis=2)
    counts = jnp.stack([counts >> 4, counts & 15], axis=1).astype(jnp.float32)
    counts = jnp.pad(counts, ((0, 0), (0, 6), (0, 128 - labels)))
    chunks = prepare_pixels(jnp.swapaxes(pixels, 1, 2), plan.micro, counts, width)
    spread = lax.all_to_all(chunks, "blk", split_axis=0, concat_axis=0, tiled=True)
    arrived = spread[:, :, features + 1 : features + 3, :labels].astype(jnp.int32)
    totals = jnp.sum(16 * arrived[:, :, 0] + arrived[:, :, 1], axis=0)
    owners = of_items(block_map)
    images = label_ids[None, :] != of_items(pad_ids)[:, None]
    totals = jnp.where(images, totals, 0)
    earlier = label_ids[None, :] < label_ids[:, None]
    starts = jnp.sum(jnp.where(earlier[None], totals[:, None, :], 0), axis=2)
    devices = jnp.arange(blocks, dtype=jnp.int32)

    def extents(wanted):
        hit = (owners[:, None, :] == wanted[:, :, None]) & images[:, None, :]
        start = jnp.sum(jnp.where(hit, starts[:, None, :], 0), axis=2)
        return start, start + jnp.sum(jnp.where(hit, totals[:, None, :], 0), axis=2)

    def chunk_at(start, place):
        first = start // width
        return first + ((place - first) & (blocks - 1))

    def source_of(chunk):
        return jnp.clip(chunk // blocks, 0, blocks - 1)

    item = jnp.arange(routed, dtype=jnp.int32)
    wanted = jnp.stack([plan.block_of(i, devices) for i in range(routed)])
    start, finish = extents(wanted)
    flat = spread.reshape(blocks * routed, FEATURE_ROWS, width)
    piece_at = source_of(chunk_at(start, plan.b)) * routed + item[:, None]
    pieces = jnp.take(flat, piece_at.T.reshape(-1), axis=0, mode="clip")
    pieces = pieces.reshape(blocks, routed, FEATURE_ROWS, width)
    fetched, sent = fetch(chunks, pieces)
    if sent is not None:
        pieces = after(pieces, sent)
    first = lax.all_to_all(pieces, "blk", split_axis=0, concat_axis=0, tiled=True)
    largest = jnp.argmax(totals, axis=1)
    largest_start = jnp.sum(jnp.where(label_ids[None, :] == largest[:, None], starts, 0), axis=1)
    second_at = source_of(chunk_at(largest_start, plan.b) + blocks) * routed + item
    second = lax.all_gather(jnp.take(flat, second_at, axis=0, mode="clip"), "blk", axis=0, tiled=False)
    mine = jnp.stack([plan.block_of(i, plan.b) for i in range(routed)])[:, None]
    start, finish = extents(mine)
    slot = (width * chunk_at(start, devices[None, :]))[:, :, None] + jnp.arange(width, dtype=jnp.int32)
    slot = slot.reshape(routed, -1)
    slot = jnp.concatenate([slot, slot + width * blocks], axis=1)
    mask = jnp.where((slot >= start) & (slot < finish), 0.0, masked_score)
    mask = jnp.broadcast_to(mask[:, None, :], (routed, 8, mask.shape[1]))
    big = ((finish - 1) // width - start // width >= blocks).astype(jnp.int32)[:, 0]
    if width < 128:
        join = 128 // width

        def merged(array):
            parts = array.reshape(blocks // join, join, routed, FEATURE_ROWS, width)
            return parts.transpose(0, 2, 3, 1, 4).reshape(blocks // join, routed, FEATURE_ROWS, 128)

        first, second = merged(first), merged(second)
    return fetched, first, second, mask, big


def on_device(
    latents,
    pixels,
    segment_ids,
    pad_ids,
    block_map,
    norm_gains,
    norm_biases,
    pixel_gain,
    pixel_bias,
    cross_query,
    cross_kv,
    cross_out,
    cross_up,
    cross_down,
    self_qkv,
    self_out,
    self_up,
    self_down,
    cotangent,
):
    micro_count, unused, rows, model = latents.shape
    features = pixels.shape[2]
    plan = Plan(micro_count, rows)
    scaling = model**-0.5

    norm_rows = jnp.concatenate([norm_gains, norm_biases], axis=0)
    early, middle = [cross_query], [cross_out, cross_up, cross_down]
    late, last = [self_qkv], [self_out, self_up, self_down]

    def fetch(chunks, pieces):
        if not plan.paired:
            return (plan.spread(latents[:, 0]), plan.columns(cross_kv, norm_rows)) + (None,) * 4, None
        latent = plan.spread(after(latents, chunks)[:, 0])
        near_early = swap(plan.fetch([after(cross_query, chunks)], 1), "fsdp", 1)
        other = plan.columns(after(cross_kv, chunks), norm_rows)
        send = plan.fetch([after(middle[0], near_early, *latent[1:], *other)] + middle[1:], 1)
        near_middle = swap(send, "fsdp", 1)
        near_late = swap(plan.fetch([after(late[0], send, pieces)], 2), "fsdp", 1)
        near_last = swap(plan.fetch([after(last[0], send, pieces)] + last[1:], 2), "fsdp", 1)
        latent = (latent[0],) + tuple(after(part, pieces) for part in latent[1:])
        near_early, other = after(near_early, pieces), (after(other[0], pieces),)
        return (latent, other, near_early, near_middle, near_late, near_last), send

    fetched, first, second, mask, big = route_pixels(plan, pixels, segment_ids, pad_ids, block_map, fetch)
    latent, other, near_early, near_middle, near_late, near_last = fetched
    latent = jnp.concatenate(latent, axis=0).astype(jnp.float32)
    w_pair, norms = plan.joined(cross_kv, norm_rows, other)
    norms = norms.astype(jnp.float32)
    gains, biases = norms[:4], norms[4:]
    w_key, w_value = w_pair[:, :model], w_pair[:, model:]
    (w_query,) = plan.whole(early, near_early, 1)
    pixel_scaler = pixel_gain.astype(jnp.float32)
    pixel_offset = pixel_bias.astype(jnp.float32)

    def widened(rows_f32, scale):
        against = jnp.sum(rows_f32 * pixel_offset, axis=-1, keepdims=True)
        wide = jnp.concatenate([rows_f32 * pixel_scaler, against], axis=1) * scale
        return jnp.pad(wide, ((0, 0), (0, FEATURE_ROWS - features - 1))).astype(low_type)

    def narrowed(wide):
        return wide[:, :features] * pixel_scaler + wide[:, features : features + 1] * pixel_offset

    normed, scale = normalise(latent)
    hidden = (normed * gains[0] + biases[0]).astype(low_type)
    queries = product(hidden, w_query).astype(low_type)
    query_features = product_nt(queries, w_key)
    wide_queries = widened(query_features, scaling)
    if plan.paired:
        near_middle, near_late = after(near_middle, wide_queries), after(near_late, first)
    w_out, w_up, w_down = plan.whole(middle, near_middle, 1)
    (w_triple,) = plan.whole(late, near_late, 2)
    summed = cross_call(
        cross_forward_kernel, big, [wide_queries], first, second, mask, plan.block_rows, plan.per_item
    )
    if plan.paired:
        near_last, cotangent = after(near_last, summed), after(cotangent, summed)
    w_self_out, w_self_up, w_self_down = plan.whole(last, near_last, 2)
    upstream = plan.spread(cotangent[:, 0])
    attended_features = narrowed(summed).astype(low_type)
    attended = product(attended_features, w_value).astype(low_type)
    first_sum = latent + product(attended, w_out)
    second_sum, stored_one = feed_forward(first_sum, gains[1], biases[1], w_up, w_down)
    normed_two, scale_two = normalise(second_sum)
    hidden_two = (normed_two * gains[2] + biases[2]).astype(low_type)
    triple = product(hidden_two, w_triple).astype(low_type)
    more = plan.partner_rows(triple[:, model:])
    blended = self_forward(triple, more, plan.groups)
    third_sum = second_sum + product(blended, w_self_out)
    mixed, stored_three = feed_forward(third_sum, gains[3], biases[3], w_self_up, w_self_down)
    mixed = mixed.astype(low_type)

    def unit(grad):
        return grad.astype(low_type).reshape(plan.shards, -1, model)

    if plan.paired:
        upstream = (upstream[0],) + tuple(after(part, third_sum) for part in upstream[1:])
    upstream = jnp.concatenate(upstream, axis=0).astype(jnp.float32)
    low = upstream.astype(low_type)
    upstream, grad_self_up, grad_self_down, gain_three, bias_three = feed_backward(
        upstream, low, third_sum, stored_three, gains[3], w_self_up, w_self_down
    )
    low = upstream.astype(low_type)
    grad_self_out = product_tn(blended, low)
    grad_self_out = product_tn(blended, low)
    one = Group(plan, [unit(grad_self_up), unit(grad_self_down)])
    grad_blended = product_nt(low, w_self_out).astype(low_type)
    grad_blended = after(grad_blended, one.over_core(), mixed)
    triple_grads, more_grads = self_backward(triple, more, grad_blended, plan.groups)
    triple_grads, more_grads = after((triple_grads, more_grads), one.over_fsdp())
    triple_grads = plan.own_pairs(triple_grads, more_grads)
    grad_q, grad_k, grad_v = (
        unit(product_tn(hidden_two, triple_grads[:, i * model : (i + 1) * model])) for i in range(3)
    )
    two, three = Group(plan, [grad_q, grad_k]), Group(plan, [grad_v, unit(grad_self_out)])
    triple_grads = after(triple_grads, two.send, three.send)
    sums_one, arrived_one = over_chips([one])
    grad_hidden = product_nt(triple_grads, w_triple)
    down, gain_two, bias_two = norm_backward(grad_hidden, normed_two, scale_two, gains[2])
    upstream = upstream + down
    low = upstream.astype(low_type)
    grad_down = product_tn(stored_one[2], low)
    low = after(low, two.over_core())
    upstream, grad_up, unused, gain_one, bias_one = feed_backward(
        upstream, low, first_sum, stored_one, gains[1], w_up, w_down
    )
    grad_up, grad_down = unit(grad_up), unit(grad_down)
    low = upstream.astype(low_type)
    low = after(low, grad_up, grad_down, two.over_fsdp(low), three.over_core(low), arrived_one)
    grad_out = product_tn(attended, low)
    four = Group(plan, [grad_up, grad_down, unit(grad_out)])
    grad_attended = product_nt(low, w_out).astype(low_type)
    grad_value = product_tn(attended_features, grad_attended)
    grad_features = product_nt(grad_attended, w_value)
    wide_grads = after(widened(grad_features, 1.0), four.send)
    score_sums = cross_call(
        cross_backward_kernel,
        big,
        [wide_queries, wide_grads],
        first,
        second,
        mask,
        plan.block_rows,
        plan.per_item,
    )
    score_sums = after(score_sums, three.over_fsdp(score_sums), four.over_core(score_sums))
    key_sums = (narrowed(score_sums) * scaling).astype(low_type)
    grad_queries = product(key_sums, w_key).astype(low_type)
    grad_key = product_tn(key_sums, queries)
    pixel_gain_term = jnp.sum(
        query_features * score_sums[:, :features] * scaling + grad_features * summed[:, :features], axis=0
    )
    pixel_bias_term = jnp.sum(
        query_features * score_sums[:, features : features + 1] * scaling
        + grad_features * summed[:, features : features + 1],
        axis=0,
    )
    grad_query = product_tn(hidden, grad_queries)
    down, gain_zero, bias_zero = norm_backward(product_nt(grad_queries, w_query), normed, scale, gains[0])
    latents_grad = (upstream + down).astype(low_type)

    shards = plan.shards
    width = 2 * model // shards
    if shards == 2:
        rows_of_pair = jnp.stack([grad_key, grad_value]).astype(low_type)
    else:
        rows_of_pair = jnp.concatenate([grad_key, grad_value], axis=1).astype(low_type)
        rows_of_pair = rows_of_pair.reshape(features, shards, width).transpose(1, 0, 2)
    norm_terms = jnp.stack(
        [gain_zero, gain_one, gain_two, gain_three, bias_zero, bias_one, bias_two, bias_three]
    )
    pixel_terms = jnp.pad(jnp.stack([pixel_gain_term, pixel_bias_term]), ((0, 0), (0, 512 - features)))
    pixel_rows = pixel_terms.reshape(1, -1, width)
    small = jnp.concatenate(
        [
            norm_terms.reshape(8, shards, model // shards).transpose(1, 0, 2).reshape(shards, 4, width),
            jnp.broadcast_to(pixel_rows, (shards,) + pixel_rows.shape[1:]),
        ],
        axis=1,
    )
    tall = jnp.pad(rows_of_pair, ((0, 0), (0, 384 - features), (0, 0)))
    tall = lax.dynamic_update_slice(tall, small.astype(low_type), (0, 264, 0))
    grad_query = unit(grad_query)
    five = Group(plan, [grad_query, tall.reshape(shards, -1, model)])
    five.send = after(five.send, four.over_fsdp(grad_query))
    sums_two, arrived_two = over_chips([two, three], five.send)
    early_sums = from_all([sums_one, sums_two])
    sums_four, unused = over_chips([four])
    five.over_core()
    arrived = five.over_fsdp()
    mixed = plan.send_back(after(mixed, arrived))
    latents_grad = plan.send_back(after(latents_grad, arrived))
    sums_five, unused = over_chips([five])
    late_sums = from_all([sums_four, sums_five])
    size = one.sizes[0]
    grad_self_up, grad_self_down = gathered(early_sums, one.sizes)
    grad_triple = side_by_side_rows(early_sums, 2, size, 3)
    (grad_self_out,) = gathered(early_sums[:, 5 * size :], [size])
    latents_grad = plan.placed(latents_grad).astype(jnp.float32)
    grad_up, grad_down, grad_out, grad_query = rows_of_each(late_sums, size, 4)
    (tall,) = gathered(late_sums[:, 4 * size :], five.sizes[1:])
    tall = tall.reshape(384, width)
    norm_part = tall[264:268].reshape(8, model // shards)
    pixel_part = tall[268 : 268 + pixel_rows.shape[1]].reshape(2, 512)
    return (
        plan.placed(mixed)[:, None],
        latents_grad[:, None],
        norm_part[:4],
        norm_part[4:],
        pixel_part[0, :features],
        pixel_part[1, :features],
        grad_query,
        tall[:features],
        grad_out,
        grad_up,
        grad_down,
        grad_triple,
        grad_self_out,
        grad_self_up,
        grad_self_down,
    )


def solution(mesh):
    placed = (
        P(None, "blk", "fsdp", None),
        P(None, "blk", None),
        P(None, "blk"),
        P(),
        P(),
        P(None, "fsdp"),
        P(None, "fsdp"),
        P(),
        P(),
        P("fsdp", None),
        P(None, "fsdp"),
        P("fsdp", None),
        P("fsdp", None),
        P("fsdp", None),
        P("fsdp", None),
        P("fsdp", None),
        P("fsdp", None),
        P("fsdp", None),
        P(None, "blk", "fsdp", None),
    )
    return jax.shard_map(
        on_device,
        mesh=mesh,
        in_specs=placed,
        out_specs=(
            P(None, "blk", "fsdp", None),
            P(None, "blk", "fsdp", None),
            P(None, "fsdp"),
            P(None, "fsdp"),
            P(),
            P(),
            P("fsdp", None),
            P(None, "fsdp"),
            P("fsdp", None),
            P("fsdp", None),
            P("fsdp", None),
            P("fsdp", None),
            P("fsdp", None),
            P("fsdp", None),
            P("fsdp", None),
        ),
        check_vma=False,
    )
```

```python
import functools

import jax
import jax.numpy as jnp
from jax import lax
from jax.experimental import pallas as pl
from jax.experimental.pallas import tpu as pltpu
from jax.sharding import PartitionSpec as P

HEADS = 8
FEATURE_ROWS = 272
VMEM_LIMIT = 56 * 1024 * 1024

epsilon = 1e-05
masked_score = -1e30
low_type = jnp.bfloat16


def product(a, b):
    return jnp.dot(a, b, preferred_element_type=jnp.float32)


def product_tn(a, b):
    return lax.dot_general(a, b, (((0,), (0,)), ((), ())), preferred_element_type=jnp.float32)


def product_nt(a, b):
    return lax.dot_general(a, b, (((1,), (1,)), ((), ())), preferred_element_type=jnp.float32)


def normalise(rows):
    centre = rows - jnp.mean(rows, axis=-1, keepdims=True)
    scale = lax.rsqrt(jnp.mean(centre * centre, axis=-1, keepdims=True) + epsilon)
    return centre * scale, scale


def norm_backward(upstream, normed, scale, gain):
    gain_term = jnp.sum(upstream * normed, axis=0)
    bias_term = jnp.sum(upstream, axis=0)
    inner = upstream * gain
    down = scale * (
        inner
        - jnp.mean(inner, axis=-1, keepdims=True)
        - normed * jnp.mean(inner * normed, axis=-1, keepdims=True)
    )
    return down, gain_term, bias_term


def feed_forward(rows, gain, bias, w_up, w_down):
    normed, scale = normalise(rows)
    hidden = (normed * gain + bias).astype(low_type)
    upward = product(hidden, w_up)
    share = 0.5 * (1.0 + lax.erf(upward * (0.5**0.5)))
    slope = share + upward * jnp.exp(-0.5 * upward * upward) * 0.3989422804014327
    active = (upward * share).astype(low_type)
    return rows + product(active, w_down), (hidden, slope, active)


def feed_backward(upstream, low, rows, stored, gain, w_up, w_down):
    hidden, slope, active = stored
    grad_down = product_tn(active, low)
    grad_upward = (product_nt(low, w_down) * slope).astype(low_type)
    grad_up = product_tn(hidden, grad_upward)
    normed, scale = normalise(rows)
    down, gain_term, bias_term = norm_backward(product_nt(grad_upward, w_up), normed, scale, gain)
    return upstream + down, grad_up, grad_down, gain_term, bias_term


def nt(a, b):
    return lax.dot_general(a, b, (((1,), (1,)), ((), ())), preferred_element_type=jnp.float32)


def tn(a, b):
    return lax.dot_general(a, b, (((0,), (0,)), ((), ())), preferred_element_type=jnp.float32)


def params(*semantics):
    return pltpu.CompilerParams(dimension_semantics=semantics, vmem_limit_bytes=VMEM_LIMIT)


def pixel_kernel(micro_ref, pixel_ref, count_ref, out_ref):
    features = pixel_ref.shape[1]
    width = out_ref.shape[3]
    pixels = pixel_ref[0].astype(jnp.float32)
    centre = pixels - jnp.mean(pixels, axis=0, keepdims=True)
    spread = jnp.mean(centre * centre, axis=0, keepdims=True)
    normed = centre * lax.rsqrt(spread + epsilon)
    pad = jnp.zeros((FEATURE_ROWS - features, normed.shape[1]), jnp.float32)
    tall = jnp.concatenate([normed, pad], axis=0)
    row = lax.broadcasted_iota(jnp.int32, (FEATURE_ROWS, width), 0)
    high, rest = count_ref[0][:1, :width], count_ref[0][1:2, :width]
    for part in range(out_ref.shape[0]):
        piece = tall[:, part * width : (part + 1) * width]
        piece = jnp.where(row == features, 1.0, piece)
        piece = jnp.where(row == features + 1, high, jnp.where(row == features + 2, rest, piece))
        out_ref[part, 0] = piece.astype(low_type)


def prepare_pixels(pixels, micro, counts, width):
    routed = micro.shape[0]
    features, slots = pixels.shape[1:]
    step = min(slots, 1024)
    return pl.pallas_call(
        pixel_kernel,
        out_shape=jax.ShapeDtypeStruct((slots // width, routed, FEATURE_ROWS, width), low_type),
        grid_spec=pltpu.PrefetchScalarGridSpec(
            num_scalar_prefetch=1,
            grid=(routed, slots // step),
            in_specs=[
                pl.BlockSpec((1, features, step), lambda i, s, m: (m[i], 0, s)),
                pl.BlockSpec((1, 8, 128), lambda i, s, m: (i, 0, 0)),
            ],
            out_specs=pl.BlockSpec((step // width, 1, FEATURE_ROWS, width), lambda i, s, m: (s, i, 0, 0)),
        ),
        compiler_params=params("arbitrary", "arbitrary"),
        name="prepare_pixels",
    )(micro, pixels, counts)


def side_by_side(ref):
    return jnp.concatenate([ref[tile, 0] for tile in range(ref.shape[0])], axis=1)


def cross_forward_kernel(items, big_ref, query_ref, first_ref, second_ref, mask_ref, out_ref):
    item = pl.program_id(0) // items
    lanes = mask_ref.shape[2] // 2

    def attend(features, mask):
        scores = product(query_ref[...], features) + mask
        top = jnp.max(scores, axis=-1, keepdims=True)
        weights = jnp.exp(scores - top)
        total = jnp.sum(weights, axis=-1, keepdims=True)
        out_ref[...] = nt(weights.astype(low_type), features) / total

    @pl.when(big_ref[item] == 0)
    def small():
        attend(side_by_side(first_ref), mask_ref[0][:1, :lanes])

    @pl.when(big_ref[item] != 0)
    def large():
        both = jnp.concatenate([side_by_side(first_ref), side_by_side(second_ref)], axis=1)
        attend(both, mask_ref[0][:1])


def cross_backward_kernel(items, big_ref, query_ref, grad_ref, first_ref, second_ref, mask_ref, out_ref):
    item = pl.program_id(0) // items
    lanes = mask_ref.shape[2] // 2

    def attend(features, mask):
        scores = product(query_ref[...], features) + mask
        top = jnp.max(scores, axis=-1, keepdims=True)
        weights = jnp.exp(scores - top)
        shares = weights * (1.0 / jnp.sum(weights, axis=-1, keepdims=True))
        grad_shares = product(grad_ref[...], features)
        inner = jnp.sum(shares * grad_shares, axis=-1, keepdims=True)
        grad_scores = (shares * (grad_shares - inner)).astype(low_type)
        out_ref[...] = nt(grad_scores, features)

    @pl.when(big_ref[item] == 0)
    def small():
        attend(side_by_side(first_ref), mask_ref[0][:1, :lanes])

    @pl.when(big_ref[item] != 0)
    def large():
        both = jnp.concatenate([side_by_side(first_ref), side_by_side(second_ref)], axis=1)
        attend(both, mask_ref[0][:1])


def cross_call(kernel, big, rows, first, second, mask, block, per_item):
    count = rows[0].shape[0]
    tiles, width = first.shape[0], first.shape[3]
    row_spec = pl.BlockSpec((block, FEATURE_ROWS), lambda i, big: (i, 0))
    tile_spec = pl.BlockSpec((tiles, 1, FEATURE_ROWS, width), lambda i, big: (0, i // per_item, 0, 0))
    return pl.pallas_call(
        functools.partial(kernel, per_item),
        out_shape=jax.ShapeDtypeStruct((count, FEATURE_ROWS), jnp.float32),
        grid_spec=pltpu.PrefetchScalarGridSpec(
            num_scalar_prefetch=1,
            grid=(count // block,),
            in_specs=[row_spec] * len(rows)
            + [tile_spec, tile_spec]
            + [pl.BlockSpec((1, 8, mask.shape[2]), lambda i, big: (i // per_item, 0, 0))],
            out_specs=row_spec,
        ),
        compiler_params=params("arbitrary"),
        name="cross_attention",
    )(big, *rows, first, second, mask)


def self_forward_kernel(groups, scaling, q_ref, k_ref, v_ref, more_k_ref, more_v_ref, out_ref):
    for q_rows, own, more in groups:
        keys, values = keys_of(own, more, k_ref, v_ref, more_k_ref, more_v_ref)
        scores = nt(q_ref[q_rows], keys) * scaling
        weights = jnp.exp(scores - jnp.max(scores, axis=-1, keepdims=True))
        total = jnp.sum(weights, axis=-1, keepdims=True)
        out_ref[q_rows, :] = (product(weights.astype(low_type), values) / total).astype(low_type)


def keys_of(own, more, k_ref, v_ref, more_k_ref, more_v_ref):
    keys, values = [], []
    if own is not None:
        keys.append(k_ref[own])
        values.append(v_ref[own])
    if more is not None:
        keys.append(more_k_ref[more])
        values.append(more_v_ref[more])
    if len(keys) == 1:
        return keys[0], values[0]
    return jnp.concatenate(keys, axis=0), jnp.concatenate(values, axis=0)


def self_backward_kernel(
    groups,
    scaling,
    q_ref,
    k_ref,
    v_ref,
    more_k_ref,
    more_v_ref,
    grad_ref,
    wide_ref,
    more_ref,
):
    head = q_ref.shape[1]
    model = wide_ref.shape[1] // 3
    column = pl.multiple_of(pl.program_id(0) * head, head)
    at_q, at_k, at_v = (pl.ds(pl.multiple_of(part * model + column, head), head) for part in range(3))
    for q_rows, own, more in groups:
        keys, values = keys_of(own, more, k_ref, v_ref, more_k_ref, more_v_ref)
        queries = q_ref[q_rows]
        grads = grad_ref[q_rows]
        scores = nt(keys, queries) * scaling
        weights = jnp.exp(scores - jnp.max(scores, axis=0, keepdims=True))
        shares = weights * (1.0 / jnp.sum(weights, axis=0, keepdims=True))
        grad_shares = nt(values, grads)
        inner = jnp.sum(shares * grad_shares, axis=0, keepdims=True)
        grad_scores = (shares * (grad_shares - inner)).astype(low_type)
        wide_ref[q_rows, at_q] = (tn(grad_scores, keys) * scaling).astype(low_type)
        dk = (product(grad_scores, queries) * scaling).astype(low_type)
        dv = product(shares.astype(low_type), grads).astype(low_type)
        split = 0
        if own is not None:
            split = own.stop - own.start
            wide_ref[own, at_k] = dk[:split]
            wide_ref[own, at_v] = dv[:split]
        if more is not None:
            more_ref[more, at_q] = dk[split:]
            more_ref[more, at_k] = dv[split:]


def self_specs(triple, more, heads):
    rows, width = triple.shape[0], triple.shape[1] // 3 // heads
    extra = more.shape[0]
    return [
        pl.BlockSpec((rows, width), lambda h: (0, h)),
        pl.BlockSpec((rows, width), lambda h: (0, heads + h)),
        pl.BlockSpec((rows, width), lambda h: (0, 2 * heads + h)),
        pl.BlockSpec((extra, width), lambda h: (0, h)),
        pl.BlockSpec((extra, width), lambda h: (0, heads + h)),
    ]


def self_forward(triple, more, groups):
    rows, model = triple.shape[0], triple.shape[1] // 3
    head = model // HEADS
    return pl.pallas_call(
        functools.partial(self_forward_kernel, groups, head**-0.5),
        out_shape=jax.ShapeDtypeStruct((rows, model), low_type),
        grid=(HEADS,),
        in_specs=self_specs(triple, more, HEADS),
        out_specs=pl.BlockSpec((rows, head), lambda h: (0, h)),
        compiler_params=params("arbitrary"),
        name="self_forward",
    )(triple, triple, triple, more, more)


def self_backward(triple, more, grads, groups):
    rows, model = triple.shape[0], triple.shape[1] // 3
    head = model // HEADS
    extra = more.shape[0]
    return pl.pallas_call(
        functools.partial(self_backward_kernel, groups, head**-0.5),
        out_shape=[
            jax.ShapeDtypeStruct((rows, 3 * model), low_type),
            jax.ShapeDtypeStruct((extra, 2 * model), low_type),
        ],
        grid=(HEADS,),
        in_specs=self_specs(triple, more, HEADS) + [pl.BlockSpec((rows, head), lambda h: (0, h))],
        out_specs=[
            pl.BlockSpec((rows, 3 * model), lambda h: (0, 0)),
            pl.BlockSpec((extra, 2 * model), lambda h: (0, 0)),
        ],
        compiler_params=params("arbitrary"),
        name="self_backward",
    )(triple, triple, triple, more, more, grads)


def widen_kernel(in_ref, out_ref):
    out_ref[...] = in_ref[...].astype(jnp.float32).reshape(out_ref.shape)


def side_by_side_rows(array, first, size, count):
    blocks, unused, width = array.shape
    rows = blocks * size
    if size % 16:
        parts = [array[:, (first + i) * size : (first + i + 1) * size] for i in range(count)]
        return jnp.concatenate([part.reshape(rows, width) for part in parts], axis=1).astype(jnp.float32)
    return pl.pallas_call(
        widen_kernel,
        out_shape=jax.ShapeDtypeStruct((rows, count * width), jnp.float32),
        grid=(count,),
        in_specs=[pl.BlockSpec((blocks, size, width), lambda i: (0, first + i, 0))],
        out_specs=pl.BlockSpec((rows, width), lambda i: (0, i)),
        compiler_params=params("arbitrary"),
        name="widen",
    )(array)


def widen_each_kernel(in_ref, *out_refs):
    size = out_refs[0].shape[0] // in_ref.shape[0]
    for i, out_ref in enumerate(out_refs):
        part = in_ref[:, i * size : (i + 1) * size].astype(jnp.float32)
        out_ref[...] = part.reshape(out_ref.shape)


def rows_of_each(array, size, count):
    blocks, unused, width = array.shape
    if size % 16:
        parts = [array[:, i * size : (i + 1) * size].astype(jnp.float32) for i in range(count)]
        return [part.reshape(blocks * size, width) for part in parts]
    half = width // 2
    return pl.pallas_call(
        widen_each_kernel,
        out_shape=[jax.ShapeDtypeStruct((blocks * size, width), jnp.float32)] * count,
        grid=(2,),
        in_specs=[pl.BlockSpec((blocks, array.shape[1], half), lambda i: (0, 0, i))],
        out_specs=[pl.BlockSpec((blocks * size, half), lambda i: (0, i))] * count,
        compiler_params=params("arbitrary"),
        name="widen_each",
    )(array)


def ordered(bit, own, other, axis=0):
    first = jnp.where(bit == 0, own, other)
    last = jnp.where(bit == 0, other, own)
    return jnp.concatenate([first, last], axis=axis)


def half_of(array, bit, axis):
    size = array.shape[axis] // 2
    return lax.dynamic_slice_in_dim(array, bit * size, size, axis)


def swap(array, axis_name, mask):
    size = lax.axis_size(axis_name)
    return lax.ppermute(array, axis_name, [(i, i ^ mask) for i in range(size)])


class Plan:
    def __init__(self, micro_count, rows):
        self.blocks = lax.axis_size("blk")
        self.shards = lax.axis_size("fsdp")
        self.b = lax.axis_index("blk")
        self.x = lax.axis_index("fsdp")
        self.core = self.b & 1
        self.side = (self.b >> 1) & 1
        self.rows = rows
        self.micro_count = micro_count
        self.paired = self.shards == 2 and self.blocks % 4 == 0 and micro_count == 3
        if self.paired:
            self.micro = jnp.stack([self.x, jnp.int32(2)]).astype(jnp.int32)
            self.block_rows = rows
            self.per_item = 2
            self.groups = (
                (slice(0, 2 * rows), slice(0, 2 * rows), None),
                (slice(2 * rows, 3 * rows), slice(2 * rows, 3 * rows), slice(0, rows)),
            )
        else:
            self.micro = jnp.arange(micro_count, dtype=jnp.int32)
            self.block_rows = rows
            self.per_item = 1
            whole = rows * self.shards
            self.groups = tuple(
                (slice(i * rows, (i + 1) * rows), None, slice(i * whole, (i + 1) * whole))
                for i in range(micro_count)
            )

    def block_of(self, item, device):
        if self.paired and item == 1:
            return (device | 1) - 1 + self.x
        return device

    def turn(self, array):
        places = []
        for x in range(2):
            for b in range(self.blocks):
                core = b % 2
                places.append((b * 2 + x, (b - core + x) * 2 + core))
        return lax.ppermute(array, ("blk", "fsdp"), places)

    def spread(self, array):
        if not self.paired:
            return (array.reshape(-1, array.shape[-1]),)
        own = lax.dynamic_index_in_dim(array, self.x, 0, False)
        away = swap(lax.dynamic_index_in_dim(array, 1 - self.x, 0, False), "fsdp", 1)
        return own, away, self.turn(array[2])

    def send_back(self, array):
        if not self.paired:
            return (array,)
        own, away, shared = (array[i * self.rows : (i + 1) * self.rows] for i in range(3))
        return own, swap(away, "fsdp", 1), self.turn(shared)

    def placed(self, parts):
        if not self.paired:
            return parts[0].reshape(self.micro_count, self.rows, -1)
        own, other, shared = parts
        return jnp.stack([jnp.where(self.x == 0, own, other), jnp.where(self.x == 0, other, own), shared])

    def columns(self, pair, norms):
        if not self.paired:
            return (
                lax.all_gather(pair, "fsdp", axis=1, tiled=True),
                lax.all_gather(norms, "fsdp", axis=1, tiled=True),
            )
        flat = norms.reshape(-1, pair.shape[1])
        return (swap(jnp.concatenate([pair, flat], axis=0), "fsdp", 1),)

    def joined(self, pair, norms, other):
        if not self.paired:
            return other
        rows = pair.shape[0]
        return (
            ordered(self.x, pair, other[0][:rows], 1),
            ordered(self.x, norms, other[0][rows:].reshape(norms.shape), 1),
        )

    def fetch(self, weights, chips):
        if not self.paired:
            return None
        part = self.core if chips == 1 else 2 * self.core + self.side
        size = weights[0].shape[0] // (2 * chips)
        parts = [lax.dynamic_slice_in_dim(weight, part * size, size, 0) for weight in weights]
        return jnp.concatenate(parts, axis=1)

    def whole(self, weights, near, chips):
        if not self.paired:
            return [lax.all_gather(weight, "fsdp", axis=0, tiled=True) for weight in weights]
        if chips == 2:
            near = ordered(self.side, near, swap(near, "blk", 2))
        away = ordered(self.core, near, swap(near, "blk", 1))
        results, at = [], 0
        for weight in weights:
            results.append(ordered(self.x, weight, away[:, at : at + weight.shape[1]]))
            at += weight.shape[1]
        return results

    def partner_rows(self, pairs):
        if self.paired:
            return swap(pairs[2 * self.rows :], "blk", 1)
        wide = pairs.reshape(self.micro_count, self.rows, -1)
        return lax.all_gather(wide, "fsdp", axis=1, tiled=True).reshape(-1, wide.shape[-1])

    def own_pairs(self, wide, more):
        model = wide.shape[1] // 3
        if self.paired:
            back = swap(more, "blk", 1).astype(jnp.float32)
            first = 2 * self.rows
            last = (wide[first:, model:].astype(jnp.float32) + back).astype(low_type)
            return lax.dynamic_update_slice(wide, last, (first, model))
        split = more.reshape(self.micro_count, self.rows * self.shards, -1)
        back = lax.psum_scatter(split, "fsdp", scatter_dimension=1, tiled=True)
        return lax.dynamic_update_slice(wide, back.reshape(-1, back.shape[-1]), (0, model))


def added(kept, received):
    return (kept.astype(jnp.float32) + received.astype(jnp.float32)).astype(low_type)


def after(value, *others):
    if not others:
        return value
    return lax.optimization_barrier((value,) + others)[0]


class Group:
    def __init__(self, plan, units):
        self.plan = plan
        count, core = plan.blocks // 2, plan.core
        pieces = [unit.reshape(plan.shards, count, 2, -1, unit.shape[2]) for unit in units]
        self.sizes = [piece.shape[3] for piece in pieces]
        self.send = jnp.concatenate(
            [lax.dynamic_index_in_dim(piece, 1 - core, 2, False) for piece in pieces], axis=2
        )
        self.kept = jnp.concatenate([lax.dynamic_index_in_dim(piece, core, 2, False) for piece in pieces], axis=2)

    def over_core(self, *earlier):
        received = after(swap(self.send, "blk", 1), *earlier)
        mask = self.plan.shards // 2
        while mask:
            bit = jnp.where((self.plan.x & mask) > 0, 1, 0)
            self.send = added(half_of(self.kept, 1 - bit, 0), half_of(received, 1 - bit, 0))
            self.kept = added(half_of(self.kept, bit, 0), half_of(received, bit, 0))
            if mask > 1:
                received = swap(self.send, "fsdp", mask)
            mask //= 2
        return self.send

    def over_fsdp(self, *earlier):
        received = after(swap(self.send, "fsdp", 1), *earlier)
        self.total = added(self.kept, received)[0]
        return received


def over_chips(groups, *earlier):
    plan = groups[0].plan
    total = jnp.concatenate([group.total for group in groups], axis=1)
    same_core = [list(range(core, plan.blocks, 2)) for core in range(2)]
    arrived = lax.all_to_all(
        total, "blk", split_axis=0, concat_axis=0, axis_index_groups=same_core, tiled=True
    )
    arrived = after(arrived, *earlier)
    return jnp.sum(arrived.astype(jnp.float32), axis=0).astype(low_type), arrived


def from_all(sums):
    return lax.all_gather(jnp.concatenate(sums, axis=0), "blk", axis=0)


def gathered(array, sizes):
    results, at = [], 0
    for size in sizes:
        part = array[:, at : at + size].astype(jnp.float32)
        results.append(part.reshape(-1, part.shape[2]))
        at += size
    return results


def route_pixels(plan, pixels, segment_ids, pad_ids, block_map, fetch):
    blocks, labels = plan.blocks, block_map.shape[1]
    slots, features = pixels.shape[1:]
    width = slots // blocks
    routed = plan.micro.shape[0]
    label_ids = jnp.arange(labels, dtype=jnp.int32)

    def of_items(array):
        return jnp.stack([lax.dynamic_index_in_dim(array, plan.micro[i], 0, False) for i in range(routed)])

    picked = of_items(segment_ids)
    counts = jnp.sum((picked[:, None, :] == label_ids[None, :, None]).astype(jnp.int32), axis=2)
    counts = jnp.stack([counts >> 4, counts & 15], axis=1).astype(jnp.float32)
    counts = jnp.pad(counts, ((0, 0), (0, 6), (0, 128 - labels)))
    chunks = prepare_pixels(jnp.swapaxes(pixels, 1, 2), plan.micro, counts, width)
    spread = lax.all_to_all(chunks, "blk", split_axis=0, concat_axis=0, tiled=True)
    arrived = spread[:, :, features + 1 : features + 3, :labels].astype(jnp.int32)
    totals = jnp.sum(16 * arrived[:, :, 0] + arrived[:, :, 1], axis=0)
    owners = of_items(block_map)
    images = label_ids[None, :] != of_items(pad_ids)[:, None]
    totals = jnp.where(images, totals, 0)
    earlier = label_ids[None, :] < label_ids[:, None]
    starts = jnp.sum(jnp.where(earlier[None], totals[:, None, :], 0), axis=2)
    devices = jnp.arange(blocks, dtype=jnp.int32)

    def extents(wanted):
        hit = (owners[:, None, :] == wanted[:, :, None]) & images[:, None, :]
        start = jnp.sum(jnp.where(hit, starts[:, None, :], 0), axis=2)
        return start, start + jnp.sum(jnp.where(hit, totals[:, None, :], 0), axis=2)

    def chunk_at(start, place):
        first = start // width
        return first + ((place - first) & (blocks - 1))

    def source_of(chunk):
        return jnp.clip(chunk // blocks, 0, blocks - 1)

    item = jnp.arange(routed, dtype=jnp.int32)
    wanted = jnp.stack([plan.block_of(i, devices) for i in range(routed)])
    start, finish = extents(wanted)
    flat = spread.reshape(blocks * routed, FEATURE_ROWS, width)
    piece_at = source_of(chunk_at(start, plan.b)) * routed + item[:, None]
    pieces = jnp.take(flat, piece_at.T.reshape(-1), axis=0, mode="clip")
    pieces = pieces.reshape(blocks, routed, FEATURE_ROWS, width)
    fetched, sent = fetch(chunks, pieces)
    if sent is not None:
        pieces = after(pieces, sent)
    first = lax.all_to_all(pieces, "blk", split_axis=0, concat_axis=0, tiled=True)
    largest = jnp.argmax(totals, axis=1)
    largest_start = jnp.sum(jnp.where(label_ids[None, :] == largest[:, None], starts, 0), axis=1)
    second_at = source_of(chunk_at(largest_start, plan.b) + blocks) * routed + item
    second = lax.all_gather(jnp.take(flat, second_at, axis=0, mode="clip"), "blk", axis=0, tiled=False)
    mine = jnp.stack([plan.block_of(i, plan.b) for i in range(routed)])[:, None]
    start, finish = extents(mine)
    slot = (width * chunk_at(start, devices[None, :]))[:, :, None] + jnp.arange(width, dtype=jnp.int32)
    slot = slot.reshape(routed, -1)
    slot = jnp.concatenate([slot, slot + width * blocks], axis=1)
    mask = jnp.where((slot >= start) & (slot < finish), 0.0, masked_score)
    mask = jnp.broadcast_to(mask[:, None, :], (routed, 8, mask.shape[1]))
    big = ((finish - 1) // width - start // width >= blocks).astype(jnp.int32)[:, 0]
    if width < 128:
        join = 128 // width

        def merged(array):
            parts = array.reshape(blocks // join, join, routed, FEATURE_ROWS, width)
            return parts.transpose(0, 2, 3, 1, 4).reshape(blocks // join, routed, FEATURE_ROWS, 128)

        first, second = merged(first), merged(second)
    return fetched, first, second, mask, big


def on_device(
    latents,
    pixels,
    segment_ids,
    pad_ids,
    block_map,
    norm_gains,
    norm_biases,
    pixel_gain,
    pixel_bias,
    cross_query,
    cross_kv,
    cross_out,
    cross_up,
    cross_down,
    self_qkv,
    self_out,
    self_up,
    self_down,
    cotangent,
):
    micro_count, unused, rows, model = latents.shape
    features = pixels.shape[2]
    plan = Plan(micro_count, rows)
    scaling = model**-0.5

    norm_rows = jnp.concatenate([norm_gains, norm_biases], axis=0)
    early, middle = [cross_query], [cross_out, cross_up, cross_down]
    late, last = [self_qkv], [self_out, self_up, self_down]

    def fetch(chunks, pieces):
        if not plan.paired:
            return (plan.spread(latents[:, 0]), plan.columns(cross_kv, norm_rows)) + (None,) * 4, None
        latent = plan.spread(after(latents, chunks)[:, 0])
        near_early = swap(plan.fetch([after(cross_query, chunks)], 1), "fsdp", 1)
        other = plan.columns(after(cross_kv, chunks), norm_rows)
        send = plan.fetch([after(middle[0], near_early, *latent[1:], *other)] + middle[1:], 1)
        near_middle = swap(send, "fsdp", 1)
        near_late = swap(plan.fetch([after(late[0], send, pieces)], 2), "fsdp", 1)
        near_last = swap(plan.fetch([after(last[0], send, pieces)] + last[1:], 2), "fsdp", 1)
        latent = (latent[0],) + tuple(after(part, pieces) for part in latent[1:])
        near_early, other = after(near_early, pieces), (after(other[0], pieces),)
        return (latent, other, near_early, near_middle, near_late, near_last), send

    fetched, first, second, mask, big = route_pixels(plan, pixels, segment_ids, pad_ids, block_map, fetch)
    latent, other, near_early, near_middle, near_late, near_last = fetched
    latent = jnp.concatenate(latent, axis=0).astype(jnp.float32)
    w_pair, norms = plan.joined(cross_kv, norm_rows, other)
    norms = norms.astype(jnp.float32)
    gains, biases = norms[:4], norms[4:]
    w_key, w_value = w_pair[:, :model], w_pair[:, model:]
    (w_query,) = plan.whole(early, near_early, 1)
    pixel_scaler = pixel_gain.astype(jnp.float32)
    pixel_offset = pixel_bias.astype(jnp.float32)

    def widened(rows_f32, scale):
        against = jnp.sum(rows_f32 * pixel_offset, axis=-1, keepdims=True)
        wide = jnp.concatenate([rows_f32 * pixel_scaler, against], axis=1) * scale
        return jnp.pad(wide, ((0, 0), (0, FEATURE_ROWS - features - 1))).astype(low_type)

    def narrowed(wide):
        return wide[:, :features] * pixel_scaler + wide[:, features : features + 1] * pixel_offset

    normed, scale = normalise(latent)
    hidden = (normed * gains[0] + biases[0]).astype(low_type)
    queries = product(hidden, w_query).astype(low_type)
    query_features = product_nt(queries, w_key)
    wide_queries = widened(query_features, scaling)
    if plan.paired:
        near_middle, near_late = after(near_middle, wide_queries), after(near_late, first)
    w_out, w_up, w_down = plan.whole(middle, near_middle, 1)
    (w_triple,) = plan.whole(late, near_late, 2)
    summed = cross_call(
        cross_forward_kernel, big, [wide_queries], first, second, mask, plan.block_rows, plan.per_item
    )
    if plan.paired:
        near_last, cotangent = after(near_last, summed), after(cotangent, summed)
    w_self_out, w_self_up, w_self_down = plan.whole(last, near_last, 2)
    upstream = plan.spread(cotangent[:, 0])
    attended_features = narrowed(summed).astype(low_type)
    attended = product(attended_features, w_value).astype(low_type)
    first_sum = latent + product(attended, w_out)
    second_sum, stored_one = feed_forward(first_sum, gains[1], biases[1], w_up, w_down)
    normed_two, scale_two = normalise(second_sum)
    hidden_two = (normed_two * gains[2] + biases[2]).astype(low_type)
    triple = product(hidden_two, w_triple).astype(low_type)
    more = plan.partner_rows(triple[:, model:])
    blended = self_forward(triple, more, plan.groups)
    third_sum = second_sum + product(blended, w_self_out)
    mixed, stored_three = feed_forward(third_sum, gains[3], biases[3], w_self_up, w_self_down)
    mixed = mixed.astype(low_type)

    def unit(grad):
        return grad.astype(low_type).reshape(plan.shards, -1, model)

    if plan.paired:
        upstream = (upstream[0],) + tuple(after(part, third_sum) for part in upstream[1:])
    upstream = jnp.concatenate(upstream, axis=0).astype(jnp.float32)
    low = upstream.astype(low_type)
    upstream, grad_self_up, grad_self_down, gain_three, bias_three = feed_backward(
        upstream, low, third_sum, stored_three, gains[3], w_self_up, w_self_down
    )
    low = upstream.astype(low_type)
    grad_self_out = product_tn(blended, low)
    grad_self_out = product_tn(blended, low)
    one = Group(plan, [unit(grad_self_up), unit(grad_self_down)])
    grad_blended = product_nt(low, w_self_out).astype(low_type)
    grad_blended = after(grad_blended, one.over_core(), mixed)
    triple_grads, more_grads = self_backward(triple, more, grad_blended, plan.groups)
    triple_grads, more_grads = after((triple_grads, more_grads), one.over_fsdp())
    triple_grads = plan.own_pairs(triple_grads, more_grads)
    grad_q, grad_k, grad_v = (
        unit(product_tn(hidden_two, triple_grads[:, i * model : (i + 1) * model])) for i in range(3)
    )
    two, three = Group(plan, [grad_q, grad_k]), Group(plan, [grad_v, unit(grad_self_out)])
    triple_grads = after(triple_grads, two.send, three.send)
    sums_one, arrived_one = over_chips([one])
    grad_hidden = product_nt(triple_grads, w_triple)
    down, gain_two, bias_two = norm_backward(grad_hidden, normed_two, scale_two, gains[2])
    upstream = upstream + down
    low = upstream.astype(low_type)
    grad_down = product_tn(stored_one[2], low)
    low = after(low, two.over_core())
    upstream, grad_up, unused, gain_one, bias_one = feed_backward(
        upstream, low, first_sum, stored_one, gains[1], w_up, w_down
    )
    grad_up, grad_down = unit(grad_up), unit(grad_down)
    low = upstream.astype(low_type)
    low = after(low, grad_up, grad_down, two.over_fsdp(low), three.over_core(low), arrived_one)
    grad_out = product_tn(attended, low)
    four = Group(plan, [grad_up, grad_down, unit(grad_out)])
    grad_attended = product_nt(low, w_out).astype(low_type)
    grad_value = product_tn(attended_features, grad_attended)
    grad_features = product_nt(grad_attended, w_value)
    wide_grads = after(widened(grad_features, 1.0), four.send)
    score_sums = cross_call(
        cross_backward_kernel,
        big,
        [wide_queries, wide_grads],
        first,
        second,
        mask,
        plan.block_rows,
        plan.per_item,
    )
    score_sums = after(score_sums, three.over_fsdp(score_sums), four.over_core(score_sums))
    key_sums = (narrowed(score_sums) * scaling).astype(low_type)
    grad_queries = product(key_sums, w_key).astype(low_type)
    grad_key = product_tn(key_sums, queries)
    pixel_gain_term = jnp.sum(
        query_features * score_sums[:, :features] * scaling + grad_features * summed[:, :features], axis=0
    )
    pixel_bias_term = jnp.sum(
        query_features * score_sums[:, features : features + 1] * scaling
        + grad_features * summed[:, features : features + 1],
        axis=0,
    )
    grad_query = product_tn(hidden, grad_queries)
    down, gain_zero, bias_zero = norm_backward(product_nt(grad_queries, w_query), normed, scale, gains[0])
    latents_grad = (upstream + down).astype(low_type)

    shards = plan.shards
    width = 2 * model // shards
    if shards == 2:
        rows_of_pair = jnp.stack([grad_key, grad_value]).astype(low_type)
    else:
        rows_of_pair = jnp.concatenate([grad_key, grad_value], axis=1).astype(low_type)
        rows_of_pair = rows_of_pair.reshape(features, shards, width).transpose(1, 0, 2)
    norm_terms = jnp.stack(
        [gain_zero, gain_one, gain_two, gain_three, bias_zero, bias_one, bias_two, bias_three]
    )
    pixel_terms = jnp.pad(jnp.stack([pixel_gain_term, pixel_bias_term]), ((0, 0), (0, 512 - features)))
    pixel_rows = pixel_terms.reshape(1, -1, width)
    small = jnp.concatenate(
        [
            norm_terms.reshape(8, shards, model // shards).transpose(1, 0, 2).reshape(shards, 4, width),
            jnp.broadcast_to(pixel_rows, (shards,) + pixel_rows.shape[1:]),
        ],
        axis=1,
    )
    tall = jnp.pad(rows_of_pair, ((0, 0), (0, 384 - features), (0, 0)))
    tall = lax.dynamic_update_slice(tall, small.astype(low_type), (0, 264, 0))
    grad_query = unit(grad_query)
    five = Group(plan, [grad_query, tall.reshape(shards, -1, model)])
    five.send = after(five.send, four.over_fsdp(grad_query))
    sums_two, arrived_two = over_chips([two, three], five.send)
    early_sums = from_all([sums_one, sums_two])
    five.over_core()
    arrived = five.over_fsdp()
    mixed = plan.send_back(after(mixed, arrived))
    latents_grad = plan.send_back(after(latents_grad, arrived))
    sums_late, unused = over_chips([four, five])
    late_sums = from_all([sums_late])
    size = one.sizes[0]
    grad_self_up, grad_self_down = gathered(early_sums, one.sizes)
    grad_triple = side_by_side_rows(early_sums, 2, size, 3)
    (grad_self_out,) = gathered(early_sums[:, 5 * size :], [size])
    latents_grad = plan.placed(latents_grad).astype(jnp.float32)
    grad_up, grad_down, grad_out, grad_query = rows_of_each(late_sums, size, 4)
    (tall,) = gathered(late_sums[:, 4 * size :], five.sizes[1:])
    tall = tall.reshape(384, width)
    norm_part = tall[264:268].reshape(8, model // shards)
    pixel_part = tall[268 : 268 + pixel_rows.shape[1]].reshape(2, 512)
    return (
        plan.placed(mixed)[:, None],
        latents_grad[:, None],
        norm_part[:4],
        norm_part[4:],
        pixel_part[0, :features],
        pixel_part[1, :features],
        grad_query,
        tall[:features],
        grad_out,
        grad_up,
        grad_down,
        grad_triple,
        grad_self_out,
        grad_self_up,
        grad_self_down,
    )


def solution(mesh):
    placed = (
        P(None, "blk", "fsdp", None),
        P(None, "blk", None),
        P(None, "blk"),
        P(),
        P(),
        P(None, "fsdp"),
        P(None, "fsdp"),
        P(),
        P(),
        P("fsdp", None),
        P(None, "fsdp"),
        P("fsdp", None),
        P("fsdp", None),
        P("fsdp", None),
        P("fsdp", None),
        P("fsdp", None),
        P("fsdp", None),
        P("fsdp", None),
        P(None, "blk", "fsdp", None),
    )
    return jax.shard_map(
        on_device,
        mesh=mesh,
        in_specs=placed,
        out_specs=(
            P(None, "blk", "fsdp", None),
            P(None, "blk", "fsdp", None),
            P(None, "fsdp"),
            P(None, "fsdp"),
            P(),
            P(),
            P("fsdp", None),
            P(None, "fsdp"),
            P("fsdp", None),
            P("fsdp", None),
            P("fsdp", None),
            P("fsdp", None),
            P("fsdp", None),
            P("fsdp", None),
            P("fsdp", None),
        ),
        check_vma=False,
    )
```
